32 devices in a mesh: dp: 8 (over y, x, core), ctx: 4 (over z).
Axes of the slice: x: 2, y: 2, z: 4, core: 2. Of those that a mesh axis runs over, the one named last changes fastest.
Arguments:
- input_gate: bfloat16 [512, 131072], P('dp', 'ctx'), may hold values from -6 to 6
- output_gate: bfloat16 [512, 131072], P('dp', 'ctx'), may hold values from -6 to 6
- values: bfloat16 [512, 131072], P('dp', 'ctx'), may hold values from -6 to 6
- cotangent: bfloat16 [512, 131072], P('dp', 'ctx'), may hold values from -6 to 6
- filter_raw: bfloat16 [16, 131072], P(None, 'ctx'), may hold values from -6 to 6
- filter_decay: float32 [16], replicated, may hold values from 0.25 to 2
- skip_gain: float32 [512], P('dp'), may hold values from -4 to 4
Outputs:
- outputs: bfloat16 [512, 131072], P('dp', 'ctx')
- grad_input_gate: bfloat16 [512, 131072], P('dp', 'ctx')
- grad_output_gate: bfloat16 [512, 131072], P('dp', 'ctx')
- grad_values: bfloat16 [512, 131072], P('dp', 'ctx')
- grad_filter: float32 [16, 131072], P(None, 'ctx')
The draws below stay inside these ranges and needn't reach their ends.
All inputs are finite; a program needn't handle non-finite values.
Results may differ from the reference program's by a relative error of at most 0.018.
Values may be sent and summed in bfloat16 or wider, within the bound.
No kernel may reach another device: no remote copies, remote signals or barrier semaphores. Data moves between devices by JAX's collectives and lax.ppermute only.
A program may use at most 256 MiB of HBM per device.

```python
import math
import jax
import jax.numpy as jnp
from jax import lax

N1 = 512
N2 = 512
CHANNELS = 512
FILTERS = 16
FFT_LEN = 262144
SEQ = 131072


def shard_levels(rng, extent, shards, least, high):
    loudness, own = 1.0, jax.random.fold_in(rng, 6)
    for dim, parts in shards:
        heights = jnp.exp(jax.random.uniform(jax.random.fold_in(own, dim), (parts,), jnp.float32, least / len(shards), high / len(shards)))
        loudness = loudness * jnp.repeat(heights, extent[dim] // parts).reshape([-1 if axis == dim else 1 for axis in range(len(extent))])
    return loudness


def scatter_about(rng, shape, deviation, limit, cuts=(), kind=jnp.bfloat16):
    values = deviation * jax.random.normal(rng, shape, jnp.float32)
    if cuts:
        values = values * shard_levels(rng, shape, cuts, -0.22, 0.18)
    return jnp.clip(values, -limit, limit).astype(kind)


def setup_inputs(seed: int = 0) -> dict:
    arg_keys = jax.random.split(jax.random.key(seed), 8)
    input_gate = scatter_about(arg_keys[0], (CHANNELS, SEQ), 1.0, 6.0, ((0, 8), (1, 4)))
    output_gate = scatter_about(arg_keys[1], (CHANNELS, SEQ), 1.0, 6.0, ((0, 8), (1, 4)))
    values = scatter_about(arg_keys[2], (CHANNELS, SEQ), 1.0, 6.0, ((0, 8), (1, 4)))
    cotangent = scatter_about(arg_keys[3], (CHANNELS, SEQ), 1.0, 6.0, ((0, 8), (1, 4)))
    filter_raw = scatter_about(arg_keys[4], (FILTERS, SEQ), 1.0, 6.0, ((1, 4),))
    filter_decay = jnp.clip(jnp.exp(jax.random.uniform(arg_keys[5], (FILTERS,), jnp.float32, math.log(0.25), math.log(2.0))), 0.25, 2.0)
    skip_gain = scatter_about(arg_keys[6], (CHANNELS,), 1.0, 4.0, ((0, 8),), jnp.float32)
    return {"input_gate": input_gate, "output_gate": output_gate, "values": values, "cotangent": cotangent, "filter_raw": filter_raw, "filter_decay": filter_decay, "skip_gain": skip_gain}


two_pi = 2.0 * math.pi


def product(form, left, right):
    return jnp.einsum(form, left.astype(jnp.float32), right.astype(jnp.float32), precision=lax.Precision.HIGHEST)


def dft_tables(row_total):
    first_index = jnp.arange(N1, dtype=jnp.int32)
    source_rows = jnp.arange(row_total, dtype=jnp.int32)
    first_angles = ((first_index[:, None] * source_rows[None, :]) % N1).astype(jnp.float32) * (two_pi / N1)
    second_index = jnp.arange(N2, dtype=jnp.int32)
    second_angles = ((second_index[:, None] * second_index[None, :]) % N2).astype(jnp.float32) * (two_pi / N2)
    return (jnp.cos(first_angles).astype(jnp.bfloat16), (-jnp.sin(first_angles)).astype(jnp.bfloat16),
            jnp.cos(second_angles).astype(jnp.bfloat16), (-jnp.sin(second_angles)).astype(jnp.bfloat16))


def twiddle_table(spectrum_rows, columns):
    angles = ((spectrum_rows[:, None] * columns[None, :]) % FFT_LEN).astype(jnp.float32) * (two_pi / FFT_LEN)
    return jnp.cos(angles), -jnp.sin(angles)


def forward_signal(signal, tables, turn):
    first_real, first_imaginary, second_real, second_imaginary = tables
    turn_real, turn_imaginary = turn
    product_real = product("km,bmn->bkn", first_real, signal)
    product_imaginary = product("km,bmn->bkn", first_imaginary, signal)
    turned_real = (product_real * turn_real - product_imaginary * turn_imaginary).astype(jnp.bfloat16)
    turned_imaginary = (product_real * turn_imaginary + product_imaginary * turn_real).astype(jnp.bfloat16)
    spectrum_real = (product("bkn,nl->bkl", turned_real, second_real)
                     - product("bkn,nl->bkl", turned_imaginary, second_imaginary))
    spectrum_imaginary = (product("bkn,nl->bkl", turned_real, second_imaginary)
                          + product("bkn,nl->bkl", turned_imaginary, second_real))
    return spectrum_real, spectrum_imaginary


def inverse_signal(spectrum_real, spectrum_imaginary, tables, turn):
    first_real, first_imaginary, second_real, second_imaginary = tables
    turn_real, turn_imaginary = turn
    back_real = (product("bkn,nl->bkl", spectrum_real, second_real)
                 + product("bkn,nl->bkl", spectrum_imaginary, second_imaginary))
    back_imaginary = (product("bkn,nl->bkl", spectrum_imaginary, second_real)
                      - product("bkn,nl->bkl", spectrum_real, second_imaginary))
    inverse_scale = 1.0 / FFT_LEN
    rotated_real = ((back_real * turn_real + back_imaginary * turn_imaginary) * inverse_scale).astype(jnp.bfloat16)
    rotated_imaginary = ((back_imaginary * turn_real - back_real * turn_imaginary) * inverse_scale).astype(jnp.bfloat16)
    result = (product("km,bkn->bmn", first_real, rotated_real)
              + product("km,bkn->bmn", first_imaginary, rotated_imaginary))
    return result.astype(jnp.bfloat16)


def reference(input_gate, output_gate, values, cotangent, filter_raw, filter_decay, skip_gain):
    row_total = SEQ // N2
    tables = dft_tables(row_total)
    turn = twiddle_table(jnp.arange(N1, dtype=jnp.int32), jnp.arange(N2, dtype=jnp.int32))
    all_positions = jnp.arange(SEQ, dtype=jnp.int32).astype(jnp.float32)
    envelope = jnp.exp(-filter_decay[:, None] * (all_positions[None, :] / SEQ))
    filter_scale = SEQ ** -0.5
    filter_taps = (filter_raw.astype(jnp.float32) * envelope * filter_scale).astype(jnp.bfloat16)
    spec_real, spec_imaginary = forward_signal(filter_taps.reshape(FILTERS, row_total, N2), tables, turn)
    filter_real = spec_real.astype(jnp.bfloat16).astype(jnp.float32)
    filter_imaginary = spec_imaginary.astype(jnp.bfloat16).astype(jnp.float32)
    groups = CHANNELS // FILTERS

    def grouped(array):
        return array.reshape(groups, FILTERS, SEQ)

    def one_group(operands):
        gate_input, gate_output, value_rows, cotangent_rows, skip_rows = operands
        mixed_input = (gate_input.astype(jnp.float32) * value_rows.astype(jnp.float32)).astype(jnp.bfloat16)
        weighted = (cotangent_rows.astype(jnp.float32) * gate_output.astype(jnp.float32)).astype(jnp.bfloat16)
        mix_real, mix_imaginary = forward_signal(mixed_input.reshape(FILTERS, row_total, N2), tables, turn)
        weight_real, weight_imaginary = forward_signal(weighted.reshape(FILTERS, row_total, N2), tables, turn)
        convolved = inverse_signal((mix_real * filter_real - mix_imaginary * filter_imaginary).astype(jnp.bfloat16),
                                   (mix_real * filter_imaginary + mix_imaginary * filter_real).astype(jnp.bfloat16),
                                   tables, turn).reshape(FILTERS, SEQ)
        correlated = inverse_signal((filter_real * weight_real + filter_imaginary * weight_imaginary).astype(jnp.bfloat16),
                                    (filter_real * weight_imaginary - filter_imaginary * weight_real).astype(jnp.bfloat16),
                                    tables, turn).reshape(FILTERS, SEQ)
        lagged = inverse_signal((mix_real * weight_real + mix_imaginary * weight_imaginary).astype(jnp.bfloat16),
                                (mix_real * weight_imaginary - mix_imaginary * weight_real).astype(jnp.bfloat16),
                                tables, turn).reshape(FILTERS, SEQ)
        summed = convolved.astype(jnp.float32) + skip_rows[:, None] * mixed_input.astype(jnp.float32)
        outputs = (gate_output.astype(jnp.float32) * summed).astype(jnp.bfloat16)
        grad_two = (cotangent_rows.astype(jnp.float32) * summed).astype(jnp.bfloat16)
        back_total = correlated.astype(jnp.float32) + skip_rows[:, None] * weighted.astype(jnp.float32)
        grad_one = (back_total * value_rows.astype(jnp.float32)).astype(jnp.bfloat16)
        grad_three = (back_total * gate_input.astype(jnp.float32)).astype(jnp.bfloat16)
        return outputs, grad_one, grad_two, grad_three, lagged

    results = lax.map(one_group, (grouped(input_gate), grouped(output_gate), grouped(values),
                                  grouped(cotangent), skip_gain.reshape(groups, FILTERS)))
    lag_total = jnp.sum(results[4].astype(jnp.float32), axis=0)
    grad_filter = lag_total * envelope * filter_scale
    return (results[0].reshape(CHANNELS, SEQ), results[1].reshape(CHANNELS, SEQ),
            results[2].reshape(CHANNELS, SEQ), results[3].reshape(CHANNELS, SEQ), grad_filter)
```

```python
import math

import jax
import jax.numpy as jnp
import ml_dtypes
import numpy as np
from jax import lax
from jax.experimental import pallas as pl
from jax.experimental.pallas import tpu as pltpu
from jax.sharding import PartitionSpec as P

N1 = 512
N2 = 512
FFT_LEN = 262144


two_pi = 2.0 * math.pi


def first_tables(row_total):
    first_index = jnp.arange(N1, dtype=jnp.int32)
    source_rows = jnp.arange(row_total, dtype=jnp.int32)
    angles = (first_index[:, None] * source_rows[None, :] % N1).astype(jnp.float32) * (two_pi / N1)
    cosine = jnp.cos(angles).astype(jnp.bfloat16)
    minus_sine = (-jnp.sin(angles)).astype(jnp.bfloat16)
    forward_table = jnp.concatenate([cosine, minus_sine], axis=0)
    inverse_table = jnp.stack([cosine.T, minus_sine.T], axis=2)
    return (forward_table, inverse_table)


def second_tables():
    second_index = jnp.arange(N2, dtype=jnp.int32)
    angles = (second_index[:, None] * second_index[None, :] % N2).astype(jnp.float32) * (
        two_pi / N2
    )
    cosine = jnp.cos(angles).astype(jnp.bfloat16)
    minus_sine = (-jnp.sin(angles)).astype(jnp.bfloat16)
    forward_table = jnp.stack(
        [
            jnp.concatenate([cosine, minus_sine], axis=1),
            jnp.concatenate([-minus_sine, cosine], axis=1),
        ],
        axis=0,
    )
    inverse_table = jnp.concatenate(
        [
            jnp.concatenate([cosine, -minus_sine], axis=1),
            jnp.concatenate([minus_sine, cosine], axis=1),
        ],
        axis=0,
    )
    return (forward_table, inverse_table)


def twiddle_table(spectrum_rows, columns):
    angles = (spectrum_rows[:, None] * columns[None, :] % FFT_LEN).astype(jnp.float32) * (
        two_pi / FFT_LEN
    )
    return (jnp.cos(angles), -jnp.sin(angles))


def halves(array):
    return (array[..., :N2], array[..., N2:])


def joined(real_part, imaginary_part):
    return jnp.concatenate([real_part, imaginary_part], axis=-1).astype(jnp.bfloat16)


def spectral_products(mix_spec, weight_spec, filter_spec, which):
    lead = mix_spec.shape[:-2]
    filters = filter_spec.shape[-2]
    filter_real, filter_imaginary = halves(filter_spec.astype(jnp.float32))
    filter_real = jnp.expand_dims(filter_real, -3)
    filter_imaginary = jnp.expand_dims(filter_imaginary, -3)
    outcome = []
    mix_real, mix_imaginary = halves(mix_spec.reshape(lead + (-1, filters, 2 * N2)))
    weight_real, weight_imaginary = halves(weight_spec.reshape(lead + (-1, filters, 2 * N2)))
    for name in which:
        if name == "convolve":
            made = joined(
                mix_real * filter_real - mix_imaginary * filter_imaginary,
                mix_real * filter_imaginary + mix_imaginary * filter_real,
            )
        elif name == "correlate":
            made = joined(
                filter_real * weight_real + filter_imaginary * weight_imaginary,
                filter_real * weight_imaginary - filter_imaginary * weight_real,
            )
        else:
            made = joined(
                mix_real * weight_real + mix_imaginary * weight_imaginary,
                mix_real * weight_imaginary - mix_imaginary * weight_real,
            )
        outcome.append(made.reshape(lead + (-1, 2 * N2)))
    return outcome


def shards(input_gate, output_gate, values, cotangent, filter_raw, filter_decay, skip_gain):
    context_size = lax.axis_size("ctx")
    context_index = lax.axis_index("ctx")
    channels, local_len = input_gate.shape
    filters = filter_raw.shape[0]
    groups = channels // filters
    row_local = local_len // N2
    row_total = row_local * context_size
    seq_len = local_len * context_size
    first_forward, first_inverse = first_tables(row_total)
    second_forward, second_inverse = second_tables()
    inverse_scale = 1.0 / FFT_LEN
    mixed_input = (input_gate.astype(jnp.float32) * values.astype(jnp.float32)).astype(jnp.bfloat16)
    weighted = (cotangent.astype(jnp.float32) * output_gate.astype(jnp.float32)).astype(
        jnp.bfloat16
    )
    global_positions = (context_index * local_len + jnp.arange(local_len, dtype=jnp.int32)).astype(
        jnp.float32
    )
    envelope = jnp.exp(-filter_decay[:, None] * (global_positions[None, :] / seq_len))
    filter_scale = seq_len ** (-0.5)
    filter_taps = (filter_raw.astype(jnp.float32) * envelope * filter_scale).astype(jnp.bfloat16)
    spread_count = filters // context_size
    full_real, full_imaginary = twiddle_table(
        jnp.arange(N1, dtype=jnp.int32), jnp.arange(N2, dtype=jnp.int32)
    )
    pair = jnp.stack([mixed_input, weighted], axis=0).reshape(2, groups, filters, row_local, N2)
    taps_block = filter_taps.reshape(1, 1, filters, row_local, N2)
    pair_whole, taps_whole = (
        lax.all_to_all(pair, "ctx", split_axis=2, concat_axis=3, tiled=True),
        lax.all_to_all(taps_block, "ctx", split_axis=2, concat_axis=3, tiled=True),
    )
    signal_count = 2 * groups * spread_count
    every = jnp.concatenate(
        [
            pair_whole.reshape(signal_count, row_total, N2),
            taps_whole.reshape(spread_count, row_total, N2),
        ],
        axis=0,
    )
    first = jnp.einsum("km,imn->ikn", first_forward, every, preferred_element_type=jnp.float32)
    first_real = first[:, :N1]
    first_imaginary = first[:, N1:]
    turned = jnp.stack(
        [
            first_real * full_real - first_imaginary * full_imaginary,
            first_real * full_imaginary + first_imaginary * full_real,
        ],
        axis=1,
    ).astype(jnp.bfloat16)
    spectra = jnp.einsum(
        "ipkn,pnl->ikl", turned, second_forward, preferred_element_type=jnp.float32
    )
    signal_spec = spectra[:signal_count].reshape(2, groups * spread_count, N1, 2 * N2)
    filter_spec = spectra[signal_count:].astype(jnp.bfloat16)
    filter_spec = jnp.transpose(filter_spec, (1, 0, 2))
    mix_spec = jnp.transpose(signal_spec[0], (1, 0, 2))
    weight_spec = jnp.transpose(signal_spec[1], (1, 0, 2))
    made = spectral_products(mix_spec, weight_spec, filter_spec, ["convolve", "correlate", "lag"])
    stacked = jnp.transpose(jnp.concatenate(made, axis=1), (1, 0, 2))
    back = jnp.einsum("ikl,lm->ikm", stacked, second_inverse, preferred_element_type=jnp.float32)
    back_real, back_imaginary = halves(back)
    rotated = jnp.stack(
        [
            (back_real * full_real + back_imaginary * full_imaginary) * inverse_scale,
            (back_imaginary * full_real - back_real * full_imaginary) * inverse_scale,
        ],
        axis=1,
    ).astype(jnp.bfloat16)
    inverted = jnp.einsum(
        "mkp,ipkn->imn", first_inverse, rotated, preferred_element_type=jnp.float32
    )
    inverted = inverted.astype(jnp.bfloat16).reshape(3, groups, spread_count, row_total, N2)
    back_rows = lax.all_to_all(inverted[:2], "ctx", split_axis=3, concat_axis=2, tiled=True)
    convolved = back_rows[0].reshape(channels, local_len)
    correlated = back_rows[1].reshape(channels, local_len)
    lag_whole = jnp.sum(inverted[2].astype(jnp.float32), axis=0)
    lag_part = (
        lax.all_to_all(
            lag_whole.astype(jnp.bfloat16), "ctx", split_axis=1, concat_axis=0, tiled=True
        )
        .astype(lag_whole.dtype)
        .reshape(filters, local_len)
    )
    summed = convolved.astype(jnp.float32) + skip_gain[:, None] * mixed_input.astype(jnp.float32)
    outputs = (output_gate.astype(jnp.float32) * summed).astype(jnp.bfloat16)
    grad_output_gate = (cotangent.astype(jnp.float32) * summed).astype(jnp.bfloat16)
    back_total = correlated.astype(jnp.float32) + skip_gain[:, None] * weighted.astype(jnp.float32)
    grad_input_gate = (back_total * values.astype(jnp.float32)).astype(jnp.bfloat16)
    grad_values = (back_total * input_gate.astype(jnp.float32)).astype(jnp.bfloat16)
    lag_total = lax.psum(lag_part.astype(jnp.bfloat16), "dp").astype(jnp.float32)
    grad_filter = lag_total * envelope * filter_scale
    return (outputs, grad_input_gate, grad_output_gate, grad_values, grad_filter)


LANES = 128
CHUNKS = 4
STRIP = 16


def block_tables(rows):
    length = 2 * rows * LANES
    k = np.arange(rows)
    m = np.arange(rows)
    n = np.arange(LANES)
    first = np.exp(-1j * np.pi * (np.outer(2 * k + 1, m) % (4 * rows)) / (2 * rows))
    turn = np.exp(-1j * np.pi * (np.outer(2 * k + 1, n) % (2 * length)) / length)
    second = np.exp(-2j * np.pi * (np.outer(n, n) % LANES) / LANES)
    first_forward = np.concatenate([first.real, first.imag], axis=0)
    first_inverse = np.concatenate([first.real.T, first.imag.T], axis=1)
    second_forward = np.block([[second.real, second.imag], [-second.imag, second.real]])
    second_inverse = np.block([[second.real, -second.imag], [second.imag, second.real]])
    half = ml_dtypes.bfloat16
    turns = np.stack([turn.real, turn.imag]).astype(np.float32)
    return tuple(
        jnp.asarray(table)
        for table in (
            first_forward.astype(half),
            second_forward.astype(half),
            second_inverse.astype(half),
            first_inverse.astype(half),
            turns,
            (turns * np.float32(2.0 / length)),
        )
    )


def block_kernel(
    side_ref,
    own_ref,
    far_ref,
    other_own_ref,
    other_next_ref,
    other_far_ref,
    taps_ref,
    first_forward_ref,
    second_forward_ref,
    second_inverse_ref,
    first_inverse_ref,
    turn_ref,
    back_turn_ref,
    near_out_ref,
    other_out_ref,
    passed_out_ref,
    lag_out_ref,
    spectra,
    products,
):
    groups, _, rows, lanes = own_ref.shape
    side = side_ref[0]
    signals = (own_ref, far_ref, other_own_ref, other_next_ref, other_far_ref, taps_ref)
    for number, signal in enumerate(signals):
        for pair in range(signal.shape[0] // 2):
            both = jnp.concatenate([signal[2 * pair, 0], signal[2 * pair + 1, 0]], axis=1)
            first = jnp.dot(first_forward_ref[...], both, preferred_element_type=jnp.float32)
            for which in range(2):
                real = first[:rows, which * lanes : (which + 1) * lanes]
                imaginary = first[rows:, which * lanes : (which + 1) * lanes]
                turned = jnp.concatenate(
                    [
                        real * turn_ref[0] - imaginary * turn_ref[1],
                        real * turn_ref[1] + imaginary * turn_ref[0],
                    ],
                    axis=1,
                ).astype(jnp.bfloat16)
                spectra[number, 2 * pair + which] = jnp.dot(
                    turned, second_forward_ref[...], preferred_element_type=jnp.float32
                )

    row_index = lax.broadcasted_iota(jnp.int32, (STRIP, lanes), 0)
    parity = 1.0 - 2.0 * (row_index % 2).astype(jnp.float32)

    def strip(step, carry):
        at = pl.ds(pl.multiple_of(step * STRIP, STRIP), STRIP)

        def load(number, which):
            return spectra[number, which, at, :lanes], spectra[number, which, at, lanes:]

        def store(number, real, imaginary):
            products[number, at, :lanes] = real.astype(jnp.bfloat16)
            products[number, at, lanes:] = imaginary.astype(jnp.bfloat16)

        filters = [load(5, delay) for delay in range(4)]
        gains = []
        for delay in range(4):
            real, imaginary = filters[delay]
            if delay:
                before_real, before_imaginary = filters[delay - 1]
                real = real - parity * before_imaginary
                imaginary = imaginary + parity * before_real
            gains.append((real, side * imaginary))
        lag = [(jnp.zeros((STRIP, lanes), jnp.float32),) * 2 for _ in range(4)]

        def times(total, left, right):
            real = left[0] * right[0] - left[1] * right[1]
            imaginary = left[0] * right[1] + left[1] * right[0]
            return (real, imaginary) if total is None else (total[0] + real, total[1] + imaginary)

        def conjugate_times(total, left, right):
            real = left[0] * right[0] + left[1] * right[1]
            imaginary = left[0] * right[1] - left[1] * right[0]
            return (real, imaginary) if total is None else (total[0] + real, total[1] + imaginary)

        for group in range(groups):
            own, far = load(0, group), load(1, group)
            near = times(times(None, gains[0], own), gains[1], far)
            store(group, *near)
            other_own, other_next, other_far = load(2, group), load(3, group), load(4, group)
            other = conjugate_times(None, gains[0], other_own)
            other = conjugate_times(other, gains[1], other_next)
            other = conjugate_times(other, gains[2], other_far)
            store(groups + group, *other)
            passed = conjugate_times(None, gains[1], other_own)
            passed = conjugate_times(passed, gains[2], other_next)
            passed = conjugate_times(passed, gains[3], other_far)
            store(2 * groups + group, *passed)
            half_own = (0.5 * own[0], 0.5 * own[1])
            lag[0] = conjugate_times(lag[0], own, other_own)
            lag[1] = conjugate_times(lag[1], far, other_own)
            lag[1] = conjugate_times(lag[1], half_own, other_next)
            lag[2] = conjugate_times(lag[2], far, other_next)
            lag[3] = conjugate_times(lag[3], far, other_far)
        lag[3] = (0.5 * lag[3][0], 0.5 * lag[3][1])
        for delay in range(4):
            real, imaginary = lag[delay][0], side * lag[delay][1]
            if delay < 3:
                real = real + parity * (side * lag[delay + 1][1])
                imaginary = imaginary - parity * lag[delay + 1][0]
            store(3 * groups + delay, real, imaginary)
        return carry

    lax.fori_loop(0, rows // STRIP, strip, 0)

    for kind, out_ref in enumerate((near_out_ref, other_out_ref, passed_out_ref, lag_out_ref)):
        for pair in range(out_ref.shape[0] // 2):
            real_parts, imaginary_parts = [], []
            for which in range(2):
                back = jnp.dot(
                    products[kind * groups + 2 * pair + which],
                    second_inverse_ref[...],
                    preferred_element_type=jnp.float32,
                )
                real, imaginary = back[:, :lanes], back[:, lanes:]
                real_parts.append(
                    (real * back_turn_ref[0] + imaginary * back_turn_ref[1]).astype(jnp.bfloat16)
                )
                imaginary_parts.append(
                    (imaginary * back_turn_ref[0] - real * back_turn_ref[1]).astype(jnp.bfloat16)
                )
            rotated = jnp.concatenate(
                [jnp.concatenate(real_parts, axis=1), jnp.concatenate(imaginary_parts, axis=1)],
                axis=0,
            )
            result = jnp.dot(first_inverse_ref[...], rotated, preferred_element_type=jnp.float32)
            result = result.astype(jnp.bfloat16)
            out_ref[2 * pair, 0] = result[:, :lanes]
            out_ref[2 * pair + 1, 0] = result[:, lanes:]


def block_products(side, signals, taps, tables):
    groups, filters, rows, lanes = signals[0].shape
    block = pl.BlockSpec((groups, 1, rows, lanes), lambda f: (0, f, 0, 0))
    taps_block = pl.BlockSpec((4, 1, rows, lanes), lambda f: (0, f, 0, 0))

    def whole(table):
        return pl.BlockSpec(table.shape, lambda f: (0,) * table.ndim)

    made = jax.ShapeDtypeStruct(signals[0].shape, jnp.bfloat16)
    lag = jax.ShapeDtypeStruct((4, filters, rows, lanes), jnp.bfloat16)
    transforms = filters * (9 * groups + 8)
    return pl.pallas_call(
        block_kernel,
        grid=(filters,),
        in_specs=[pl.BlockSpec(memory_space=pltpu.SMEM)]
        + [block] * 5
        + [taps_block]
        + [whole(table) for table in tables],
        out_specs=[block, block, block, taps_block],
        out_shape=[made, made, made, lag],
        scratch_shapes=[
            pltpu.VMEM((6, groups, rows, 2 * lanes), jnp.float32),
            pltpu.VMEM((3 * groups + 4, rows, 2 * lanes), jnp.bfloat16),
        ],
        compiler_params=pltpu.CompilerParams(vmem_limit_bytes=48 * 2**20),
        cost_estimate=pl.CostEstimate(
            flops=transforms * 2 * (2 * rows * rows * lanes + rows * 4 * lanes * lanes),
            bytes_accessed=filters * (8 * groups + 8) * rows * lanes * 2,
            transcendentals=0,
        ),
    )(side, *signals, taps, *tables)


def block_shards(input_gate, output_gate, values, cotangent, filter_raw, filter_decay, skip_gain):
    context_index = lax.axis_index("ctx")
    channels, local_len = input_gate.shape
    filters = filter_raw.shape[0]
    groups = channels // filters
    rows = local_len // LANES
    seq_len = local_len * lax.axis_size("ctx")
    tables = block_tables(rows)
    near_start = context_index < 2
    side = jnp.where(near_start, 1.0, -1.0).astype(jnp.float32).reshape(1)

    def product(left, right):
        return (left.astype(jnp.float32) * right.astype(jnp.float32)).astype(jnp.bfloat16)

    mixed_input = product(input_gate, values)
    weighted = product(cotangent, output_gate)
    own = jnp.where(near_start, mixed_input, weighted).reshape(groups, filters, rows, LANES)
    other = jnp.where(near_start, weighted, mixed_input).reshape(groups, filters, rows, LANES)

    positions = (context_index * local_len + jnp.arange(local_len, dtype=jnp.int32)).astype(
        jnp.float32
    )
    filter_scale = seq_len ** (-0.5)

    def envelope(decay):
        return jnp.exp(-decay[:, None] * (positions[None, :] / seq_len))

    share = filters // lax.axis_size("dp")
    first_filter = lax.axis_index("dp") * share
    raw_share = lax.dynamic_slice_in_dim(filter_raw, first_filter, share, 0)
    decay_share = lax.dynamic_slice_in_dim(filter_decay, first_filter, share, 0)
    taps = (raw_share.astype(jnp.float32) * envelope(decay_share) * filter_scale).astype(
        jnp.bfloat16
    )
    taps = lax.all_gather(taps[None], "ctx", axis=0, tiled=True)
    taps = lax.all_gather(taps, "dp", axis=1, tiled=True)
    taps = taps.reshape(4, filters, rows, LANES)

    part = filters // CHUNKS
    near_parts, other_parts, lag_parts = [], [], []
    for chunk in range(CHUNKS):
        chosen = slice(chunk * part, (chunk + 1) * part)
        own_part = own[:, chosen]
        other_next = lax.ppermute(own_part, "ctx", [(1, 2), (2, 1)])
        other_far = lax.ppermute(own_part, "ctx", [(0, 2), (3, 1)])
        far = lax.ppermute(own_part, "ctx", [(0, 1), (3, 2)])
        near_out, other_out, passed, lag = block_products(
            side,
            (own_part, far, other[:, chosen], other_next, other_far),
            taps[:, chosen],
            tables,
        )
        received = lax.ppermute(passed, "ctx", [(1, 0), (2, 3)])
        near_parts.append(near_out)
        other_parts.append(other_out.astype(jnp.float32) + received.astype(jnp.float32))
        lag_parts.append(lag)
    near_whole = jnp.concatenate(near_parts, axis=1).reshape(channels, local_len)
    other_whole = jnp.concatenate(other_parts, axis=1).reshape(channels, local_len)
    near_whole = near_whole.astype(jnp.float32)
    convolved = jnp.where(near_start, near_whole, other_whole)
    correlated = jnp.where(near_start, other_whole, near_whole)

    summed = convolved + skip_gain[:, None] * mixed_input.astype(jnp.float32)
    outputs = (output_gate.astype(jnp.float32) * summed).astype(jnp.bfloat16)
    grad_output_gate = (cotangent.astype(jnp.float32) * summed).astype(jnp.bfloat16)
    back_total = correlated + skip_gain[:, None] * weighted.astype(jnp.float32)
    grad_input_gate = (back_total * values.astype(jnp.float32)).astype(jnp.bfloat16)
    grad_values = (back_total * input_gate.astype(jnp.float32)).astype(jnp.bfloat16)

    lag = jnp.concatenate(lag_parts, axis=1).reshape(4, filters, local_len)
    lag = lax.psum_scatter(lag, "dp", scatter_dimension=1, tiled=True)
    lag = lax.psum_scatter(lag, "ctx", scatter_dimension=0, tiled=True)
    lag = lax.all_gather(lag[0], "dp", axis=0, tiled=True)
    grad_filter = lag.astype(jnp.float32) * envelope(filter_decay) * filter_scale
    return (outputs, grad_input_gate, grad_output_gate, grad_values, grad_filter)


def chosen_shards(dp, ctx):
    def run(input_gate, *others):
        channels, local_len = input_gate.shape
        filters = others[3].shape[0]
        by_blocks = (
            ctx == 4
            and local_len % (LANES * STRIP) == 0
            and channels % (2 * filters) == 0
            and filters % dp == 0
            and filters % CHUNKS == 0
        )
        return (block_shards if by_blocks else shards)(input_gate, *others)

    return run


def solution(mesh):
    return jax.shard_map(
        chosen_shards(mesh.shape["dp"], mesh.shape["ctx"]),
        mesh=mesh,
        in_specs=(
            P("dp", "ctx"),
            P("dp", "ctx"),
            P("dp", "ctx"),
            P("dp", "ctx"),
            P(None, "ctx"),
            P(),
            P("dp"),
        ),
        out_specs=(P("dp", "ctx"), P("dp", "ctx"), P("dp", "ctx"), P("dp", "ctx"), P(None, "ctx")),
        check_vma=False,
    )
```

```python
import math

import jax
import jax.numpy as jnp
import ml_dtypes
import numpy as np
from jax import lax
from jax.experimental import pallas as pl
from jax.experimental.pallas import tpu as pltpu
from jax.sharding import PartitionSpec as P

N1 = 512
N2 = 512
FFT_LEN = 262144


two_pi = 2.0 * math.pi


def first_tables(row_total):
    first_index = jnp.arange(N1, dtype=jnp.int32)
    source_rows = jnp.arange(row_total, dtype=jnp.int32)
    angles = (first_index[:, None] * source_rows[None, :] % N1).astype(jnp.float32) * (two_pi / N1)
    cosine = jnp.cos(angles).astype(jnp.bfloat16)
    minus_sine = (-jnp.sin(angles)).astype(jnp.bfloat16)
    forward_table = jnp.concatenate([cosine, minus_sine], axis=0)
    inverse_table = jnp.stack([cosine.T, minus_sine.T], axis=2)
    return (forward_table, inverse_table)


def second_tables():
    second_index = jnp.arange(N2, dtype=jnp.int32)
    angles = (second_index[:, None] * second_index[None, :] % N2).astype(jnp.float32) * (
        two_pi / N2
    )
    cosine = jnp.cos(angles).astype(jnp.bfloat16)
    minus_sine = (-jnp.sin(angles)).astype(jnp.bfloat16)
    forward_table = jnp.stack(
        [
            jnp.concatenate([cosine, minus_sine], axis=1),
            jnp.concatenate([-minus_sine, cosine], axis=1),
        ],
        axis=0,
    )
    inverse_table = jnp.concatenate(
        [
            jnp.concatenate([cosine, -minus_sine], axis=1),
            jnp.concatenate([minus_sine, cosine], axis=1),
        ],
        axis=0,
    )
    return (forward_table, inverse_table)


def twiddle_table(spectrum_rows, columns):
    angles = (spectrum_rows[:, None] * columns[None, :] % FFT_LEN).astype(jnp.float32) * (
        two_pi / FFT_LEN
    )
    return (jnp.cos(angles), -jnp.sin(angles))


def halves(array):
    return (array[..., :N2], array[..., N2:])


def joined(real_part, imaginary_part):
    return jnp.concatenate([real_part, imaginary_part], axis=-1).astype(jnp.bfloat16)


def spectral_products(mix_spec, weight_spec, filter_spec, which):
    lead = mix_spec.shape[:-2]
    filters = filter_spec.shape[-2]
    filter_real, filter_imaginary = halves(filter_spec.astype(jnp.float32))
    filter_real = jnp.expand_dims(filter_real, -3)
    filter_imaginary = jnp.expand_dims(filter_imaginary, -3)
    outcome = []
    mix_real, mix_imaginary = halves(mix_spec.reshape(lead + (-1, filters, 2 * N2)))
    weight_real, weight_imaginary = halves(weight_spec.reshape(lead + (-1, filters, 2 * N2)))
    for name in which:
        if name == "convolve":
            made = joined(
                mix_real * filter_real - mix_imaginary * filter_imaginary,
                mix_real * filter_imaginary + mix_imaginary * filter_real,
            )
        elif name == "correlate":
            made = joined(
                filter_real * weight_real + filter_imaginary * weight_imaginary,
                filter_real * weight_imaginary - filter_imaginary * weight_real,
            )
        else:
            made = joined(
                mix_real * weight_real + mix_imaginary * weight_imaginary,
                mix_real * weight_imaginary - mix_imaginary * weight_real,
            )
        outcome.append(made.reshape(lead + (-1, 2 * N2)))
    return outcome


def shards(input_gate, output_gate, values, cotangent, filter_raw, filter_decay, skip_gain):
    context_size = lax.axis_size("ctx")
    context_index = lax.axis_index("ctx")
    channels, local_len = input_gate.shape
    filters = filter_raw.shape[0]
    groups = channels // filters
    row_local = local_len // N2
    row_total = row_local * context_size
    seq_len = local_len * context_size
    first_forward, first_inverse = first_tables(row_total)
    second_forward, second_inverse = second_tables()
    inverse_scale = 1.0 / FFT_LEN
    mixed_input = (input_gate.astype(jnp.float32) * values.astype(jnp.float32)).astype(jnp.bfloat16)
    weighted = (cotangent.astype(jnp.float32) * output_gate.astype(jnp.float32)).astype(
        jnp.bfloat16
    )
    global_positions = (context_index * local_len + jnp.arange(local_len, dtype=jnp.int32)).astype(
        jnp.float32
    )
    envelope = jnp.exp(-filter_decay[:, None] * (global_positions[None, :] / seq_len))
    filter_scale = seq_len ** (-0.5)
    filter_taps = (filter_raw.astype(jnp.float32) * envelope * filter_scale).astype(jnp.bfloat16)
    spread_count = filters // context_size
    full_real, full_imaginary = twiddle_table(
        jnp.arange(N1, dtype=jnp.int32), jnp.arange(N2, dtype=jnp.int32)
    )
    pair = jnp.stack([mixed_input, weighted], axis=0).reshape(2, groups, filters, row_local, N2)
    taps_block = filter_taps.reshape(1, 1, filters, row_local, N2)
    pair_whole, taps_whole = (
        lax.all_to_all(pair, "ctx", split_axis=2, concat_axis=3, tiled=True),
        lax.all_to_all(taps_block, "ctx", split_axis=2, concat_axis=3, tiled=True),
    )
    signal_count = 2 * groups * spread_count
    every = jnp.concatenate(
        [
            pair_whole.reshape(signal_count, row_total, N2),
            taps_whole.reshape(spread_count, row_total, N2),
        ],
        axis=0,
    )
    first = jnp.einsum("km,imn->ikn", first_forward, every, preferred_element_type=jnp.float32)
    first_real = first[:, :N1]
    first_imaginary = first[:, N1:]
    turned = jnp.stack(
        [
            first_real * full_real - first_imaginary * full_imaginary,
            first_real * full_imaginary + first_imaginary * full_real,
        ],
        axis=1,
    ).astype(jnp.bfloat16)
    spectra = jnp.einsum(
        "ipkn,pnl->ikl", turned, second_forward, preferred_element_type=jnp.float32
    )
    signal_spec = spectra[:signal_count].reshape(2, groups * spread_count, N1, 2 * N2)
    filter_spec = spectra[signal_count:].astype(jnp.bfloat16)
    filter_spec = jnp.transpose(filter_spec, (1, 0, 2))
    mix_spec = jnp.transpose(signal_spec[0], (1, 0, 2))
    weight_spec = jnp.transpose(signal_spec[1], (1, 0, 2))
    made = spectral_products(mix_spec, weight_spec, filter_spec, ["convolve", "correlate", "lag"])
    stacked = jnp.transpose(jnp.concatenate(made, axis=1), (1, 0, 2))
    back = jnp.einsum("ikl,lm->ikm", stacked, second_inverse, preferred_element_type=jnp.float32)
    back_real, back_imaginary = halves(back)
    rotated = jnp.stack(
        [
            (back_real * full_real + back_imaginary * full_imaginary) * inverse_scale,
            (back_imaginary * full_real - back_real * full_imaginary) * inverse_scale,
        ],
        axis=1,
    ).astype(jnp.bfloat16)
    inverted = jnp.einsum(
        "mkp,ipkn->imn", first_inverse, rotated, preferred_element_type=jnp.float32
    )
    inverted = inverted.astype(jnp.bfloat16).reshape(3, groups, spread_count, row_total, N2)
    back_rows = lax.all_to_all(inverted[:2], "ctx", split_axis=3, concat_axis=2, tiled=True)
    convolved = back_rows[0].reshape(channels, local_len)
    correlated = back_rows[1].reshape(channels, local_len)
    lag_whole = jnp.sum(inverted[2].astype(jnp.float32), axis=0)
    lag_part = (
        lax.all_to_all(
            lag_whole.astype(jnp.bfloat16), "ctx", split_axis=1, concat_axis=0, tiled=True
        )
        .astype(lag_whole.dtype)
        .reshape(filters, local_len)
    )
    summed = convolved.astype(jnp.float32) + skip_gain[:, None] * mixed_input.astype(jnp.float32)
    outputs = (output_gate.astype(jnp.float32) * summed).astype(jnp.bfloat16)
    grad_output_gate = (cotangent.astype(jnp.float32) * summed).astype(jnp.bfloat16)
    back_total = correlated.astype(jnp.float32) + skip_gain[:, None] * weighted.astype(jnp.float32)
    grad_input_gate = (back_total * values.astype(jnp.float32)).astype(jnp.bfloat16)
    grad_values = (back_total * input_gate.astype(jnp.float32)).astype(jnp.bfloat16)
    lag_total = lax.psum(lag_part.astype(jnp.bfloat16), "dp").astype(jnp.float32)
    grad_filter = lag_total * envelope * filter_scale
    return (outputs, grad_input_gate, grad_output_gate, grad_values, grad_filter)


LANES = 128
SHARES = (6, 5, 3, 2)
STRIP = 16
EDGE_ROWS = 16


def block_tables(rows):
    length = 2 * rows * LANES
    k = np.arange(rows)
    m = np.arange(rows)
    n = np.arange(LANES)
    first = np.exp(-1j * np.pi * (np.outer(2 * k + 1, m) % (4 * rows)) / (2 * rows))
    turn = np.exp(-1j * np.pi * (np.outer(2 * k + 1, n) % (2 * length)) / length)
    second = np.exp(-2j * np.pi * (np.outer(n, n) % LANES) / LANES)
    first_forward = np.concatenate([first.real, first.imag], axis=0)
    first_inverse = np.concatenate([first.real.T, first.imag.T], axis=1)
    second_forward = np.block([[second.real, second.imag], [-second.imag, second.real]])
    second_inverse = np.block([[second.real, -second.imag], [second.imag, second.real]])
    half = ml_dtypes.bfloat16
    turns = np.stack([turn.real, turn.imag]).astype(np.float32)
    return tuple(
        jnp.asarray(table)
        for table in (
            first_forward.astype(half),
            second_forward.astype(half),
            second_inverse.astype(half),
            first_inverse.astype(half),
            turns,
            (turns * np.float32(2.0 / length)),
        )
    )


def block_kernel(
    side_ref,
    own_ref,
    far_ref,
    other_own_ref,
    other_next_ref,
    other_far_ref,
    taps_ref,
    first_forward_ref,
    second_forward_ref,
    second_inverse_ref,
    first_inverse_ref,
    turn_ref,
    back_turn_ref,
    near_out_ref,
    other_out_ref,
    passed_out_ref,
    lag_out_ref,
    spectra,
    products,
):
    groups, _, rows, lanes = own_ref.shape
    side = side_ref[0]
    signals = (own_ref, far_ref, other_own_ref, other_next_ref, other_far_ref, taps_ref)
    for number, signal in enumerate(signals):
        for pair in range(signal.shape[0] // 2):
            both = jnp.concatenate([signal[2 * pair, 0], signal[2 * pair + 1, 0]], axis=1)
            first = jnp.dot(first_forward_ref[...], both, preferred_element_type=jnp.float32)
            for which in range(2):
                real = first[:rows, which * lanes : (which + 1) * lanes]
                imaginary = first[rows:, which * lanes : (which + 1) * lanes]
                turned = jnp.concatenate(
                    [
                        real * turn_ref[0] - imaginary * turn_ref[1],
                        real * turn_ref[1] + imaginary * turn_ref[0],
                    ],
                    axis=1,
                ).astype(jnp.bfloat16)
                spectra[number, 2 * pair + which] = jnp.dot(
                    turned, second_forward_ref[...], preferred_element_type=jnp.float32
                )

    row_index = lax.broadcasted_iota(jnp.int32, (STRIP, lanes), 0)
    parity = 1.0 - 2.0 * (row_index % 2).astype(jnp.float32)

    def strip(step, carry):
        at = pl.ds(pl.multiple_of(step * STRIP, STRIP), STRIP)

        def load(number, which):
            return spectra[number, which, at, :lanes], spectra[number, which, at, lanes:]

        def store(number, real, imaginary):
            products[number, at, :lanes] = real.astype(jnp.bfloat16)
            products[number, at, lanes:] = imaginary.astype(jnp.bfloat16)

        filters = [load(5, delay) for delay in range(4)]
        gains = []
        for delay in range(4):
            real, imaginary = filters[delay]
            if delay:
                before_real, before_imaginary = filters[delay - 1]
                real = real - parity * before_imaginary
                imaginary = imaginary + parity * before_real
            gains.append((real, side * imaginary))
        lag = [(jnp.zeros((STRIP, lanes), jnp.float32),) * 2 for _ in range(4)]

        def times(total, left, right):
            real = left[0] * right[0] - left[1] * right[1]
            imaginary = left[0] * right[1] + left[1] * right[0]
            return (real, imaginary) if total is None else (total[0] + real, total[1] + imaginary)

        def conjugate_times(total, left, right):
            real = left[0] * right[0] + left[1] * right[1]
            imaginary = left[0] * right[1] - left[1] * right[0]
            return (real, imaginary) if total is None else (total[0] + real, total[1] + imaginary)

        for group in range(groups):
            own, far = load(0, group), load(1, group)
            near = times(times(None, gains[0], own), gains[1], far)
            store(group, *near)
            other_own, other_next, other_far = load(2, group), load(3, group), load(4, group)
            other = conjugate_times(None, gains[0], other_own)
            other = conjugate_times(other, gains[1], other_next)
            other = conjugate_times(other, gains[2], other_far)
            store(groups + group, *other)
            passed = conjugate_times(None, gains[1], other_own)
            passed = conjugate_times(passed, gains[2], other_next)
            passed = conjugate_times(passed, gains[3], other_far)
            store(2 * groups + group, *passed)
            half_own = (0.5 * own[0], 0.5 * own[1])
            lag[0] = conjugate_times(lag[0], own, other_own)
            lag[1] = conjugate_times(lag[1], far, other_own)
            lag[1] = conjugate_times(lag[1], half_own, other_next)
            lag[2] = conjugate_times(lag[2], far, other_next)
            lag[3] = conjugate_times(lag[3], far, other_far)
        lag[3] = (0.5 * lag[3][0], 0.5 * lag[3][1])
        for delay in range(4):
            real, imaginary = lag[delay][0], side * lag[delay][1]
            if delay < 3:
                real = real + parity * (side * lag[delay + 1][1])
                imaginary = imaginary - parity * lag[delay + 1][0]
            store(3 * groups + delay, real, imaginary)
        return carry

    lax.fori_loop(0, rows // STRIP, strip, 0)

    shares = lag_out_ref.shape[0]
    for kind, out_ref in enumerate((near_out_ref, other_out_ref, passed_out_ref, None)):
        for pair in range((groups if kind < 3 else 4) // 2):
            real_parts, imaginary_parts = [], []
            for which in range(2):
                back = jnp.dot(
                    products[kind * groups + 2 * pair + which],
                    second_inverse_ref[...],
                    preferred_element_type=jnp.float32,
                )
                real, imaginary = back[:, :lanes], back[:, lanes:]
                real_parts.append(
                    (real * back_turn_ref[0] + imaginary * back_turn_ref[1]).astype(jnp.bfloat16)
                )
                imaginary_parts.append(
                    (imaginary * back_turn_ref[0] - real * back_turn_ref[1]).astype(jnp.bfloat16)
                )
            rotated = jnp.concatenate(
                [jnp.concatenate(real_parts, axis=1), jnp.concatenate(imaginary_parts, axis=1)],
                axis=0,
            )
            result = jnp.dot(first_inverse_ref[...], rotated, preferred_element_type=jnp.float32)
            result = result.astype(jnp.bfloat16)
            for which in range(2):
                column = result[:, which * lanes : (which + 1) * lanes]
                if kind < 3:
                    out_ref[2 * pair + which, 0] = column
                else:
                    column = column.reshape(shares, rows // shares, lanes)
                    lag_out_ref[:, 2 * pair + which, 0] = column


def block_products(side, signals, other, taps, tables, start, shares):
    groups, filters, rows, lanes = signals[0].shape
    block = pl.BlockSpec((groups, 1, rows, lanes), lambda f: (0, f, 0, 0))
    other_block = pl.BlockSpec((groups, 1, rows, lanes), lambda f: (0, f + start, 0, 0))
    taps_block = pl.BlockSpec((4, 1, rows, lanes), lambda f: (0, f + start, 0, 0))
    lag_block = pl.BlockSpec((shares, 4, 1, rows // shares, lanes), lambda f: (0, 0, f, 0, 0))

    def whole(table):
        return pl.BlockSpec(table.shape, lambda f: (0,) * table.ndim)

    made = jax.ShapeDtypeStruct(signals[0].shape, jnp.bfloat16)
    lag = jax.ShapeDtypeStruct((shares, 4, filters, rows // shares, lanes), jnp.bfloat16)
    transforms = filters * (9 * groups + 8)
    own, far, other_next, other_far = signals
    return pl.pallas_call(
        block_kernel,
        grid=(filters,),
        in_specs=[pl.BlockSpec(memory_space=pltpu.SMEM)]
        + [block, block, other_block, block, block, taps_block]
        + [whole(table) for table in tables],
        out_specs=[block, block, block, lag_block],
        out_shape=[made, made, made, lag],
        scratch_shapes=[
            pltpu.VMEM((6, groups, rows, 2 * lanes), jnp.float32),
            pltpu.VMEM((3 * groups + 4, rows, 2 * lanes), jnp.bfloat16),
        ],
        compiler_params=pltpu.CompilerParams(vmem_limit_bytes=48 * 2**20),
        cost_estimate=pl.CostEstimate(
            flops=transforms * 2 * (2 * rows * rows * lanes + rows * 4 * lanes * lanes),
            bytes_accessed=filters * (8 * groups + 8) * rows * lanes * 2,
            transcendentals=0,
        ),
    )(side, own, far, other, other_next, other_far, taps, *tables)


def product(left, right):
    return (left.astype(jnp.float32) * right.astype(jnp.float32)).astype(jnp.bfloat16)


def enter_kernel(side_ref, gate_ref, values_ref, cotangent_ref, out_gate_ref, *out_refs):
    channels, width = gate_ref.shape
    *own_refs, other_ref = out_refs
    groups, filters, rows, lanes = other_ref.shape
    near_start = side_ref[0] > 0
    mixed = product(gate_ref[...], values_ref[...]).astype(jnp.float32)
    weighted = product(cotangent_ref[...], out_gate_ref[...]).astype(jnp.float32)

    def blocks(array):
        array = array.reshape(channels, rows, lanes).astype(jnp.bfloat16)
        return array.reshape(groups, filters, rows, lanes)

    own = blocks(jnp.where(near_start, mixed, weighted))
    start = 0
    for own_ref in own_refs:
        own_ref[...] = own[:, start : start + own_ref.shape[1]]
        start += own_ref.shape[1]
    other_ref[...] = blocks(jnp.where(near_start, weighted, mixed))


def enter(side, flat, filters):
    channels, local_len = flat[0].shape
    groups, rows = channels // filters, local_len // LANES
    counts = SHARES + (filters,)
    return pl.pallas_call(
        enter_kernel,
        grid=(rows // EDGE_ROWS,),
        in_specs=[pl.BlockSpec(memory_space=pltpu.SMEM)]
        + [pl.BlockSpec((channels, EDGE_ROWS * LANES), lambda i: (0, i))] * 4,
        out_specs=[
            pl.BlockSpec((groups, count, EDGE_ROWS, LANES), lambda i: (0, 0, i, 0))
            for count in counts
        ],
        out_shape=[
            jax.ShapeDtypeStruct((groups, count, rows, LANES), jnp.bfloat16) for count in counts
        ],
        compiler_params=pltpu.CompilerParams(vmem_limit_bytes=40 * 2**20),
        cost_estimate=pl.CostEstimate(
            flops=4 * channels * local_len,
            bytes_accessed=12 * channels * local_len,
            transcendentals=0,
        ),
    )(side, *flat)


def leave_kernel(side_ref, skip_ref, gate_ref, values_ref, cotangent_ref, out_gate_ref, *refs):
    channels, width = gate_ref.shape
    parts = len(SHARES)
    near_refs, other_refs = refs[:parts], refs[parts : 2 * parts]
    received_refs = refs[2 * parts : 3 * parts]
    outputs_ref, grad_gate_ref, grad_out_gate_ref, grad_values_ref = refs[3 * parts :]
    near_start = side_ref[0] > 0

    def flat(part_refs):
        whole = jnp.concatenate([ref[...] for ref in part_refs], axis=1).astype(jnp.float32)
        return whole.reshape(channels, width // LANES, LANES).reshape(channels, width)

    near = flat(near_refs)
    other = flat(other_refs) + flat(received_refs)
    skip = skip_ref[...]
    gate, values = gate_ref[...].astype(jnp.float32), values_ref[...].astype(jnp.float32)
    cotangent = cotangent_ref[...].astype(jnp.float32)
    out_gate = out_gate_ref[...].astype(jnp.float32)
    mixed = (gate * values).astype(jnp.bfloat16).astype(jnp.float32)
    weighted = (cotangent * out_gate).astype(jnp.bfloat16).astype(jnp.float32)
    summed = jnp.where(near_start, near, other) + skip * mixed
    outputs_ref[...] = (out_gate * summed).astype(jnp.bfloat16)
    grad_out_gate_ref[...] = (cotangent * summed).astype(jnp.bfloat16)
    back_total = jnp.where(near_start, other, near) + skip * weighted
    grad_gate_ref[...] = (back_total * values).astype(jnp.bfloat16)
    grad_values_ref[...] = (back_total * gate).astype(jnp.bfloat16)


def leave(side, skip_gain, flat, near_parts, other_parts, received_parts):
    channels, local_len = flat[0].shape
    parts = (*near_parts, *other_parts, *received_parts)
    flat_block = pl.BlockSpec((channels, EDGE_ROWS * LANES), lambda i: (0, i))
    return pl.pallas_call(
        leave_kernel,
        grid=(local_len // (EDGE_ROWS * LANES),),
        in_specs=[
            pl.BlockSpec(memory_space=pltpu.SMEM),
            pl.BlockSpec((channels, 1), lambda i: (0, 0)),
        ]
        + [flat_block] * 4
        + [
            pl.BlockSpec((*part.shape[:2], EDGE_ROWS, LANES), lambda i: (0, 0, i, 0))
            for part in parts
        ],
        out_specs=[flat_block] * 4,
        out_shape=[jax.ShapeDtypeStruct((channels, local_len), jnp.bfloat16)] * 4,
        compiler_params=pltpu.CompilerParams(vmem_limit_bytes=40 * 2**20),
        cost_estimate=pl.CostEstimate(
            flops=12 * channels * local_len,
            bytes_accessed=22 * channels * local_len,
            transcendentals=0,
        ),
    )(side, skip_gain[:, None], *flat, *parts)


def after(array, *earlier):
    return lax.optimization_barrier((array, *earlier))[0]


def block_shards(input_gate, output_gate, values, cotangent, filter_raw, filter_decay, skip_gain):
    context_index = lax.axis_index("ctx")
    channels, local_len = input_gate.shape
    filters = filter_raw.shape[0]
    rows = local_len // LANES
    seq_len = local_len * lax.axis_size("ctx")
    data_size = lax.axis_size("dp")
    tables = block_tables(rows)
    side = jnp.where(context_index < 2, 1.0, -1.0).astype(jnp.float32).reshape(1)
    flat = (input_gate, values, cotangent, output_gate)
    *own_parts, other = enter(side, flat, filters)

    positions = (context_index * local_len + jnp.arange(local_len, dtype=jnp.int32)).astype(
        jnp.float32
    )
    filter_scale = seq_len ** (-0.5)

    def envelope(decay):
        return jnp.exp(-decay[:, None] * (positions[None, :] / seq_len))

    share = filters // data_size
    first_filter = lax.axis_index("dp") * share
    raw_share = lax.dynamic_slice_in_dim(filter_raw, first_filter, share, 0)
    decay_share = lax.dynamic_slice_in_dim(filter_decay, first_filter, share, 0)
    taps = (raw_share.astype(jnp.float32) * envelope(decay_share) * filter_scale).astype(
        jnp.bfloat16
    )
    taps = after(taps.reshape(1, share, rows, LANES), own_parts[0])
    taps = lax.all_gather(taps, "ctx", axis=0, tiled=True)
    taps = lax.all_gather(taps, "dp", axis=1, tiled=True)

    def lag_sum(pieces):
        pieces = lax.all_to_all(pieces, "ctx", split_axis=0, concat_axis=0, tiled=True)
        total = jnp.sum(pieces.astype(jnp.float32), axis=0).astype(jnp.bfloat16)
        return lax.all_gather(total, "dp", axis=1, tiled=True)

    near_parts, other_parts, received_parts, lag_parts = [], [], [], []
    start = 0
    for number, own in enumerate(own_parts):
        other_next = lax.ppermute(own, "ctx", [(1, 2), (2, 1)])
        other_far = lax.ppermute(own, "ctx", [(0, 2), (3, 1)])
        far = lax.ppermute(own, "ctx", [(0, 1), (3, 2)])
        if number >= 2:
            own = after(own, received_parts[number - 2], lag_parts[number - 2])
        near_out, other_out, passed, lag = block_products(
            side, (own, far, other_next, other_far), other, taps, tables, start, data_size
        )
        start += own.shape[1]
        near_parts.append(near_out)
        other_parts.append(other_out)
        received_parts.append(lax.ppermute(passed, "ctx", [(1, 0), (2, 3)]))
        lag = lax.all_to_all(lag, "dp", split_axis=0, concat_axis=0, tiled=True)
        lag_parts.append(jnp.sum(lag.astype(jnp.float32), axis=0).astype(jnp.bfloat16))
    lag = jnp.concatenate(
        [
            lag_sum(jnp.concatenate(lag_parts[:2], axis=1)),
            lag_sum(jnp.concatenate(lag_parts[2:], axis=1)),
        ],
        axis=0,
    ).reshape(filters, local_len)
    grad_filter = lag.astype(jnp.float32) * envelope(filter_decay) * filter_scale
    outputs, grad_input_gate, grad_output_gate, grad_values = leave(
        side, skip_gain, flat, near_parts, other_parts, received_parts
    )
    return (outputs, grad_input_gate, grad_output_gate, grad_values, grad_filter)


def chosen_shards(dp, ctx):
    def run(input_gate, *others):
        channels, local_len = input_gate.shape
        filters = others[3].shape[0]
        by_blocks = (
            ctx == 4
            and local_len % (LANES * STRIP * dp) == 0
            and local_len % (LANES * EDGE_ROWS) == 0
            and channels % (2 * filters) == 0
            and filters % dp == 0
            and filters == sum(SHARES)
        )
        return (block_shards if by_blocks else shards)(input_gate, *others)

    return run


def solution(mesh):
    return jax.shard_map(
        chosen_shards(mesh.shape["dp"], mesh.shape["ctx"]),
        mesh=mesh,
        in_specs=(
            P("dp", "ctx"),
            P("dp", "ctx"),
            P("dp", "ctx"),
            P("dp", "ctx"),
            P(None, "ctx"),
            P(),
            P("dp"),
        ),
        out_specs=(P("dp", "ctx"), P("dp", "ctx"), P("dp", "ctx"), P("dp", "ctx"), P(None, "ctx")),
        check_vma=False,
    )
```

```python
import math

import jax
import jax.numpy as jnp
import ml_dtypes
import numpy as np
from jax import lax
from jax.experimental import pallas as pl
from jax.experimental.pallas import tpu as pltpu
from jax.sharding import PartitionSpec as P

N1 = 512
N2 = 512
FFT_LEN = 262144


two_pi = 2.0 * math.pi


def first_tables(row_total):
    first_index = jnp.arange(N1, dtype=jnp.int32)
    source_rows = jnp.arange(row_total, dtype=jnp.int32)
    angles = (first_index[:, None] * source_rows[None, :] % N1).astype(jnp.float32) * (two_pi / N1)
    cosine = jnp.cos(angles).astype(jnp.bfloat16)
    minus_sine = (-jnp.sin(angles)).astype(jnp.bfloat16)
    forward_table = jnp.concatenate([cosine, minus_sine], axis=0)
    inverse_table = jnp.stack([cosine.T, minus_sine.T], axis=2)
    return (forward_table, inverse_table)


def second_tables():
    second_index = jnp.arange(N2, dtype=jnp.int32)
    angles = (second_index[:, None] * second_index[None, :] % N2).astype(jnp.float32) * (
        two_pi / N2
    )
    cosine = jnp.cos(angles).astype(jnp.bfloat16)
    minus_sine = (-jnp.sin(angles)).astype(jnp.bfloat16)
    forward_table = jnp.stack(
        [
            jnp.concatenate([cosine, minus_sine], axis=1),
            jnp.concatenate([-minus_sine, cosine], axis=1),
        ],
        axis=0,
    )
    inverse_table = jnp.concatenate(
        [
            jnp.concatenate([cosine, -minus_sine], axis=1),
            jnp.concatenate([minus_sine, cosine], axis=1),
        ],
        axis=0,
    )
    return (forward_table, inverse_table)


def twiddle_table(spectrum_rows, columns):
    angles = (spectrum_rows[:, None] * columns[None, :] % FFT_LEN).astype(jnp.float32) * (
        two_pi / FFT_LEN
    )
    return (jnp.cos(angles), -jnp.sin(angles))


def halves(array):
    return (array[..., :N2], array[..., N2:])


def joined(real_part, imaginary_part):
    return jnp.concatenate([real_part, imaginary_part], axis=-1).astype(jnp.bfloat16)


def spectral_products(mix_spec, weight_spec, filter_spec, which):
    lead = mix_spec.shape[:-2]
    filters = filter_spec.shape[-2]
    filter_real, filter_imaginary = halves(filter_spec.astype(jnp.float32))
    filter_real = jnp.expand_dims(filter_real, -3)
    filter_imaginary = jnp.expand_dims(filter_imaginary, -3)
    outcome = []
    mix_real, mix_imaginary = halves(mix_spec.reshape(lead + (-1, filters, 2 * N2)))
    weight_real, weight_imaginary = halves(weight_spec.reshape(lead + (-1, filters, 2 * N2)))
    for name in which:
        if name == "convolve":
            made = joined(
                mix_real * filter_real - mix_imaginary * filter_imaginary,
                mix_real * filter_imaginary + mix_imaginary * filter_real,
            )
        elif name == "correlate":
            made = joined(
                filter_real * weight_real + filter_imaginary * weight_imaginary,
                filter_real * weight_imaginary - filter_imaginary * weight_real,
            )
        else:
            made = joined(
                mix_real * weight_real + mix_imaginary * weight_imaginary,
                mix_real * weight_imaginary - mix_imaginary * weight_real,
            )
        outcome.append(made.reshape(lead + (-1, 2 * N2)))
    return outcome


def shards(input_gate, output_gate, values, cotangent, filter_raw, filter_decay, skip_gain):
    context_size = lax.axis_size("ctx")
    context_index = lax.axis_index("ctx")
    channels, local_len = input_gate.shape
    filters = filter_raw.shape[0]
    groups = channels // filters
    row_local = local_len // N2
    row_total = row_local * context_size
    seq_len = local_len * context_size
    first_forward, first_inverse = first_tables(row_total)
    second_forward, second_inverse = second_tables()
    inverse_scale = 1.0 / FFT_LEN
    mixed_input = (input_gate.astype(jnp.float32) * values.astype(jnp.float32)).astype(jnp.bfloat16)
    weighted = (cotangent.astype(jnp.float32) * output_gate.astype(jnp.float32)).astype(
        jnp.bfloat16
    )
    global_positions = (context_index * local_len + jnp.arange(local_len, dtype=jnp.int32)).astype(
        jnp.float32
    )
    envelope = jnp.exp(-filter_decay[:, None] * (global_positions[None, :] / seq_len))
    filter_scale = seq_len ** (-0.5)
    filter_taps = (filter_raw.astype(jnp.float32) * envelope * filter_scale).astype(jnp.bfloat16)
    spread_count = filters // context_size
    full_real, full_imaginary = twiddle_table(
        jnp.arange(N1, dtype=jnp.int32), jnp.arange(N2, dtype=jnp.int32)
    )
    pair = jnp.stack([mixed_input, weighted], axis=0).reshape(2, groups, filters, row_local, N2)
    taps_block = filter_taps.reshape(1, 1, filters, row_local, N2)
    pair_whole, taps_whole = (
        lax.all_to_all(pair, "ctx", split_axis=2, concat_axis=3, tiled=True),
        lax.all_to_all(taps_block, "ctx", split_axis=2, concat_axis=3, tiled=True),
    )
    signal_count = 2 * groups * spread_count
    every = jnp.concatenate(
        [
            pair_whole.reshape(signal_count, row_total, N2),
            taps_whole.reshape(spread_count, row_total, N2),
        ],
        axis=0,
    )
    first = jnp.einsum("km,imn->ikn", first_forward, every, preferred_element_type=jnp.float32)
    first_real = first[:, :N1]
    first_imaginary = first[:, N1:]
    turned = jnp.stack(
        [
            first_real * full_real - first_imaginary * full_imaginary,
            first_real * full_imaginary + first_imaginary * full_real,
        ],
        axis=1,
    ).astype(jnp.bfloat16)
    spectra = jnp.einsum(
        "ipkn,pnl->ikl", turned, second_forward, preferred_element_type=jnp.float32
    )
    signal_spec = spectra[:signal_count].reshape(2, groups * spread_count, N1, 2 * N2)
    filter_spec = spectra[signal_count:].astype(jnp.bfloat16)
    filter_spec = jnp.transpose(filter_spec, (1, 0, 2))
    mix_spec = jnp.transpose(signal_spec[0], (1, 0, 2))
    weight_spec = jnp.transpose(signal_spec[1], (1, 0, 2))
    made = spectral_products(mix_spec, weight_spec, filter_spec, ["convolve", "correlate", "lag"])
    stacked = jnp.transpose(jnp.concatenate(made, axis=1), (1, 0, 2))
    back = jnp.einsum("ikl,lm->ikm", stacked, second_inverse, preferred_element_type=jnp.float32)
    back_real, back_imaginary = halves(back)
    rotated = jnp.stack(
        [
            (back_real * full_real + back_imaginary * full_imaginary) * inverse_scale,
            (back_imaginary * full_real - back_real * full_imaginary) * inverse_scale,
        ],
        axis=1,
    ).astype(jnp.bfloat16)
    inverted = jnp.einsum(
        "mkp,ipkn->imn", first_inverse, rotated, preferred_element_type=jnp.float32
    )
    inverted = inverted.astype(jnp.bfloat16).reshape(3, groups, spread_count, row_total, N2)
    back_rows = lax.all_to_all(inverted[:2], "ctx", split_axis=3, concat_axis=2, tiled=True)
    convolved = back_rows[0].reshape(channels, local_len)
    correlated = back_rows[1].reshape(channels, local_len)
    lag_whole = jnp.sum(inverted[2].astype(jnp.float32), axis=0)
    lag_part = (
        lax.all_to_all(
            lag_whole.astype(jnp.bfloat16), "ctx", split_axis=1, concat_axis=0, tiled=True
        )
        .astype(lag_whole.dtype)
        .reshape(filters, local_len)
    )
    summed = convolved.astype(jnp.float32) + skip_gain[:, None] * mixed_input.astype(jnp.float32)
    outputs = (output_gate.astype(jnp.float32) * summed).astype(jnp.bfloat16)
    grad_output_gate = (cotangent.astype(jnp.float32) * summed).astype(jnp.bfloat16)
    back_total = correlated.astype(jnp.float32) + skip_gain[:, None] * weighted.astype(jnp.float32)
    grad_input_gate = (back_total * values.astype(jnp.float32)).astype(jnp.bfloat16)
    grad_values = (back_total * input_gate.astype(jnp.float32)).astype(jnp.bfloat16)
    lag_total = lax.psum(lag_part.astype(jnp.bfloat16), "dp").astype(jnp.float32)
    grad_filter = lag_total * envelope * filter_scale
    return (outputs, grad_input_gate, grad_output_gate, grad_values, grad_filter)


LANES = 128
SHARES = (6, 6, 2, 2)
STRIP = 16
EDGE_ROWS = 16
VMEM_BYTES = 60 * 2**20


def block_tables(rows):
    length = 2 * rows * LANES
    k = np.arange(rows)
    m = np.arange(rows)
    n = np.arange(LANES)
    first = np.exp(-1j * np.pi * (np.outer(2 * k + 1, m) % (4 * rows)) / (2 * rows))
    turn = np.exp(-1j * np.pi * (np.outer(2 * k + 1, n) % (2 * length)) / length)
    second = np.exp(-2j * np.pi * (np.outer(n, n) % LANES) / LANES)
    first_forward = np.concatenate([first.real, first.imag], axis=0)
    first_inverse = np.concatenate([first.real.T, first.imag.T], axis=1)
    second_forward = np.block([[second.real, second.imag], [-second.imag, second.real]])
    second_inverse = np.block([[second.real, -second.imag], [second.imag, second.real]])
    half = ml_dtypes.bfloat16
    turns = np.stack([turn.real, turn.imag]).astype(np.float32)
    return tuple(
        jnp.asarray(table)
        for table in (
            first_forward.astype(half),
            second_forward.astype(half),
            second_inverse.astype(half),
            first_inverse.astype(half),
            turns,
            (turns * np.float32(2.0 / length)),
        )
    )


def block_kernel(
    side_ref,
    own_ref,
    far_ref,
    other_own_ref,
    other_next_ref,
    other_far_ref,
    taps_ref,
    first_forward_ref,
    second_forward_ref,
    second_inverse_ref,
    first_inverse_ref,
    turn_ref,
    back_turn_ref,
    near_out_ref,
    other_out_ref,
    passed_out_ref,
    lag_out_ref,
    spectra,
    products,
):
    groups, _, rows, lanes = own_ref.shape
    side = side_ref[0]
    signals = (own_ref, far_ref, other_own_ref, other_next_ref, other_far_ref, taps_ref)
    for number, signal in enumerate(signals):
        for pair in range(signal.shape[0] // 2):
            both = jnp.concatenate([signal[2 * pair, 0], signal[2 * pair + 1, 0]], axis=1)
            first = jnp.dot(first_forward_ref[...], both, preferred_element_type=jnp.float32)
            for which in range(2):
                real = first[:rows, which * lanes : (which + 1) * lanes]
                imaginary = first[rows:, which * lanes : (which + 1) * lanes]
                turned = jnp.concatenate(
                    [
                        real * turn_ref[0] - imaginary * turn_ref[1],
                        real * turn_ref[1] + imaginary * turn_ref[0],
                    ],
                    axis=1,
                ).astype(jnp.bfloat16)
                spectra[number, 2 * pair + which] = jnp.dot(
                    turned, second_forward_ref[...], preferred_element_type=jnp.float32
                )

    row_index = lax.broadcasted_iota(jnp.int32, (STRIP, lanes), 0)
    parity = 1.0 - 2.0 * (row_index % 2).astype(jnp.float32)

    def strip(step, carry):
        at = pl.ds(pl.multiple_of(step * STRIP, STRIP), STRIP)

        def load(number, which):
            return spectra[number, which, at, :lanes], spectra[number, which, at, lanes:]

        def store(number, real, imaginary):
            products[number, at, :lanes] = real.astype(jnp.bfloat16)
            products[number, at, lanes:] = imaginary.astype(jnp.bfloat16)

        filters = [load(5, delay) for delay in range(4)]
        gains = []
        for delay in range(4):
            real, imaginary = filters[delay]
            if delay:
                before_real, before_imaginary = filters[delay - 1]
                real = real - parity * before_imaginary
                imaginary = imaginary + parity * before_real
            gains.append((real, side * imaginary))
        lag = [(jnp.zeros((STRIP, lanes), jnp.float32),) * 2 for _ in range(4)]

        def times(total, left, right):
            real = left[0] * right[0] - left[1] * right[1]
            imaginary = left[0] * right[1] + left[1] * right[0]
            return (real, imaginary) if total is None else (total[0] + real, total[1] + imaginary)

        def conjugate_times(total, left, right):
            real = left[0] * right[0] + left[1] * right[1]
            imaginary = left[0] * right[1] - left[1] * right[0]
            return (real, imaginary) if total is None else (total[0] + real, total[1] + imaginary)

        for group in range(groups):
            own, far = load(0, group), load(1, group)
            near = times(times(None, gains[0], own), gains[1], far)
            store(group, *near)
            other_own, other_next, other_far = load(2, group), load(3, group), load(4, group)
            other = conjugate_times(None, gains[0], other_own)
            other = conjugate_times(other, gains[1], other_next)
            other = conjugate_times(other, gains[2], other_far)
            store(groups + group, *other)
            passed = conjugate_times(None, gains[1], other_own)
            passed = conjugate_times(passed, gains[2], other_next)
            passed = conjugate_times(passed, gains[3], other_far)
            store(2 * groups + group, *passed)
            half_own = (0.5 * own[0], 0.5 * own[1])
            lag[0] = conjugate_times(lag[0], own, other_own)
            lag[1] = conjugate_times(lag[1], far, other_own)
            lag[1] = conjugate_times(lag[1], half_own, other_next)
            lag[2] = conjugate_times(lag[2], far, other_next)
            lag[3] = conjugate_times(lag[3], far, other_far)
        lag[3] = (0.5 * lag[3][0], 0.5 * lag[3][1])
        for delay in range(4):
            real, imaginary = lag[delay][0], side * lag[delay][1]
            if delay < 3:
                real = real + parity * (side * lag[delay + 1][1])
                imaginary = imaginary - parity * lag[delay + 1][0]
            store(3 * groups + delay, real, imaginary)
        return carry

    lax.fori_loop(0, rows // STRIP, strip, 0)

    shares = lag_out_ref.shape[0]
    for kind, out_ref in enumerate((near_out_ref, other_out_ref, passed_out_ref, None)):
        for pair in range((groups if kind < 3 else 4) // 2):
            real_parts, imaginary_parts = [], []
            for which in range(2):
                back = jnp.dot(
                    products[kind * groups + 2 * pair + which],
                    second_inverse_ref[...],
                    preferred_element_type=jnp.float32,
                )
                real, imaginary = back[:, :lanes], back[:, lanes:]
                real_parts.append(
                    (real * back_turn_ref[0] + imaginary * back_turn_ref[1]).astype(jnp.bfloat16)
                )
                imaginary_parts.append(
                    (imaginary * back_turn_ref[0] - real * back_turn_ref[1]).astype(jnp.bfloat16)
                )
            rotated = jnp.concatenate(
                [jnp.concatenate(real_parts, axis=1), jnp.concatenate(imaginary_parts, axis=1)],
                axis=0,
            )
            result = jnp.dot(first_inverse_ref[...], rotated, preferred_element_type=jnp.float32)
            result = result.astype(jnp.bfloat16)
            for which in range(2):
                column = result[:, which * lanes : (which + 1) * lanes]
                if kind < 3:
                    out_ref[2 * pair + which, 0] = column
                else:
                    column = column.reshape(shares, rows // shares, lanes)
                    lag_out_ref[:, 2 * pair + which, 0] = column


def block_products(side, signals, other, taps, tables, start, shares):
    groups, filters, rows, lanes = signals[0].shape
    block = pl.BlockSpec((groups, 1, rows, lanes), lambda f: (0, f, 0, 0))
    other_block = pl.BlockSpec((groups, 1, rows, lanes), lambda f: (0, f + start, 0, 0))
    taps_block = pl.BlockSpec((4, 1, rows, lanes), lambda f: (0, f + start, 0, 0))
    lag_block = pl.BlockSpec((shares, 4, 1, rows // shares, lanes), lambda f: (0, 0, f, 0, 0))

    def whole(table):
        return pl.BlockSpec(table.shape, lambda f: (0,) * table.ndim)

    made = jax.ShapeDtypeStruct(signals[0].shape, jnp.bfloat16)
    lag = jax.ShapeDtypeStruct((shares, 4, filters, rows // shares, lanes), jnp.bfloat16)
    own, far, other_next, other_far = signals
    return pl.pallas_call(
        block_kernel,
        grid=(filters,),
        in_specs=[pl.BlockSpec(memory_space=pltpu.SMEM)]
        + [block, block, other_block, block, block, taps_block]
        + [whole(table) for table in tables],
        out_specs=[block, block, block, lag_block],
        out_shape=[made, made, made, lag],
        scratch_shapes=[
            pltpu.VMEM((6, groups, rows, 2 * lanes), jnp.float32),
            pltpu.VMEM((3 * groups + 4, rows, 2 * lanes), jnp.bfloat16),
        ],
        compiler_params=pltpu.CompilerParams(vmem_limit_bytes=VMEM_BYTES),
        cost_estimate=pl.CostEstimate(flops=1, bytes_accessed=1, transcendentals=0),
    )(side, own, far, other, other_next, other_far, taps, *tables)


def product(left, right):
    return (left.astype(jnp.float32) * right.astype(jnp.float32)).astype(jnp.bfloat16)


def enter_kernel(side_ref, gate_ref, values_ref, cotangent_ref, out_gate_ref, *out_refs):
    channels, width = gate_ref.shape
    *own_refs, other_ref = out_refs
    groups, filters, rows, lanes = other_ref.shape
    near_start = side_ref[0] > 0
    mixed = product(gate_ref[...], values_ref[...]).astype(jnp.float32)
    weighted = product(cotangent_ref[...], out_gate_ref[...]).astype(jnp.float32)

    def blocks(array):
        array = array.reshape(channels, rows, lanes).astype(jnp.bfloat16)
        return array.reshape(groups, filters, rows, lanes)

    own = blocks(jnp.where(near_start, mixed, weighted))
    start = 0
    for own_ref in own_refs:
        own_ref[...] = own[:, start : start + own_ref.shape[1]]
        start += own_ref.shape[1]
    other_ref[...] = blocks(jnp.where(near_start, weighted, mixed))


def enter(side, flat, filters):
    channels, local_len = flat[0].shape
    groups, rows = channels // filters, local_len // LANES
    counts = SHARES + (filters,)
    return pl.pallas_call(
        enter_kernel,
        grid=(rows // EDGE_ROWS,),
        in_specs=[pl.BlockSpec(memory_space=pltpu.SMEM)]
        + [pl.BlockSpec((channels, EDGE_ROWS * LANES), lambda i: (0, i))] * 4,
        out_specs=[
            pl.BlockSpec((groups, count, EDGE_ROWS, LANES), lambda i: (0, 0, i, 0))
            for count in counts
        ],
        out_shape=[
            jax.ShapeDtypeStruct((groups, count, rows, LANES), jnp.bfloat16) for count in counts
        ],
        compiler_params=pltpu.CompilerParams(vmem_limit_bytes=VMEM_BYTES),
        cost_estimate=pl.CostEstimate(
            flops=4 * channels * local_len,
            bytes_accessed=12 * channels * local_len,
            transcendentals=0,
        ),
    )(side, *flat)


def leave_kernel(side_ref, skip_ref, gate_ref, values_ref, cotangent_ref, out_gate_ref, *refs):
    channels, width = gate_ref.shape
    parts = len(SHARES)
    near_refs, other_refs = refs[:parts], refs[parts : 2 * parts]
    received_refs = refs[2 * parts : 3 * parts]
    outputs_ref, grad_gate_ref, grad_out_gate_ref, grad_values_ref = refs[3 * parts :]
    near_start = side_ref[0] > 0

    def whole(part_refs):
        return jnp.concatenate([ref[...] for ref in part_refs], axis=1).astype(jnp.float32)

    def flat(array):
        return array.reshape(channels, width // LANES, LANES).reshape(channels, width)

    near = flat(whole(near_refs))
    other = flat(whole(other_refs) + whole(received_refs))
    skip = skip_ref[...]
    gate, values = gate_ref[...].astype(jnp.float32), values_ref[...].astype(jnp.float32)
    cotangent = cotangent_ref[...].astype(jnp.float32)
    out_gate = out_gate_ref[...].astype(jnp.float32)
    mixed = (gate * values).astype(jnp.bfloat16).astype(jnp.float32)
    weighted = (cotangent * out_gate).astype(jnp.bfloat16).astype(jnp.float32)
    summed = jnp.where(near_start, near, other) + skip * mixed
    outputs_ref[...] = (out_gate * summed).astype(jnp.bfloat16)
    grad_out_gate_ref[...] = (cotangent * summed).astype(jnp.bfloat16)
    back_total = jnp.where(near_start, other, near) + skip * weighted
    grad_gate_ref[...] = (back_total * values).astype(jnp.bfloat16)
    grad_values_ref[...] = (back_total * gate).astype(jnp.bfloat16)


def leave(side, skip_gain, flat, near_parts, other_parts, received_parts):
    channels, local_len = flat[0].shape
    parts = (*near_parts, *other_parts, *received_parts)
    flat_block = pl.BlockSpec((channels, EDGE_ROWS * LANES), lambda i: (0, i))
    return pl.pallas_call(
        leave_kernel,
        grid=(local_len // (EDGE_ROWS * LANES),),
        in_specs=[
            pl.BlockSpec(memory_space=pltpu.SMEM),
            pl.BlockSpec((channels, 1), lambda i: (0, 0)),
        ]
        + [flat_block] * 4
        + [
            pl.BlockSpec((*part.shape[:2], EDGE_ROWS, LANES), lambda i: (0, 0, i, 0))
            for part in parts
        ],
        out_specs=[flat_block] * 4,
        out_shape=[jax.ShapeDtypeStruct((channels, local_len), jnp.bfloat16)] * 4,
        compiler_params=pltpu.CompilerParams(vmem_limit_bytes=VMEM_BYTES),
        cost_estimate=pl.CostEstimate(
            flops=12 * channels * local_len,
            bytes_accessed=22 * channels * local_len,
            transcendentals=0,
        ),
    )(side, skip_gain[:, None], *flat, *parts)


def after(array, *earlier):
    return lax.optimization_barrier((array, *earlier))[0]


def block_shards(input_gate, output_gate, values, cotangent, filter_raw, filter_decay, skip_gain):
    context_index = lax.axis_index("ctx")
    channels, local_len = input_gate.shape
    filters = filter_raw.shape[0]
    rows = local_len // LANES
    seq_len = local_len * lax.axis_size("ctx")
    data_size = lax.axis_size("dp")
    tables = block_tables(rows)
    side = jnp.where(context_index < 2, 1.0, -1.0).astype(jnp.float32).reshape(1)
    flat = (input_gate, values, cotangent, output_gate)
    *own_parts, other = enter(side, flat, filters)

    positions = (context_index * local_len + jnp.arange(local_len, dtype=jnp.int32)).astype(
        jnp.float32
    )
    filter_scale = seq_len ** (-0.5)

    def envelope(decay):
        return jnp.exp(-decay[:, None] * (positions[None, :] / seq_len))

    share = filters // data_size
    first_filter = lax.axis_index("dp") * share
    raw_share = lax.dynamic_slice_in_dim(filter_raw, first_filter, share, 0)
    decay_share = lax.dynamic_slice_in_dim(filter_decay, first_filter, share, 0)
    taps = (raw_share.astype(jnp.float32) * envelope(decay_share) * filter_scale).astype(
        jnp.bfloat16
    )
    taps = after(taps.reshape(1, share, rows, LANES), own_parts[0])
    taps = jnp.broadcast_to(taps, (4, share, rows, LANES))
    taps = lax.all_to_all(taps, "ctx", split_axis=0, concat_axis=0, tiled=True)
    taps = lax.all_gather(taps, "dp", axis=1, tiled=True)

    def lag_shares(pieces):
        pieces = lax.all_to_all(pieces, "dp", split_axis=0, concat_axis=0, tiled=True)
        return jnp.sum(pieces.astype(jnp.float32), axis=0).astype(jnp.bfloat16)

    def lag_sum(pieces):
        pieces = lax.all_to_all(pieces, "ctx", split_axis=0, concat_axis=0, tiled=True)
        total = jnp.sum(pieces.astype(jnp.float32), axis=0).astype(jnp.bfloat16)
        spread = jnp.broadcast_to(total[None], (data_size, *total.shape))
        spread = lax.all_to_all(spread, "dp", split_axis=0, concat_axis=0, tiled=True)
        return jnp.transpose(spread, (1, 0, 2, 3)).reshape(total.shape[0], rows, LANES)

    routes = ([(1, 2), (2, 1)], [(0, 2), (3, 1)], [(0, 1), (3, 2)])
    arrivals, near_parts, other_parts, received_parts, lag_parts = [], [], [], [], []

    def send(number):
        own, made = own_parts[number], []
        for stream, route in enumerate(routes):
            earlier = [arrivals[number - 1][stream]] if number else []
            earlier += near_parts[number - 2 : number - 1] if number >= 2 else []
            made.append(lax.ppermute(after(own, *earlier), "ctx", route))
        arrivals.append(made)

    start = 0
    send(0)
    for number, own in enumerate(own_parts):
        if number + 1 < len(own_parts):
            send(number + 1)
        other_next, other_far, far = arrivals[number]
        if number >= 1:
            own = after(own, near_parts[number - 1])
        if number >= 2:
            own = after(own, received_parts[number - 2], lag_parts[number - 2])
        near_out, other_out, passed, lag = block_products(
            side, (own, far, other_next, other_far), other, taps, tables, start, data_size
        )
        start += own.shape[1]
        near_parts.append(near_out)
        other_parts.append(other_out)
        if number == len(own_parts) - 1:
            passed = after(passed, received_parts[number - 1])
        received_parts.append(lax.ppermute(passed, "ctx", [(1, 0), (2, 3)]))
        lag_parts.append(lag_shares(lag) if number < 2 else lag)
    late = lag_shares(jnp.concatenate(lag_parts[2:], axis=2))
    late = after(late, received_parts[-1])
    lag = lag_sum(jnp.concatenate([*lag_parts[:2], late], axis=1)).reshape(filters, local_len)
    grad_filter = lag.astype(jnp.float32) * envelope(filter_decay) * filter_scale
    outputs, grad_input_gate, grad_output_gate, grad_values = leave(
        side, skip_gain, flat, near_parts, other_parts, received_parts
    )
    return (outputs, grad_input_gate, grad_output_gate, grad_values, grad_filter)


def chosen_shards(dp, ctx):
    def run(input_gate, *others):
        channels, local_len = input_gate.shape
        filters = others[3].shape[0]
        by_blocks = (
            ctx == 4
            and local_len % (LANES * STRIP * dp) == 0
            and local_len % (LANES * EDGE_ROWS) == 0
            and channels % (2 * filters) == 0
            and filters % dp == 0
            and filters == sum(SHARES)
        )
        return (block_shards if by_blocks else shards)(input_gate, *others)

    return run


def solution(mesh):
    return jax.shard_map(
        chosen_shards(mesh.shape["dp"], mesh.shape["ctx"]),
        mesh=mesh,
        in_specs=(
            P("dp", "ctx"),
            P("dp", "ctx"),
            P("dp", "ctx"),
            P("dp", "ctx"),
            P(None, "ctx"),
            P(),
            P("dp"),
        ),
        out_specs=(P("dp", "ctx"), P("dp", "ctx"), P("dp", "ctx"), P("dp", "ctx"), P(None, "ctx")),
        check_vma=False,
    )
```

```python
import math

import jax
import jax.numpy as jnp
import ml_dtypes
import numpy as np
from jax import lax
from jax.experimental import pallas as pl
from jax.experimental.pallas import tpu as pltpu
from jax.sharding import PartitionSpec as P

N1 = 512
N2 = 512
FFT_LEN = 262144


two_pi = 2.0 * math.pi


def first_tables(row_total):
    first_index = jnp.arange(N1, dtype=jnp.int32)
    source_rows = jnp.arange(row_total, dtype=jnp.int32)
    angles = (first_index[:, None] * source_rows[None, :] % N1).astype(jnp.float32) * (two_pi / N1)
    cosine = jnp.cos(angles).astype(jnp.bfloat16)
    minus_sine = (-jnp.sin(angles)).astype(jnp.bfloat16)
    forward_table = jnp.concatenate([cosine, minus_sine], axis=0)
    inverse_table = jnp.stack([cosine.T, minus_sine.T], axis=2)
    return (forward_table, inverse_table)


def second_tables():
    second_index = jnp.arange(N2, dtype=jnp.int32)
    angles = (second_index[:, None] * second_index[None, :] % N2).astype(jnp.float32) * (
        two_pi / N2
    )
    cosine = jnp.cos(angles).astype(jnp.bfloat16)
    minus_sine = (-jnp.sin(angles)).astype(jnp.bfloat16)
    forward_table = jnp.stack(
        [
            jnp.concatenate([cosine, minus_sine], axis=1),
            jnp.concatenate([-minus_sine, cosine], axis=1),
        ],
        axis=0,
    )
    inverse_table = jnp.concatenate(
        [
            jnp.concatenate([cosine, -minus_sine], axis=1),
            jnp.concatenate([minus_sine, cosine], axis=1),
        ],
        axis=0,
    )
    return (forward_table, inverse_table)


def twiddle_table(spectrum_rows, columns):
    angles = (spectrum_rows[:, None] * columns[None, :] % FFT_LEN).astype(jnp.float32) * (
        two_pi / FFT_LEN
    )
    return (jnp.cos(angles), -jnp.sin(angles))


def halves(array):
    return (array[..., :N2], array[..., N2:])


def joined(real_part, imaginary_part):
    return jnp.concatenate([real_part, imaginary_part], axis=-1).astype(jnp.bfloat16)


def spectral_products(mix_spec, weight_spec, filter_spec, which):
    lead = mix_spec.shape[:-2]
    filters = filter_spec.shape[-2]
    filter_real, filter_imaginary = halves(filter_spec.astype(jnp.float32))
    filter_real = jnp.expand_dims(filter_real, -3)
    filter_imaginary = jnp.expand_dims(filter_imaginary, -3)
    outcome = []
    mix_real, mix_imaginary = halves(mix_spec.reshape(lead + (-1, filters, 2 * N2)))
    weight_real, weight_imaginary = halves(weight_spec.reshape(lead + (-1, filters, 2 * N2)))
    for name in which:
        if name == "convolve":
            made = joined(
                mix_real * filter_real - mix_imaginary * filter_imaginary,
                mix_real * filter_imaginary + mix_imaginary * filter_real,
            )
        elif name == "correlate":
            made = joined(
                filter_real * weight_real + filter_imaginary * weight_imaginary,
                filter_real * weight_imaginary - filter_imaginary * weight_real,
            )
        else:
            made = joined(
                mix_real * weight_real + mix_imaginary * weight_imaginary,
                mix_real * weight_imaginary - mix_imaginary * weight_real,
            )
        outcome.append(made.reshape(lead + (-1, 2 * N2)))
    return outcome


def shards(input_gate, output_gate, values, cotangent, filter_raw, filter_decay, skip_gain):
    context_size = lax.axis_size("ctx")
    context_index = lax.axis_index("ctx")
    channels, local_len = input_gate.shape
    filters = filter_raw.shape[0]
    groups = channels // filters
    row_local = local_len // N2
    row_total = row_local * context_size
    seq_len = local_len * context_size
    first_forward, first_inverse = first_tables(row_total)
    second_forward, second_inverse = second_tables()
    inverse_scale = 1.0 / FFT_LEN
    mixed_input = (input_gate.astype(jnp.float32) * values.astype(jnp.float32)).astype(jnp.bfloat16)
    weighted = (cotangent.astype(jnp.float32) * output_gate.astype(jnp.float32)).astype(
        jnp.bfloat16
    )
    global_positions = (context_index * local_len + jnp.arange(local_len, dtype=jnp.int32)).astype(
        jnp.float32
    )
    envelope = jnp.exp(-filter_decay[:, None] * (global_positions[None, :] / seq_len))
    filter_scale = seq_len ** (-0.5)
    filter_taps = (filter_raw.astype(jnp.float32) * envelope * filter_scale).astype(jnp.bfloat16)
    spread_count = filters // context_size
    full_real, full_imaginary = twiddle_table(
        jnp.arange(N1, dtype=jnp.int32), jnp.arange(N2, dtype=jnp.int32)
    )
    pair = jnp.stack([mixed_input, weighted], axis=0).reshape(2, groups, filters, row_local, N2)
    taps_block = filter_taps.reshape(1, 1, filters, row_local, N2)
    pair_whole, taps_whole = (
        lax.all_to_all(pair, "ctx", split_axis=2, concat_axis=3, tiled=True),
        lax.all_to_all(taps_block, "ctx", split_axis=2, concat_axis=3, tiled=True),
    )
    signal_count = 2 * groups * spread_count
    every = jnp.concatenate(
        [
            pair_whole.reshape(signal_count, row_total, N2),
            taps_whole.reshape(spread_count, row_total, N2),
        ],
        axis=0,
    )
    first = jnp.einsum("km,imn->ikn", first_forward, every, preferred_element_type=jnp.float32)
    first_real = first[:, :N1]
    first_imaginary = first[:, N1:]
    turned = jnp.stack(
        [
            first_real * full_real - first_imaginary * full_imaginary,
            first_real * full_imaginary + first_imaginary * full_real,
        ],
        axis=1,
    ).astype(jnp.bfloat16)
    spectra = jnp.einsum(
        "ipkn,pnl->ikl", turned, second_forward, preferred_element_type=jnp.float32
    )
    signal_spec = spectra[:signal_count].reshape(2, groups * spread_count, N1, 2 * N2)
    filter_spec = spectra[signal_count:].astype(jnp.bfloat16)
    filter_spec = jnp.transpose(filter_spec, (1, 0, 2))
    mix_spec = jnp.transpose(signal_spec[0], (1, 0, 2))
    weight_spec = jnp.transpose(signal_spec[1], (1, 0, 2))
    made = spectral_products(mix_spec, weight_spec, filter_spec, ["convolve", "correlate", "lag"])
    stacked = jnp.transpose(jnp.concatenate(made, axis=1), (1, 0, 2))
    back = jnp.einsum("ikl,lm->ikm", stacked, second_inverse, preferred_element_type=jnp.float32)
    back_real, back_imaginary = halves(back)
    rotated = jnp.stack(
        [
            (back_real * full_real + back_imaginary * full_imaginary) * inverse_scale,
            (back_imaginary * full_real - back_real * full_imaginary) * inverse_scale,
        ],
        axis=1,
    ).astype(jnp.bfloat16)
    inverted = jnp.einsum(
        "mkp,ipkn->imn", first_inverse, rotated, preferred_element_type=jnp.float32
    )
    inverted = inverted.astype(jnp.bfloat16).reshape(3, groups, spread_count, row_total, N2)
    back_rows = lax.all_to_all(inverted[:2], "ctx", split_axis=3, concat_axis=2, tiled=True)
    convolved = back_rows[0].reshape(channels, local_len)
    correlated = back_rows[1].reshape(channels, local_len)
    lag_whole = jnp.sum(inverted[2].astype(jnp.float32), axis=0)
    lag_part = (
        lax.all_to_all(
            lag_whole.astype(jnp.bfloat16), "ctx", split_axis=1, concat_axis=0, tiled=True
        )
        .astype(lag_whole.dtype)
        .reshape(filters, local_len)
    )
    summed = convolved.astype(jnp.float32) + skip_gain[:, None] * mixed_input.astype(jnp.float32)
    outputs = (output_gate.astype(jnp.float32) * summed).astype(jnp.bfloat16)
    grad_output_gate = (cotangent.astype(jnp.float32) * summed).astype(jnp.bfloat16)
    back_total = correlated.astype(jnp.float32) + skip_gain[:, None] * weighted.astype(jnp.float32)
    grad_input_gate = (back_total * values.astype(jnp.float32)).astype(jnp.bfloat16)
    grad_values = (back_total * input_gate.astype(jnp.float32)).astype(jnp.bfloat16)
    lag_total = lax.psum(lag_part.astype(jnp.bfloat16), "dp").astype(jnp.float32)
    grad_filter = lag_total * envelope * filter_scale
    return (outputs, grad_input_gate, grad_output_gate, grad_values, grad_filter)


LANES = 128
SHARES = (5, 5, 3, 3)
STRIP = 16
EDGE_ROWS = 16
VMEM_BYTES = 60 * 2**20


def block_tables(rows):
    length = 2 * rows * LANES
    k = np.arange(rows)
    m = np.arange(rows)
    n = np.arange(LANES)
    first = np.exp(-1j * np.pi * (np.outer(2 * k + 1, m) % (4 * rows)) / (2 * rows))
    turn = np.exp(-1j * np.pi * (np.outer(2 * k + 1, n) % (2 * length)) / length)
    second = np.exp(-2j * np.pi * (np.outer(n, n) % LANES) / LANES)
    first_forward = np.concatenate([first.real, first.imag], axis=0)
    first_inverse = np.concatenate([first.real.T, first.imag.T], axis=1)
    second_forward = np.block([[second.real, second.imag], [-second.imag, second.real]])
    second_inverse = np.block([[second.real, -second.imag], [second.imag, second.real]])
    half = ml_dtypes.bfloat16
    turns = np.stack([turn.real, turn.imag]).astype(np.float32)
    return tuple(
        jnp.asarray(table)
        for table in (
            first_forward.astype(half),
            second_forward.astype(half),
            second_inverse.astype(half),
            first_inverse.astype(half),
            turns,
            (turns * np.float32(2.0 / length)),
        )
    )


def block_kernel(
    side_ref,
    own_ref,
    far_ref,
    other_own_ref,
    other_next_ref,
    other_far_ref,
    taps_ref,
    first_forward_ref,
    second_forward_ref,
    second_inverse_ref,
    first_inverse_ref,
    turn_ref,
    back_turn_ref,
    near_out_ref,
    other_out_ref,
    passed_out_ref,
    lag_out_ref,
    spectra,
    products,
):
    groups, _, rows, lanes = own_ref.shape
    side = side_ref[0]
    signals = (own_ref, far_ref, other_own_ref, other_next_ref, other_far_ref, taps_ref)
    for number, signal in enumerate(signals):
        for pair in range(signal.shape[0] // 2):
            both = jnp.concatenate([signal[2 * pair, 0], signal[2 * pair + 1, 0]], axis=1)
            first = jnp.dot(first_forward_ref[...], both, preferred_element_type=jnp.float32)
            for which in range(2):
                real = first[:rows, which * lanes : (which + 1) * lanes]
                imaginary = first[rows:, which * lanes : (which + 1) * lanes]
                turned = jnp.concatenate(
                    [
                        real * turn_ref[0] - imaginary * turn_ref[1],
                        real * turn_ref[1] + imaginary * turn_ref[0],
                    ],
                    axis=1,
                ).astype(jnp.bfloat16)
                spectra[number, 2 * pair + which] = jnp.dot(
                    turned, second_forward_ref[...], preferred_element_type=jnp.float32
                )

    row_index = lax.broadcasted_iota(jnp.int32, (STRIP, lanes), 0)
    parity = 1.0 - 2.0 * (row_index % 2).astype(jnp.float32)

    def strip(step, carry):
        at = pl.ds(pl.multiple_of(step * STRIP, STRIP), STRIP)

        def load(number, which):
            return spectra[number, which, at, :lanes], spectra[number, which, at, lanes:]

        def store(number, real, imaginary):
            products[number, at, :lanes] = real.astype(jnp.bfloat16)
            products[number, at, lanes:] = imaginary.astype(jnp.bfloat16)

        filters = [load(5, delay) for delay in range(4)]
        gains = []
        for delay in range(4):
            real, imaginary = filters[delay]
            if delay:
                before_real, before_imaginary = filters[delay - 1]
                real = real - parity * before_imaginary
                imaginary = imaginary + parity * before_real
            gains.append((real, side * imaginary))
        lag = [(jnp.zeros((STRIP, lanes), jnp.float32),) * 2 for _ in range(4)]

        def times(total, left, right):
            real = left[0] * right[0] - left[1] * right[1]
            imaginary = left[0] * right[1] + left[1] * right[0]
            return (real, imaginary) if total is None else (total[0] + real, total[1] + imaginary)

        def conjugate_times(total, left, right):
            real = left[0] * right[0] + left[1] * right[1]
            imaginary = left[0] * right[1] - left[1] * right[0]
            return (real, imaginary) if total is None else (total[0] + real, total[1] + imaginary)

        for group in range(groups):
            own, far = load(0, group), load(1, group)
            near = times(times(None, gains[0], own), gains[1], far)
            store(group, *near)
            other_own, other_next, other_far = load(2, group), load(3, group), load(4, group)
            other = conjugate_times(None, gains[0], other_own)
            other = conjugate_times(other, gains[1], other_next)
            other = conjugate_times(other, gains[2], other_far)
            store(groups + group, *other)
            passed = conjugate_times(None, gains[1], other_own)
            passed = conjugate_times(passed, gains[2], other_next)
            passed = conjugate_times(passed, gains[3], other_far)
            store(2 * groups + group, *passed)
            half_own = (0.5 * own[0], 0.5 * own[1])
            lag[0] = conjugate_times(lag[0], own, other_own)
            lag[1] = conjugate_times(lag[1], far, other_own)
            lag[1] = conjugate_times(lag[1], half_own, other_next)
            lag[2] = conjugate_times(lag[2], far, other_next)
            lag[3] = conjugate_times(lag[3], far, other_far)
        lag[3] = (0.5 * lag[3][0], 0.5 * lag[3][1])
        for delay in range(4):
            real, imaginary = lag[delay][0], side * lag[delay][1]
            if delay < 3:
                real = real + parity * (side * lag[delay + 1][1])
                imaginary = imaginary - parity * lag[delay + 1][0]
            store(3 * groups + delay, real, imaginary)
        return carry

    lax.fori_loop(0, rows // STRIP, strip, 0)

    shares = lag_out_ref.shape[0]
    for kind, out_ref in enumerate((near_out_ref, other_out_ref, passed_out_ref, None)):
        for pair in range((groups if kind < 3 else 4) // 2):
            real_parts, imaginary_parts = [], []
            for which in range(2):
                back = jnp.dot(
                    products[kind * groups + 2 * pair + which],
                    second_inverse_ref[...],
                    preferred_element_type=jnp.float32,
                )
                real, imaginary = back[:, :lanes], back[:, lanes:]
                real_parts.append(
                    (real * back_turn_ref[0] + imaginary * back_turn_ref[1]).astype(jnp.bfloat16)
                )
                imaginary_parts.append(
                    (imaginary * back_turn_ref[0] - real * back_turn_ref[1]).astype(jnp.bfloat16)
                )
            rotated = jnp.concatenate(
                [jnp.concatenate(real_parts, axis=1), jnp.concatenate(imaginary_parts, axis=1)],
                axis=0,
            )
            result = jnp.dot(first_inverse_ref[...], rotated, preferred_element_type=jnp.float32)
            result = result.astype(jnp.bfloat16)
            for which in range(2):
                column = result[:, which * lanes : (which + 1) * lanes]
                if kind < 3:
                    out_ref[2 * pair + which, 0] = column
                else:
                    column = column.reshape(shares, rows // shares, lanes)
                    lag_out_ref[:, 2 * pair + which, 0] = column


def block_products(side, signals, other, taps, tables, start, shares):
    groups, filters, rows, lanes = signals[0].shape
    block = pl.BlockSpec((groups, 1, rows, lanes), lambda f: (0, f, 0, 0))
    other_block = pl.BlockSpec((groups, 1, rows, lanes), lambda f: (0, f + start, 0, 0))
    taps_block = pl.BlockSpec((4, 1, rows, lanes), lambda f: (0, f + start, 0, 0))
    lag_block = pl.BlockSpec((shares, 4, 1, rows // shares, lanes), lambda f: (0, 0, f, 0, 0))

    def whole(table):
        return pl.BlockSpec(table.shape, lambda f: (0,) * table.ndim)

    made = jax.ShapeDtypeStruct(signals[0].shape, jnp.bfloat16)
    lag = jax.ShapeDtypeStruct((shares, 4, filters, rows // shares, lanes), jnp.bfloat16)
    own, far, other_next, other_far = signals
    return pl.pallas_call(
        block_kernel,
        grid=(filters,),
        in_specs=[pl.BlockSpec(memory_space=pltpu.SMEM)]
        + [block, block, other_block, block, block, taps_block]
        + [whole(table) for table in tables],
        out_specs=[block, block, block, lag_block],
        out_shape=[made, made, made, lag],
        scratch_shapes=[
            pltpu.VMEM((6, groups, rows, 2 * lanes), jnp.float32),
            pltpu.VMEM((3 * groups + 4, rows, 2 * lanes), jnp.bfloat16),
        ],
        compiler_params=pltpu.CompilerParams(vmem_limit_bytes=VMEM_BYTES),
        cost_estimate=pl.CostEstimate(flops=1, bytes_accessed=1, transcendentals=0),
    )(side, own, far, other, other_next, other_far, taps, *tables)


def product(left, right):
    return (left.astype(jnp.float32) * right.astype(jnp.float32)).astype(jnp.bfloat16)


def enter_kernel(side_ref, gate_ref, values_ref, cotangent_ref, out_gate_ref, *out_refs):
    channels, width = gate_ref.shape
    *own_refs, other_ref = out_refs
    groups, filters, rows, lanes = other_ref.shape
    near_start = side_ref[0] > 0
    mixed = product(gate_ref[...], values_ref[...]).astype(jnp.float32)
    weighted = product(cotangent_ref[...], out_gate_ref[...]).astype(jnp.float32)

    def blocks(array):
        array = array.reshape(channels, rows, lanes).astype(jnp.bfloat16)
        return array.reshape(groups, filters, rows, lanes)

    own = blocks(jnp.where(near_start, mixed, weighted))
    start = 0
    for own_ref in own_refs:
        own_ref[...] = own[:, start : start + own_ref.shape[1]]
        start += own_ref.shape[1]
    other_ref[...] = blocks(jnp.where(near_start, weighted, mixed))


def enter(side, flat, filters):
    channels, local_len = flat[0].shape
    groups, rows = channels // filters, local_len // LANES
    counts = SHARES + (filters,)
    return pl.pallas_call(
        enter_kernel,
        grid=(rows // EDGE_ROWS,),
        in_specs=[pl.BlockSpec(memory_space=pltpu.SMEM)]
        + [pl.BlockSpec((channels, EDGE_ROWS * LANES), lambda i: (0, i))] * 4,
        out_specs=[
            pl.BlockSpec((groups, count, EDGE_ROWS, LANES), lambda i: (0, 0, i, 0))
            for count in counts
        ],
        out_shape=[
            jax.ShapeDtypeStruct((groups, count, rows, LANES), jnp.bfloat16) for count in counts
        ],
        compiler_params=pltpu.CompilerParams(vmem_limit_bytes=VMEM_BYTES),
        cost_estimate=pl.CostEstimate(
            flops=4 * channels * local_len,
            bytes_accessed=12 * channels * local_len,
            transcendentals=0,
        ),
    )(side, *flat)


def leave_kernel(side_ref, skip_ref, gate_ref, values_ref, cotangent_ref, out_gate_ref, *refs):
    channels, width = gate_ref.shape
    parts = len(SHARES)
    near_refs, other_refs = refs[:parts], refs[parts : 2 * parts]
    received_refs = refs[2 * parts : 3 * parts]
    outputs_ref, grad_gate_ref, grad_out_gate_ref, grad_values_ref = refs[3 * parts :]
    near_start = side_ref[0] > 0

    def whole(part_refs):
        return jnp.concatenate([ref[...] for ref in part_refs], axis=1).astype(jnp.float32)

    def flat(array):
        return array.reshape(channels, width // LANES, LANES).reshape(channels, width)

    near = flat(whole(near_refs))
    other = flat(whole(other_refs) + whole(received_refs))
    skip = skip_ref[...]
    gate, values = gate_ref[...].astype(jnp.float32), values_ref[...].astype(jnp.float32)
    cotangent = cotangent_ref[...].astype(jnp.float32)
    out_gate = out_gate_ref[...].astype(jnp.float32)
    mixed = (gate * values).astype(jnp.bfloat16).astype(jnp.float32)
    weighted = (cotangent * out_gate).astype(jnp.bfloat16).astype(jnp.float32)
    summed = jnp.where(near_start, near, other) + skip * mixed
    outputs_ref[...] = (out_gate * summed).astype(jnp.bfloat16)
    grad_out_gate_ref[...] = (cotangent * summed).astype(jnp.bfloat16)
    back_total = jnp.where(near_start, other, near) + skip * weighted
    grad_gate_ref[...] = (back_total * values).astype(jnp.bfloat16)
    grad_values_ref[...] = (back_total * gate).astype(jnp.bfloat16)


def leave(side, skip_gain, flat, near_parts, other_parts, received_parts):
    channels, local_len = flat[0].shape
    parts = (*near_parts, *other_parts, *received_parts)
    flat_block = pl.BlockSpec((channels, EDGE_ROWS * LANES), lambda i: (0, i))
    return pl.pallas_call(
        leave_kernel,
        grid=(local_len // (EDGE_ROWS * LANES),),
        in_specs=[
            pl.BlockSpec(memory_space=pltpu.SMEM),
            pl.BlockSpec((channels, 1), lambda i: (0, 0)),
        ]
        + [flat_block] * 4
        + [
            pl.BlockSpec((*part.shape[:2], EDGE_ROWS, LANES), lambda i: (0, 0, i, 0))
            for part in parts
        ],
        out_specs=[flat_block] * 4,
        out_shape=[jax.ShapeDtypeStruct((channels, local_len), jnp.bfloat16)] * 4,
        compiler_params=pltpu.CompilerParams(vmem_limit_bytes=VMEM_BYTES),
        cost_estimate=pl.CostEstimate(
            flops=12 * channels * local_len,
            bytes_accessed=22 * channels * local_len,
            transcendentals=0,
        ),
    )(side, skip_gain[:, None], *flat, *parts)


def rotation(hop):
    return [(index, (index + hop) % 4) for index in range(4)]


def block_shards(input_gate, output_gate, values, cotangent, filter_raw, filter_decay, skip_gain):
    context_index = lax.axis_index("ctx")
    channels, local_len = input_gate.shape
    filters = filter_raw.shape[0]
    rows = local_len // LANES
    seq_len = local_len * lax.axis_size("ctx")
    data_size = lax.axis_size("dp")
    tables = block_tables(rows)
    side = jnp.where(context_index < 2, 1.0, -1.0).astype(jnp.float32).reshape(1)
    flat = (input_gate, values, cotangent, output_gate)
    *own_parts, other = enter(side, flat, filters)

    positions = (context_index * local_len + jnp.arange(local_len, dtype=jnp.int32)).astype(
        jnp.float32
    )
    filter_scale = seq_len ** (-0.5)

    def envelope(decay):
        return jnp.exp(-decay[:, None] * (positions[None, :] / seq_len))

    share = filters // data_size
    first_filter = lax.axis_index("dp") * share
    raw_share = lax.dynamic_slice_in_dim(filter_raw, first_filter, share, 0)
    decay_share = lax.dynamic_slice_in_dim(filter_decay, first_filter, share, 0)
    taps = (raw_share.astype(jnp.float32) * envelope(decay_share) * filter_scale).astype(
        jnp.bfloat16
    )
    taps = taps.reshape(1, share, rows, LANES)
    turned = [taps] + [lax.ppermute(taps, "ctx", rotation(hop)) for hop in (1, 2, 3)]
    turned = jnp.concatenate(turned[::-1] + turned[:0:-1], axis=0)
    taps = lax.dynamic_slice_in_dim(turned, 3 - context_index, 4, 0)
    taps = lax.all_gather(taps, "dp", axis=1, tiled=True)

    def lag_shares(pieces):
        pieces = lax.all_to_all(pieces, "dp", split_axis=0, concat_axis=0, tiled=True)
        return jnp.sum(pieces.astype(jnp.float32), axis=0).astype(jnp.bfloat16)

    def lag_sum(pieces):
        def block(index):
            return lax.dynamic_index_in_dim(pieces, index, 0, keepdims=False)

        total = block(context_index).astype(jnp.float32)
        for hop in (1, 2, 3):
            leaving = block((context_index + hop) % 4)
            total += lax.ppermute(leaving, "ctx", rotation(hop)).astype(jnp.float32)
        total = total.astype(jnp.bfloat16)
        spread = jnp.broadcast_to(total[None], (data_size, *total.shape))
        spread = lax.all_to_all(spread, "dp", split_axis=0, concat_axis=0, tiled=True)
        return jnp.transpose(spread, (1, 0, 2, 3)).reshape(total.shape[0], rows, LANES)

    routes = ([(1, 2), (2, 1)], [(0, 2), (3, 1)], [(0, 1), (3, 2)])
    back_route = [(1, 0), (2, 3)]
    near_parts, other_parts, received_parts, lag_parts = [], [], [], []
    arrivals = [lax.ppermute(own_parts[0], "ctx", route) for route in routes]
    start, pending = 0, None
    for number, own in enumerate(own_parts):
        leaving = own_parts[number + 1] if number + 1 < len(own_parts) else None
        arrivals, own, leaving, pending, received_parts, lag_parts, near_parts = (
            lax.optimization_barrier(
                (arrivals, own, leaving, pending, received_parts, lag_parts, near_parts)
            )
        )
        other_next, other_far, far = arrivals
        if leaving is not None:
            arrivals = [lax.ppermute(leaving, "ctx", route) for route in routes]
        if pending is not None:
            received_parts.append(lax.ppermute(pending[0], "ctx", back_route))
            lag_parts.append(lag_shares(pending[1]))
        near_out, other_out, *pending = block_products(
            side, (own, far, other_next, other_far), other, taps, tables, start, data_size
        )
        start += own.shape[1]
        near_parts.append(near_out)
        other_parts.append(other_out)
    pending, received_parts, lag_parts = lax.optimization_barrier(
        (pending, received_parts, lag_parts)
    )
    received = lax.ppermute(pending[0], "ctx", back_route)
    received, late = lax.optimization_barrier((received, lag_shares(pending[1])))
    received_parts.append(received)
    lag = lag_sum(jnp.concatenate([*lag_parts, late], axis=1)).reshape(filters, local_len)
    grad_filter = lag.astype(jnp.float32) * envelope(filter_decay) * filter_scale
    outputs, grad_input_gate, grad_output_gate, grad_values = leave(
        side, skip_gain, flat, near_parts, other_parts, received_parts
    )
    return (outputs, grad_input_gate, grad_output_gate, grad_values, grad_filter)


def chosen_shards(dp, ctx):
    def run(input_gate, *others):
        channels, local_len = input_gate.shape
        filters = others[3].shape[0]
        by_blocks = (
            ctx == 4
            and local_len % (LANES * STRIP * dp) == 0
            and local_len % (LANES * EDGE_ROWS) == 0
            and channels % (2 * filters) == 0
            and filters % dp == 0
            and filters == sum(SHARES)
        )
        return (block_shards if by_blocks else shards)(input_gate, *others)

    return run


def solution(mesh):
    return jax.shard_map(
        chosen_shards(mesh.shape["dp"], mesh.shape["ctx"]),
        mesh=mesh,
        in_specs=(
            P("dp", "ctx"),
            P("dp", "ctx"),
            P("dp", "ctx"),
            P("dp", "ctx"),
            P(None, "ctx"),
            P(),
            P("dp"),
        ),
        out_specs=(P("dp", "ctx"), P("dp", "ctx"), P("dp", "ctx"), P("dp", "ctx"), P(None, "ctx")),
        check_vma=False,
    )
```

```python
import math

import jax
import jax.numpy as jnp
import ml_dtypes
import numpy as np
from jax import lax
from jax.experimental import pallas as pl
from jax.experimental.pallas import tpu as pltpu
from jax.sharding import PartitionSpec as P

N1 = 512
N2 = 512
FFT_LEN = 262144


two_pi = 2.0 * math.pi


def first_tables(row_total):
    first_index = jnp.arange(N1, dtype=jnp.int32)
    source_rows = jnp.arange(row_total, dtype=jnp.int32)
    angles = (first_index[:, None] * source_rows[None, :] % N1).astype(jnp.float32) * (two_pi / N1)
    cosine = jnp.cos(angles).astype(jnp.bfloat16)
    minus_sine = (-jnp.sin(angles)).astype(jnp.bfloat16)
    forward_table = jnp.concatenate([cosine, minus_sine], axis=0)
    inverse_table = jnp.stack([cosine.T, minus_sine.T], axis=2)
    return (forward_table, inverse_table)


def second_tables():
    second_index = jnp.arange(N2, dtype=jnp.int32)
    angles = (second_index[:, None] * second_index[None, :] % N2).astype(jnp.float32) * (
        two_pi / N2
    )
    cosine = jnp.cos(angles).astype(jnp.bfloat16)
    minus_sine = (-jnp.sin(angles)).astype(jnp.bfloat16)
    forward_table = jnp.stack(
        [
            jnp.concatenate([cosine, minus_sine], axis=1),
            jnp.concatenate([-minus_sine, cosine], axis=1),
        ],
        axis=0,
    )
    inverse_table = jnp.concatenate(
        [
            jnp.concatenate([cosine, -minus_sine], axis=1),
            jnp.concatenate([minus_sine, cosine], axis=1),
        ],
        axis=0,
    )
    return (forward_table, inverse_table)


def twiddle_table(spectrum_rows, columns):
    angles = (spectrum_rows[:, None] * columns[None, :] % FFT_LEN).astype(jnp.float32) * (
        two_pi / FFT_LEN
    )
    return (jnp.cos(angles), -jnp.sin(angles))


def halves(array):
    return (array[..., :N2], array[..., N2:])


def joined(real_part, imaginary_part):
    return jnp.concatenate([real_part, imaginary_part], axis=-1).astype(jnp.bfloat16)


def spectral_products(mix_spec, weight_spec, filter_spec, which):
    lead = mix_spec.shape[:-2]
    filters = filter_spec.shape[-2]
    filter_real, filter_imaginary = halves(filter_spec.astype(jnp.float32))
    filter_real = jnp.expand_dims(filter_real, -3)
    filter_imaginary = jnp.expand_dims(filter_imaginary, -3)
    outcome = []
    mix_real, mix_imaginary = halves(mix_spec.reshape(lead + (-1, filters, 2 * N2)))
    weight_real, weight_imaginary = halves(weight_spec.reshape(lead + (-1, filters, 2 * N2)))
    for name in which:
        if name == "convolve":
            made = joined(
                mix_real * filter_real - mix_imaginary * filter_imaginary,
                mix_real * filter_imaginary + mix_imaginary * filter_real,
            )
        elif name == "correlate":
            made = joined(
                filter_real * weight_real + filter_imaginary * weight_imaginary,
                filter_real * weight_imaginary - filter_imaginary * weight_real,
            )
        else:
            made = joined(
                mix_real * weight_real + mix_imaginary * weight_imaginary,
                mix_real * weight_imaginary - mix_imaginary * weight_real,
            )
        outcome.append(made.reshape(lead + (-1, 2 * N2)))
    return outcome


def shards(input_gate, output_gate, values, cotangent, filter_raw, filter_decay, skip_gain):
    context_size = lax.axis_size("ctx")
    context_index = lax.axis_index("ctx")
    channels, local_len = input_gate.shape
    filters = filter_raw.shape[0]
    groups = channels // filters
    row_local = local_len // N2
    row_total = row_local * context_size
    seq_len = local_len * context_size
    first_forward, first_inverse = first_tables(row_total)
    second_forward, second_inverse = second_tables()
    inverse_scale = 1.0 / FFT_LEN
    mixed_input = (input_gate.astype(jnp.float32) * values.astype(jnp.float32)).astype(jnp.bfloat16)
    weighted = (cotangent.astype(jnp.float32) * output_gate.astype(jnp.float32)).astype(
        jnp.bfloat16
    )
    global_positions = (context_index * local_len + jnp.arange(local_len, dtype=jnp.int32)).astype(
        jnp.float32
    )
    envelope = jnp.exp(-filter_decay[:, None] * (global_positions[None, :] / seq_len))
    filter_scale = seq_len ** (-0.5)
    filter_taps = (filter_raw.astype(jnp.float32) * envelope * filter_scale).astype(jnp.bfloat16)
    spread_count = filters // context_size
    full_real, full_imaginary = twiddle_table(
        jnp.arange(N1, dtype=jnp.int32), jnp.arange(N2, dtype=jnp.int32)
    )
    pair = jnp.stack([mixed_input, weighted], axis=0).reshape(2, groups, filters, row_local, N2)
    taps_block = filter_taps.reshape(1, 1, filters, row_local, N2)
    pair_whole, taps_whole = (
        lax.all_to_all(pair, "ctx", split_axis=2, concat_axis=3, tiled=True),
        lax.all_to_all(taps_block, "ctx", split_axis=2, concat_axis=3, tiled=True),
    )
    signal_count = 2 * groups * spread_count
    every = jnp.concatenate(
        [
            pair_whole.reshape(signal_count, row_total, N2),
            taps_whole.reshape(spread_count, row_total, N2),
        ],
        axis=0,
    )
    first = jnp.einsum("km,imn->ikn", first_forward, every, preferred_element_type=jnp.float32)
    first_real = first[:, :N1]
    first_imaginary = first[:, N1:]
    turned = jnp.stack(
        [
            first_real * full_real - first_imaginary * full_imaginary,
            first_real * full_imaginary + first_imaginary * full_real,
        ],
        axis=1,
    ).astype(jnp.bfloat16)
    spectra = jnp.einsum(
        "ipkn,pnl->ikl", turned, second_forward, preferred_element_type=jnp.float32
    )
    signal_spec = spectra[:signal_count].reshape(2, groups * spread_count, N1, 2 * N2)
    filter_spec = spectra[signal_count:].astype(jnp.bfloat16)
    filter_spec = jnp.transpose(filter_spec, (1, 0, 2))
    mix_spec = jnp.transpose(signal_spec[0], (1, 0, 2))
    weight_spec = jnp.transpose(signal_spec[1], (1, 0, 2))
    made = spectral_products(mix_spec, weight_spec, filter_spec, ["convolve", "correlate", "lag"])
    stacked = jnp.transpose(jnp.concatenate(made, axis=1), (1, 0, 2))
    back = jnp.einsum("ikl,lm->ikm", stacked, second_inverse, preferred_element_type=jnp.float32)
    back_real, back_imaginary = halves(back)
    rotated = jnp.stack(
        [
            (back_real * full_real + back_imaginary * full_imaginary) * inverse_scale,
            (back_imaginary * full_real - back_real * full_imaginary) * inverse_scale,
        ],
        axis=1,
    ).astype(jnp.bfloat16)
    inverted = jnp.einsum(
        "mkp,ipkn->imn", first_inverse, rotated, preferred_element_type=jnp.float32
    )
    inverted = inverted.astype(jnp.bfloat16).reshape(3, groups, spread_count, row_total, N2)
    back_rows = lax.all_to_all(inverted[:2], "ctx", split_axis=3, concat_axis=2, tiled=True)
    convolved = back_rows[0].reshape(channels, local_len)
    correlated = back_rows[1].reshape(channels, local_len)
    lag_whole = jnp.sum(inverted[2].astype(jnp.float32), axis=0)
    lag_part = (
        lax.all_to_all(
            lag_whole.astype(jnp.bfloat16), "ctx", split_axis=1, concat_axis=0, tiled=True
        )
        .astype(lag_whole.dtype)
        .reshape(filters, local_len)
    )
    summed = convolved.astype(jnp.float32) + skip_gain[:, None] * mixed_input.astype(jnp.float32)
    outputs = (output_gate.astype(jnp.float32) * summed).astype(jnp.bfloat16)
    grad_output_gate = (cotangent.astype(jnp.float32) * summed).astype(jnp.bfloat16)
    back_total = correlated.astype(jnp.float32) + skip_gain[:, None] * weighted.astype(jnp.float32)
    grad_input_gate = (back_total * values.astype(jnp.float32)).astype(jnp.bfloat16)
    grad_values = (back_total * input_gate.astype(jnp.float32)).astype(jnp.bfloat16)
    lag_total = lax.psum(lag_part.astype(jnp.bfloat16), "dp").astype(jnp.float32)
    grad_filter = lag_total * envelope * filter_scale
    return (outputs, grad_input_gate, grad_output_gate, grad_values, grad_filter)


LANES = 128
SHARES = (7, 6, 3)
STRIP = 16
EDGE_ROWS = 16
VMEM_BYTES = 60 * 2**20


def block_tables(rows):
    length = 2 * rows * LANES
    k = np.arange(rows)
    m = np.arange(rows)
    n = np.arange(LANES)
    first = np.exp(-1j * np.pi * (np.outer(2 * k + 1, m) % (4 * rows)) / (2 * rows))
    turn = np.exp(-1j * np.pi * (np.outer(2 * k + 1, n) % (2 * length)) / length)
    second = np.exp(-2j * np.pi * (np.outer(n, n) % LANES) / LANES)
    first_forward = np.concatenate([first.real, first.imag], axis=0)
    first_inverse = np.concatenate([first.real.T, first.imag.T], axis=1)
    second_forward = np.block([[second.real, second.imag], [-second.imag, second.real]])
    second_inverse = np.block([[second.real, -second.imag], [second.imag, second.real]])
    half = ml_dtypes.bfloat16
    turns = np.stack([turn.real, turn.imag]).astype(np.float32)
    return tuple(
        jnp.asarray(table)
        for table in (
            first_forward.astype(half),
            second_forward.astype(half),
            second_inverse.astype(half),
            first_inverse.astype(half),
            turns,
            (turns * np.float32(2.0 / length)),
        )
    )


def block_kernel(
    side_ref,
    own_ref,
    far_ref,
    other_own_ref,
    other_next_ref,
    other_far_ref,
    taps_ref,
    first_forward_ref,
    second_forward_ref,
    second_inverse_ref,
    first_inverse_ref,
    turn_ref,
    back_turn_ref,
    near_out_ref,
    other_out_ref,
    passed_out_ref,
    lag_out_ref,
    spectra,
    products,
):
    groups, _, rows, lanes = own_ref.shape
    side = side_ref[0]
    signals = (own_ref, far_ref, other_own_ref, other_next_ref, other_far_ref, taps_ref)
    for number, signal in enumerate(signals):
        for pair in range(signal.shape[0] // 2):
            both = jnp.concatenate([signal[2 * pair, 0], signal[2 * pair + 1, 0]], axis=1)
            first = jnp.dot(first_forward_ref[...], both, preferred_element_type=jnp.float32)
            for which in range(2):
                real = first[:rows, which * lanes : (which + 1) * lanes]
                imaginary = first[rows:, which * lanes : (which + 1) * lanes]
                turned = jnp.concatenate(
                    [
                        real * turn_ref[0] - imaginary * turn_ref[1],
                        real * turn_ref[1] + imaginary * turn_ref[0],
                    ],
                    axis=1,
                ).astype(jnp.bfloat16)
                spectra[number, 2 * pair + which] = jnp.dot(
                    turned, second_forward_ref[...], preferred_element_type=jnp.float32
                )

    row_index = lax.broadcasted_iota(jnp.int32, (STRIP, lanes), 0)
    parity = 1.0 - 2.0 * (row_index % 2).astype(jnp.float32)

    def strip(step, carry):
        at = pl.ds(pl.multiple_of(step * STRIP, STRIP), STRIP)

        def load(number, which):
            return spectra[number, which, at, :lanes], spectra[number, which, at, lanes:]

        def store(number, real, imaginary):
            products[number, at, :lanes] = real.astype(jnp.bfloat16)
            products[number, at, lanes:] = imaginary.astype(jnp.bfloat16)

        filters = [load(5, delay) for delay in range(4)]
        gains = []
        for delay in range(4):
            real, imaginary = filters[delay]
            if delay:
                before_real, before_imaginary = filters[delay - 1]
                real = real - parity * before_imaginary
                imaginary = imaginary + parity * before_real
            gains.append((real, side * imaginary))
        lag = [(jnp.zeros((STRIP, lanes), jnp.float32),) * 2 for _ in range(4)]

        def times(total, left, right):
            real = left[0] * right[0] - left[1] * right[1]
            imaginary = left[0] * right[1] + left[1] * right[0]
            return (real, imaginary) if total is None else (total[0] + real, total[1] + imaginary)

        def conjugate_times(total, left, right):
            real = left[0] * right[0] + left[1] * right[1]
            imaginary = left[0] * right[1] - left[1] * right[0]
            return (real, imaginary) if total is None else (total[0] + real, total[1] + imaginary)

        for group in range(groups):
            own, far = load(0, group), load(1, group)
            near = times(times(None, gains[0], own), gains[1], far)
            store(group, *near)
            other_own, other_next, other_far = load(2, group), load(3, group), load(4, group)
            other = conjugate_times(None, gains[0], other_own)
            other = conjugate_times(other, gains[1], other_next)
            other = conjugate_times(other, gains[2], other_far)
            store(groups + group, *other)
            passed = conjugate_times(None, gains[1], other_own)
            passed = conjugate_times(passed, gains[2], other_next)
            passed = conjugate_times(passed, gains[3], other_far)
            store(2 * groups + group, *passed)
            half_own = (0.5 * own[0], 0.5 * own[1])
            lag[0] = conjugate_times(lag[0], own, other_own)
            lag[1] = conjugate_times(lag[1], far, other_own)
            lag[1] = conjugate_times(lag[1], half_own, other_next)
            lag[2] = conjugate_times(lag[2], far, other_next)
            lag[3] = conjugate_times(lag[3], far, other_far)
        lag[3] = (0.5 * lag[3][0], 0.5 * lag[3][1])
        for delay in range(4):
            real, imaginary = lag[delay][0], side * lag[delay][1]
            if delay < 3:
                real = real + parity * (side * lag[delay + 1][1])
                imaginary = imaginary - parity * lag[delay + 1][0]
            store(3 * groups + delay, real, imaginary)
        return carry

    lax.fori_loop(0, rows // STRIP, strip, 0)

    shares = lag_out_ref.shape[0]
    for kind, out_ref in enumerate((near_out_ref, other_out_ref, passed_out_ref, None)):
        for pair in range((groups if kind < 3 else 4) // 2):
            real_parts, imaginary_parts = [], []
            for which in range(2):
                back = jnp.dot(
                    products[kind * groups + 2 * pair + which],
                    second_inverse_ref[...],
                    preferred_element_type=jnp.float32,
                )
                real, imaginary = back[:, :lanes], back[:, lanes:]
                real_parts.append(
                    (real * back_turn_ref[0] + imaginary * back_turn_ref[1]).astype(jnp.bfloat16)
                )
                imaginary_parts.append(
                    (imaginary * back_turn_ref[0] - real * back_turn_ref[1]).astype(jnp.bfloat16)
                )
            rotated = jnp.concatenate(
                [jnp.concatenate(real_parts, axis=1), jnp.concatenate(imaginary_parts, axis=1)],
                axis=0,
            )
            result = jnp.dot(first_inverse_ref[...], rotated, preferred_element_type=jnp.float32)
            result = result.astype(jnp.bfloat16)
            for which in range(2):
                column = result[:, which * lanes : (which + 1) * lanes]
                if kind < 3:
                    out_ref[2 * pair + which, 0] = column
                else:
                    column = column.reshape(shares, rows // shares, lanes)
                    lag_out_ref[:, 2 * pair + which, 0] = column


def block_products(side, signals, other, taps, tables, start, shares):
    groups, filters, rows, lanes = signals[0].shape
    block = pl.BlockSpec((groups, 1, rows, lanes), lambda f: (0, f, 0, 0))
    other_block = pl.BlockSpec((groups, 1, rows, lanes), lambda f: (0, f + start, 0, 0))
    taps_block = pl.BlockSpec((4, 1, rows, lanes), lambda f: (0, f + start, 0, 0))
    lag_block = pl.BlockSpec((shares, 4, 1, rows // shares, lanes), lambda f: (0, 0, f, 0, 0))

    def whole(table):
        return pl.BlockSpec(table.shape, lambda f: (0,) * table.ndim)

    made = jax.ShapeDtypeStruct(signals[0].shape, jnp.bfloat16)
    lag = jax.ShapeDtypeStruct((shares, 4, filters, rows // shares, lanes), jnp.bfloat16)
    own, far, other_next, other_far = signals
    return pl.pallas_call(
        block_kernel,
        grid=(filters,),
        in_specs=[pl.BlockSpec(memory_space=pltpu.SMEM)]
        + [block, block, other_block, block, block, taps_block]
        + [whole(table) for table in tables],
        out_specs=[block, block, block, lag_block],
        out_shape=[made, made, made, lag],
        scratch_shapes=[
            pltpu.VMEM((6, groups, rows, 2 * lanes), jnp.float32),
            pltpu.VMEM((3 * groups + 4, rows, 2 * lanes), jnp.bfloat16),
        ],
        compiler_params=pltpu.CompilerParams(vmem_limit_bytes=VMEM_BYTES),
        cost_estimate=pl.CostEstimate(flops=1, bytes_accessed=1, transcendentals=0),
    )(side, own, far, other, other_next, other_far, taps, *tables)


def product(left, right):
    return (left.astype(jnp.float32) * right.astype(jnp.float32)).astype(jnp.bfloat16)


def enter_kernel(first_ref, gate_ref, values_ref, cotangent_ref, out_gate_ref, *refs):
    channels, width = gate_ref.shape
    *out_refs, turned = refs
    rows = width // LANES

    def fill(left_ref, right_ref):
        made = product(left_ref[...], right_ref[...]).astype(jnp.float32)
        for row in range(rows):
            column = made[:, row * LANES : (row + 1) * LANES]
            turned[pl.ds(row, channels, stride=rows), :] = column

    @pl.when(first_ref[0] == 1)
    def _():
        fill(gate_ref, values_ref)

    @pl.when(first_ref[0] == 0)
    def _():
        fill(cotangent_ref, out_gate_ref)

    groups = out_refs[0].shape[0]
    made = turned[...].astype(jnp.bfloat16).reshape(groups, channels // groups, rows, LANES)
    start = 0
    for out_ref in out_refs:
        out_ref[...] = made[:, start : start + out_ref.shape[1]]
        start += out_ref.shape[1]


def enter(first, flat, filters, counts):
    channels, local_len = flat[0].shape
    groups, rows = channels // filters, local_len // LANES
    block = (channels, EDGE_ROWS * LANES)
    of_first = pl.BlockSpec(block, lambda i, first: (0, i * first[0]))
    of_second = pl.BlockSpec(block, lambda i, first: (0, i * (1 - first[0])))
    return pl.pallas_call(
        enter_kernel,
        grid_spec=pltpu.PrefetchScalarGridSpec(
            num_scalar_prefetch=1,
            grid=(rows // EDGE_ROWS,),
            in_specs=[of_first, of_first, of_second, of_second],
            out_specs=[
                pl.BlockSpec((groups, count, EDGE_ROWS, LANES), lambda i, first: (0, 0, i, 0))
                for count in counts
            ],
            scratch_shapes=[pltpu.VMEM((channels * EDGE_ROWS, LANES), jnp.float32)],
        ),
        out_shape=[
            jax.ShapeDtypeStruct((groups, count, rows, LANES), jnp.bfloat16) for count in counts
        ],
        compiler_params=pltpu.CompilerParams(vmem_limit_bytes=VMEM_BYTES),
        cost_estimate=pl.CostEstimate(
            flops=2 * channels * local_len,
            bytes_accessed=6 * channels * local_len,
            transcendentals=0,
        ),
    )(first, *flat)


def leave_kernel(has_received, has_made, *refs):
    first_ref, skip_ref, gate_ref, values_ref, cotangent_ref, out_gate_ref, *refs = refs
    channels, width = gate_ref.shape
    parts, rows = len(SHARES), width // LANES
    signal_refs, refs = refs[:parts], refs[parts:]
    signal = jnp.concatenate([ref[...] for ref in signal_refs], axis=1).astype(jnp.float32)
    if has_received:
        received = jnp.concatenate([ref[...] for ref in refs[:parts]], axis=1)
        signal, refs = signal + received.astype(jnp.float32), refs[parts:]
    if has_made:
        made_refs, refs = refs[:4], refs[4:]
    *out_refs, turned = refs
    turned[...] = signal.reshape(channels * rows, LANES)
    signal = jnp.concatenate(
        [turned[pl.ds(row, channels, stride=rows), :] for row in range(rows)], axis=1
    )
    skip = skip_ref[...]

    def finish(left_ref, right_ref, factor_refs, result_refs, kept):
        term = product(left_ref[...], right_ref[...]).astype(jnp.float32)
        total = signal + skip * term
        for factor_ref, result_ref in zip(factor_refs, result_refs):
            result_ref[...] = (factor_ref[...].astype(jnp.float32) * total).astype(jnp.bfloat16)
        if has_made:

            @pl.when(pl.program_id(0) == 0)
            def _():
                for number in kept:
                    out_refs[number][...] = made_refs[number][...]

    @pl.when(first_ref[0] == 1)
    def _():
        finish(gate_ref, values_ref, (out_gate_ref, cotangent_ref), out_refs[:2], (2, 3))

    @pl.when(first_ref[0] == 0)
    def _():
        finish(cotangent_ref, out_gate_ref, (values_ref, gate_ref), out_refs[2:], (0, 1))


def leave(first, skip_gain, flat, signal_parts, received_parts=(), made=()):
    channels, local_len = flat[0].shape
    parts = (*signal_parts, *received_parts)
    block = (channels, EDGE_ROWS * LANES)
    flat_block = pl.BlockSpec(block, lambda i, first: (0, i))
    still_block = pl.BlockSpec(block, lambda i, first: (0, 0))
    of_first = pl.BlockSpec(block, lambda i, first: (0, i * first[0]))
    of_second = pl.BlockSpec(block, lambda i, first: (0, i * (1 - first[0])))
    before = 6 + len(parts)
    return pl.pallas_call(
        lambda *refs: leave_kernel(bool(received_parts), bool(made), *refs),
        grid_spec=pltpu.PrefetchScalarGridSpec(
            num_scalar_prefetch=1,
            grid=(local_len // (EDGE_ROWS * LANES),),
            in_specs=[pl.BlockSpec((channels, 1), lambda i, first: (0, 0))]
            + [flat_block] * 4
            + [
                pl.BlockSpec((*part.shape[:2], EDGE_ROWS, LANES), lambda i, first: (0, 0, i, 0))
                for part in parts
            ]
            + [still_block] * len(made),
            out_specs=[of_first, of_first, of_second, of_second],
            scratch_shapes=[pltpu.VMEM((channels * EDGE_ROWS, LANES), jnp.float32)],
        ),
        out_shape=[jax.ShapeDtypeStruct((channels, local_len), jnp.bfloat16)] * 4,
        input_output_aliases={before + number: number for number in range(len(made))},
        compiler_params=pltpu.CompilerParams(vmem_limit_bytes=VMEM_BYTES),
        cost_estimate=pl.CostEstimate(
            flops=8 * channels * local_len,
            bytes_accessed=14 * channels * local_len,
            transcendentals=0,
        ),
    )(first, skip_gain[:, None], *flat, *parts, *made)


def rotation(hop):
    return [(index, (index + hop) % 4) for index in range(4)]


def block_shards(input_gate, output_gate, values, cotangent, filter_raw, filter_decay, skip_gain):
    context_index = lax.axis_index("ctx")
    channels, local_len = input_gate.shape
    filters = filter_raw.shape[0]
    rows = local_len // LANES
    seq_len = local_len * lax.axis_size("ctx")
    data_size = lax.axis_size("dp")
    tables = block_tables(rows)
    side = jnp.where(context_index < 2, 1.0, -1.0).astype(jnp.float32).reshape(1)
    near_start = (context_index < 2).astype(jnp.int32).reshape(1)
    flat = (input_gate, values, cotangent, output_gate)
    own_parts = enter(near_start, flat, filters, SHARES)
    routes = ([(1, 2), (2, 1)], [(0, 2), (3, 1)], [(0, 1), (3, 2)])
    back_route = [(1, 0), (2, 3)]

    positions = (context_index * local_len + jnp.arange(local_len, dtype=jnp.int32)).astype(
        jnp.float32
    )
    filter_scale = seq_len ** (-0.5)

    def envelope(decay):
        return jnp.exp(-decay[:, None] * (positions[None, :] / seq_len))

    share = filters // data_size
    first_filter = lax.axis_index("dp") * share
    raw_share = lax.dynamic_slice_in_dim(filter_raw, first_filter, share, 0)
    decay_share = lax.dynamic_slice_in_dim(filter_decay, first_filter, share, 0)
    taps = (raw_share.astype(jnp.float32) * envelope(decay_share) * filter_scale).astype(
        jnp.bfloat16
    )
    taps = taps.reshape(1, share, rows, LANES)
    turned = [taps] + [lax.ppermute(taps, "ctx", rotation(hop)) for hop in (1, 2, 3)]
    turned = jnp.concatenate(turned[::-1] + turned[:0:-1], axis=0)
    taps = lax.dynamic_slice_in_dim(turned, 3 - context_index, 4, 0)
    own_parts, taps, rest = lax.optimization_barrier((own_parts, taps, 1 - near_start))
    arrivals = [lax.ppermute(own_parts[0], "ctx", route) for route in routes]
    taps = lax.all_gather(taps, "dp", axis=1, tiled=True)
    (other,) = enter(rest, flat, filters, (filters,))

    def lag_shares(pieces):
        pieces = lax.all_to_all(pieces, "dp", split_axis=0, concat_axis=0, tiled=True)
        return jnp.sum(pieces.astype(jnp.float32), axis=0).astype(jnp.bfloat16)

    def lag_sum(pieces):
        def block(index):
            return lax.dynamic_index_in_dim(pieces, index, 0, keepdims=False)

        total = block(context_index).astype(jnp.float32)
        for hop in (1, 2, 3):
            leaving = block((context_index + hop) % 4)
            total += lax.ppermute(leaving, "ctx", rotation(hop)).astype(jnp.float32)
        total = total.astype(jnp.bfloat16)
        spread = jnp.broadcast_to(total[None], (data_size, *total.shape))
        spread = lax.all_to_all(spread, "dp", split_axis=0, concat_axis=0, tiled=True)
        return jnp.transpose(spread, (1, 0, 2, 3)).reshape(total.shape[0], rows, LANES)

    near_parts, other_parts, received_parts, lag_parts = [], [], [], []
    start, pending = 0, None
    for number, own in enumerate(own_parts):
        leaving = own_parts[number + 1] if number + 1 < len(own_parts) else None
        arrivals, own, leaving, pending, received_parts, lag_parts, near_parts, other = (
            lax.optimization_barrier(
                (arrivals, own, leaving, pending, received_parts, lag_parts, near_parts, other)
            )
        )
        other_next, other_far, far = arrivals
        if leaving is not None:
            arrivals = [lax.ppermute(leaving, "ctx", route) for route in routes]
        if pending is not None:
            received_parts.append(lax.ppermute(pending[0], "ctx", back_route))
            lag_parts.append(lag_shares(pending[1]))
        near_out, other_out, *pending = block_products(
            side, (own, far, other_next, other_far), other, taps, tables, start, data_size
        )
        start += own.shape[1]
        near_parts.append(near_out)
        other_parts.append(other_out)
    pending, received_parts, lag_parts, near_parts = lax.optimization_barrier(
        (pending, received_parts, lag_parts, near_parts)
    )
    received = lax.ppermute(pending[0], "ctx", back_route)
    made = leave(near_start, skip_gain, flat, near_parts)
    received, late, made = lax.optimization_barrier((received, lag_shares(pending[1]), made))
    received_parts.append(received)
    lag = lag_sum(jnp.concatenate([*lag_parts, late], axis=1)).reshape(filters, local_len)
    grad_filter = lag.astype(jnp.float32) * envelope(filter_decay) * filter_scale
    outputs, grad_output_gate, grad_input_gate, grad_values = leave(
        1 - near_start, skip_gain, flat, other_parts, received_parts, made
    )
    return (outputs, grad_input_gate, grad_output_gate, grad_values, grad_filter)


def chosen_shards(dp, ctx):
    def run(input_gate, *others):
        channels, local_len = input_gate.shape
        filters = others[3].shape[0]
        by_blocks = (
            ctx == 4
            and local_len % (LANES * STRIP * dp) == 0
            and local_len % (LANES * EDGE_ROWS) == 0
            and channels % (2 * filters) == 0
            and filters % dp == 0
            and filters == sum(SHARES)
        )
        return (block_shards if by_blocks else shards)(input_gate, *others)

    return run


def solution(mesh):
    return jax.shard_map(
        chosen_shards(mesh.shape["dp"], mesh.shape["ctx"]),
        mesh=mesh,
        in_specs=(
            P("dp", "ctx"),
            P("dp", "ctx"),
            P("dp", "ctx"),
            P("dp", "ctx"),
            P(None, "ctx"),
            P(),
            P("dp"),
        ),
        out_specs=(P("dp", "ctx"), P("dp", "ctx"), P("dp", "ctx"), P("dp", "ctx"), P(None, "ctx")),
        check_vma=False,
    )
```

```python
import math

import jax
import jax.numpy as jnp
import ml_dtypes
import numpy as np
from jax import lax
from jax.experimental import pallas as pl
from jax.experimental.pallas import tpu as pltpu
from jax.sharding import PartitionSpec as P

N1 = 512
N2 = 512
FFT_LEN = 262144


two_pi = 2.0 * math.pi


def first_tables(row_total):
    first_index = jnp.arange(N1, dtype=jnp.int32)
    source_rows = jnp.arange(row_total, dtype=jnp.int32)
    angles = (first_index[:, None] * source_rows[None, :] % N1).astype(jnp.float32) * (two_pi / N1)
    cosine = jnp.cos(angles).astype(jnp.bfloat16)
    minus_sine = (-jnp.sin(angles)).astype(jnp.bfloat16)
    forward_table = jnp.concatenate([cosine, minus_sine], axis=0)
    inverse_table = jnp.stack([cosine.T, minus_sine.T], axis=2)
    return (forward_table, inverse_table)


def second_tables():
    second_index = jnp.arange(N2, dtype=jnp.int32)
    angles = (second_index[:, None] * second_index[None, :] % N2).astype(jnp.float32) * (
        two_pi / N2
    )
    cosine = jnp.cos(angles).astype(jnp.bfloat16)
    minus_sine = (-jnp.sin(angles)).astype(jnp.bfloat16)
    forward_table = jnp.stack(
        [
            jnp.concatenate([cosine, minus_sine], axis=1),
            jnp.concatenate([-minus_sine, cosine], axis=1),
        ],
        axis=0,
    )
    inverse_table = jnp.concatenate(
        [
            jnp.concatenate([cosine, -minus_sine], axis=1),
            jnp.concatenate([minus_sine, cosine], axis=1),
        ],
        axis=0,
    )
    return (forward_table, inverse_table)


def twiddle_table(spectrum_rows, columns):
    angles = (spectrum_rows[:, None] * columns[None, :] % FFT_LEN).astype(jnp.float32) * (
        two_pi / FFT_LEN
    )
    return (jnp.cos(angles), -jnp.sin(angles))


def halves(array):
    return (array[..., :N2], array[..., N2:])


def joined(real_part, imaginary_part):
    return jnp.concatenate([real_part, imaginary_part], axis=-1).astype(jnp.bfloat16)


def spectral_products(mix_spec, weight_spec, filter_spec, which):
    lead = mix_spec.shape[:-2]
    filters = filter_spec.shape[-2]
    filter_real, filter_imaginary = halves(filter_spec.astype(jnp.float32))
    filter_real = jnp.expand_dims(filter_real, -3)
    filter_imaginary = jnp.expand_dims(filter_imaginary, -3)
    outcome = []
    mix_real, mix_imaginary = halves(mix_spec.reshape(lead + (-1, filters, 2 * N2)))
    weight_real, weight_imaginary = halves(weight_spec.reshape(lead + (-1, filters, 2 * N2)))
    for name in which:
        if name == "convolve":
            made = joined(
                mix_real * filter_real - mix_imaginary * filter_imaginary,
                mix_real * filter_imaginary + mix_imaginary * filter_real,
            )
        elif name == "correlate":
            made = joined(
                filter_real * weight_real + filter_imaginary * weight_imaginary,
                filter_real * weight_imaginary - filter_imaginary * weight_real,
            )
        else:
            made = joined(
                mix_real * weight_real + mix_imaginary * weight_imaginary,
                mix_real * weight_imaginary - mix_imaginary * weight_real,
            )
        outcome.append(made.reshape(lead + (-1, 2 * N2)))
    return outcome


def shards(input_gate, output_gate, values, cotangent, filter_raw, filter_decay, skip_gain):
    context_size = lax.axis_size("ctx")
    context_index = lax.axis_index("ctx")
    channels, local_len = input_gate.shape
    filters = filter_raw.shape[0]
    groups = channels // filters
    row_local = local_len // N2
    row_total = row_local * context_size
    seq_len = local_len * context_size
    first_forward, first_inverse = first_tables(row_total)
    second_forward, second_inverse = second_tables()
    inverse_scale = 1.0 / FFT_LEN
    mixed_input = (input_gate.astype(jnp.float32) * values.astype(jnp.float32)).astype(jnp.bfloat16)
    weighted = (cotangent.astype(jnp.float32) * output_gate.astype(jnp.float32)).astype(
        jnp.bfloat16
    )
    global_positions = (context_index * local_len + jnp.arange(local_len, dtype=jnp.int32)).astype(
        jnp.float32
    )
    envelope = jnp.exp(-filter_decay[:, None] * (global_positions[None, :] / seq_len))
    filter_scale = seq_len ** (-0.5)
    filter_taps = (filter_raw.astype(jnp.float32) * envelope * filter_scale).astype(jnp.bfloat16)
    spread_count = filters // context_size
    full_real, full_imaginary = twiddle_table(
        jnp.arange(N1, dtype=jnp.int32), jnp.arange(N2, dtype=jnp.int32)
    )
    pair = jnp.stack([mixed_input, weighted], axis=0).reshape(2, groups, filters, row_local, N2)
    taps_block = filter_taps.reshape(1, 1, filters, row_local, N2)
    pair_whole, taps_whole = (
        lax.all_to_all(pair, "ctx", split_axis=2, concat_axis=3, tiled=True),
        lax.all_to_all(taps_block, "ctx", split_axis=2, concat_axis=3, tiled=True),
    )
    signal_count = 2 * groups * spread_count
    every = jnp.concatenate(
        [
            pair_whole.reshape(signal_count, row_total, N2),
            taps_whole.reshape(spread_count, row_total, N2),
        ],
        axis=0,
    )
    first = jnp.einsum("km,imn->ikn", first_forward, every, preferred_element_type=jnp.float32)
    first_real = first[:, :N1]
    first_imaginary = first[:, N1:]
    turned = jnp.stack(
        [
            first_real * full_real - first_imaginary * full_imaginary,
            first_real * full_imaginary + first_imaginary * full_real,
        ],
        axis=1,
    ).astype(jnp.bfloat16)
    spectra = jnp.einsum(
        "ipkn,pnl->ikl", turned, second_forward, preferred_element_type=jnp.float32
    )
    signal_spec = spectra[:signal_count].reshape(2, groups * spread_count, N1, 2 * N2)
    filter_spec = spectra[signal_count:].astype(jnp.bfloat16)
    filter_spec = jnp.transpose(filter_spec, (1, 0, 2))
    mix_spec = jnp.transpose(signal_spec[0], (1, 0, 2))
    weight_spec = jnp.transpose(signal_spec[1], (1, 0, 2))
    made = spectral_products(mix_spec, weight_spec, filter_spec, ["convolve", "correlate", "lag"])
    stacked = jnp.transpose(jnp.concatenate(made, axis=1), (1, 0, 2))
    back = jnp.einsum("ikl,lm->ikm", stacked, second_inverse, preferred_element_type=jnp.float32)
    back_real, back_imaginary = halves(back)
    rotated = jnp.stack(
        [
            (back_real * full_real + back_imaginary * full_imaginary) * inverse_scale,
            (back_imaginary * full_real - back_real * full_imaginary) * inverse_scale,
        ],
        axis=1,
    ).astype(jnp.bfloat16)
    inverted = jnp.einsum(
        "mkp,ipkn->imn", first_inverse, rotated, preferred_element_type=jnp.float32
    )
    inverted = inverted.astype(jnp.bfloat16).reshape(3, groups, spread_count, row_total, N2)
    back_rows = lax.all_to_all(inverted[:2], "ctx", split_axis=3, concat_axis=2, tiled=True)
    convolved = back_rows[0].reshape(channels, local_len)
    correlated = back_rows[1].reshape(channels, local_len)
    lag_whole = jnp.sum(inverted[2].astype(jnp.float32), axis=0)
    lag_part = (
        lax.all_to_all(
            lag_whole.astype(jnp.bfloat16), "ctx", split_axis=1, concat_axis=0, tiled=True
        )
        .astype(lag_whole.dtype)
        .reshape(filters, local_len)
    )
    summed = convolved.astype(jnp.float32) + skip_gain[:, None] * mixed_input.astype(jnp.float32)
    outputs = (output_gate.astype(jnp.float32) * summed).astype(jnp.bfloat16)
    grad_output_gate = (cotangent.astype(jnp.float32) * summed).astype(jnp.bfloat16)
    back_total = correlated.astype(jnp.float32) + skip_gain[:, None] * weighted.astype(jnp.float32)
    grad_input_gate = (back_total * values.astype(jnp.float32)).astype(jnp.bfloat16)
    grad_values = (back_total * input_gate.astype(jnp.float32)).astype(jnp.bfloat16)
    lag_total = lax.psum(lag_part.astype(jnp.bfloat16), "dp").astype(jnp.float32)
    grad_filter = lag_total * envelope * filter_scale
    return (outputs, grad_input_gate, grad_output_gate, grad_values, grad_filter)


LANES = 128
SHARES = (6, 5, 3, 2)
STRIP = 16
EDGE_ROWS = 16
VMEM_BYTES = 60 * 2**20


def block_tables(rows):
    length = 2 * rows * LANES
    k = np.arange(rows)
    m = np.arange(rows)
    n = np.arange(LANES)
    first = np.exp(-1j * np.pi * (np.outer(2 * k + 1, m) % (4 * rows)) / (2 * rows))
    turn = np.exp(-1j * np.pi * (np.outer(2 * k + 1, n) % (2 * length)) / length)
    second = np.exp(-2j * np.pi * (np.outer(n, n) % LANES) / LANES)
    first_forward = np.concatenate([first.real, first.imag], axis=0)
    first_inverse = np.concatenate([first.real.T, first.imag.T], axis=1)
    second_forward = np.block([[second.real, second.imag], [-second.imag, second.real]])
    second_inverse = np.block([[second.real, -second.imag], [second.imag, second.real]])
    half = ml_dtypes.bfloat16
    turns = np.stack([turn.real, turn.imag]).astype(np.float32)
    return tuple(
        jnp.asarray(table)
        for table in (
            first_forward.astype(half),
            second_forward.astype(half),
            second_inverse.astype(half),
            first_inverse.astype(half),
            turns,
            (turns * np.float32(2.0 / length)),
        )
    )


def block_kernel(
    side_ref,
    own_ref,
    far_ref,
    other_own_ref,
    other_next_ref,
    other_far_ref,
    taps_ref,
    first_forward_ref,
    second_forward_ref,
    second_inverse_ref,
    first_inverse_ref,
    turn_ref,
    back_turn_ref,
    near_out_ref,
    other_out_ref,
    passed_out_ref,
    lag_out_ref,
    spectra,
    products,
):
    groups, _, rows, lanes = own_ref.shape
    side = side_ref[0]
    signals = (own_ref, far_ref, other_own_ref, other_next_ref, other_far_ref, taps_ref)
    for number, signal in enumerate(signals):
        for pair in range(signal.shape[0] // 2):
            both = jnp.concatenate([signal[2 * pair, 0], signal[2 * pair + 1, 0]], axis=1)
            first = jnp.dot(first_forward_ref[...], both, preferred_element_type=jnp.float32)
            for which in range(2):
                real = first[:rows, which * lanes : (which + 1) * lanes]
                imaginary = first[rows:, which * lanes : (which + 1) * lanes]
                turned = jnp.concatenate(
                    [
                        real * turn_ref[0] - imaginary * turn_ref[1],
                        real * turn_ref[1] + imaginary * turn_ref[0],
                    ],
                    axis=1,
                ).astype(jnp.bfloat16)
                spectra[number, 2 * pair + which] = jnp.dot(
                    turned, second_forward_ref[...], preferred_element_type=jnp.float32
                )

    row_index = lax.broadcasted_iota(jnp.int32, (STRIP, lanes), 0)
    parity = 1.0 - 2.0 * (row_index % 2).astype(jnp.float32)

    def strip(step, carry):
        at = pl.ds(pl.multiple_of(step * STRIP, STRIP), STRIP)

        def load(number, which):
            return spectra[number, which, at, :lanes], spectra[number, which, at, lanes:]

        def store(number, real, imaginary):
            products[number, at, :lanes] = real.astype(jnp.bfloat16)
            products[number, at, lanes:] = imaginary.astype(jnp.bfloat16)

        filters = [load(5, delay) for delay in range(4)]
        gains = []
        for delay in range(4):
            real, imaginary = filters[delay]
            if delay:
                before_real, before_imaginary = filters[delay - 1]
                real = real - parity * before_imaginary
                imaginary = imaginary + parity * before_real
            gains.append((real, side * imaginary))
        lag = [(jnp.zeros((STRIP, lanes), jnp.float32),) * 2 for _ in range(4)]

        def times(total, left, right):
            real = left[0] * right[0] - left[1] * right[1]
            imaginary = left[0] * right[1] + left[1] * right[0]
            return (real, imaginary) if total is None else (total[0] + real, total[1] + imaginary)

        def conjugate_times(total, left, right):
            real = left[0] * right[0] + left[1] * right[1]
            imaginary = left[0] * right[1] - left[1] * right[0]
            return (real, imaginary) if total is None else (total[0] + real, total[1] + imaginary)

        for group in range(groups):
            own, far = load(0, group), load(1, group)
            near = times(times(None, gains[0], own), gains[1], far)
            store(group, *near)
            other_own, other_next, other_far = load(2, group), load(3, group), load(4, group)
            other = conjugate_times(None, gains[0], other_own)
            other = conjugate_times(other, gains[1], other_next)
            other = conjugate_times(other, gains[2], other_far)
            store(groups + group, *other)
            passed = conjugate_times(None, gains[1], other_own)
            passed = conjugate_times(passed, gains[2], other_next)
            passed = conjugate_times(passed, gains[3], other_far)
            store(2 * groups + group, *passed)
            half_own = (0.5 * own[0], 0.5 * own[1])
            lag[0] = conjugate_times(lag[0], own, other_own)
            lag[1] = conjugate_times(lag[1], far, other_own)
            lag[1] = conjugate_times(lag[1], half_own, other_next)
            lag[2] = conjugate_times(lag[2], far, other_next)
            lag[3] = conjugate_times(lag[3], far, other_far)
        lag[3] = (0.5 * lag[3][0], 0.5 * lag[3][1])
        for delay in range(4):
            real, imaginary = lag[delay][0], side * lag[delay][1]
            if delay < 3:
                real = real + parity * (side * lag[delay + 1][1])
                imaginary = imaginary - parity * lag[delay + 1][0]
            store(3 * groups + delay, real, imaginary)
        return carry

    lax.fori_loop(0, rows // STRIP, strip, 0)

    shares = lag_out_ref.shape[0]
    for kind, out_ref in enumerate((near_out_ref, other_out_ref, passed_out_ref, None)):
        for pair in range((groups if kind < 3 else 4) // 2):
            real_parts, imaginary_parts = [], []
            for which in range(2):
                back = jnp.dot(
                    products[kind * groups + 2 * pair + which],
                    second_inverse_ref[...],
                    preferred_element_type=jnp.float32,
                )
                real, imaginary = back[:, :lanes], back[:, lanes:]
                real_parts.append(
                    (real * back_turn_ref[0] + imaginary * back_turn_ref[1]).astype(jnp.bfloat16)
                )
                imaginary_parts.append(
                    (imaginary * back_turn_ref[0] - real * back_turn_ref[1]).astype(jnp.bfloat16)
                )
            rotated = jnp.concatenate(
                [jnp.concatenate(real_parts, axis=1), jnp.concatenate(imaginary_parts, axis=1)],
                axis=0,
            )
            result = jnp.dot(first_inverse_ref[...], rotated, preferred_element_type=jnp.float32)
            result = result.astype(jnp.bfloat16)
            for which in range(2):
                column = result[:, which * lanes : (which + 1) * lanes]
                if kind < 3:
                    out_ref[2 * pair + which, 0] = column
                else:
                    column = column.reshape(shares, rows // shares, lanes)
                    lag_out_ref[:, 2 * pair + which, 0] = column


def block_products(side, signals, other, taps, tables, start, shares):
    groups, filters, rows, lanes = signals[0].shape
    block = pl.BlockSpec((groups, 1, rows, lanes), lambda f: (0, f, 0, 0))
    other_block = pl.BlockSpec((groups, 1, rows, lanes), lambda f: (0, f + start, 0, 0))
    taps_block = pl.BlockSpec((4, 1, rows, lanes), lambda f: (0, f + start, 0, 0))
    lag_block = pl.BlockSpec((shares, 4, 1, rows // shares, lanes), lambda f: (0, 0, f, 0, 0))

    def whole(table):
        return pl.BlockSpec(table.shape, lambda f: (0,) * table.ndim)

    made = jax.ShapeDtypeStruct(signals[0].shape, jnp.bfloat16)
    lag = jax.ShapeDtypeStruct((shares, 4, filters, rows // shares, lanes), jnp.bfloat16)
    own, far, other_next, other_far = signals
    return pl.pallas_call(
        block_kernel,
        grid=(filters,),
        in_specs=[pl.BlockSpec(memory_space=pltpu.SMEM)]
        + [block, block, other_block, block, block, taps_block]
        + [whole(table) for table in tables],
        out_specs=[block, block, block, lag_block],
        out_shape=[made, made, made, lag],
        scratch_shapes=[
            pltpu.VMEM((6, groups, rows, 2 * lanes), jnp.float32),
            pltpu.VMEM((3 * groups + 4, rows, 2 * lanes), jnp.bfloat16),
        ],
        compiler_params=pltpu.CompilerParams(vmem_limit_bytes=VMEM_BYTES),
        cost_estimate=pl.CostEstimate(flops=1, bytes_accessed=1, transcendentals=0),
    )(side, own, far, other, other_next, other_far, taps, *tables)


def product(left, right):
    return (left.astype(jnp.float32) * right.astype(jnp.float32)).astype(jnp.bfloat16)


def enter_kernel(first_ref, gate_ref, values_ref, cotangent_ref, out_gate_ref, *out_refs):
    channels, width = gate_ref.shape
    groups, rows = out_refs[0].shape[0], width // LANES

    def fill(left_ref, right_ref):
        made = product(left_ref[...], right_ref[...]).astype(jnp.float32)
        made = made.reshape(channels, rows, LANES).astype(jnp.bfloat16)
        made = made.reshape(groups, channels // groups, rows, LANES)
        start = 0
        for out_ref in out_refs:
            out_ref[...] = made[:, start : start + out_ref.shape[1]]
            start += out_ref.shape[1]

    @pl.when(first_ref[0] == 1)
    def _():
        fill(gate_ref, values_ref)

    @pl.when(first_ref[0] == 0)
    def _():
        fill(cotangent_ref, out_gate_ref)


def enter(first, flat, filters, counts):
    channels, local_len = flat[0].shape
    groups, rows = channels // filters, local_len // LANES
    block = (channels, EDGE_ROWS * LANES)
    of_first = pl.BlockSpec(block, lambda i, first: (0, i * first[0]))
    of_second = pl.BlockSpec(block, lambda i, first: (0, i * (1 - first[0])))
    return pl.pallas_call(
        enter_kernel,
        grid_spec=pltpu.PrefetchScalarGridSpec(
            num_scalar_prefetch=1,
            grid=(rows // EDGE_ROWS,),
            in_specs=[of_first, of_first, of_second, of_second],
            out_specs=[
                pl.BlockSpec((groups, count, EDGE_ROWS, LANES), lambda i, first: (0, 0, i, 0))
                for count in counts
            ],
        ),
        out_shape=[
            jax.ShapeDtypeStruct((groups, count, rows, LANES), jnp.bfloat16) for count in counts
        ],
        compiler_params=pltpu.CompilerParams(vmem_limit_bytes=VMEM_BYTES),
        cost_estimate=pl.CostEstimate(
            flops=2 * channels * local_len,
            bytes_accessed=6 * channels * local_len,
            transcendentals=0,
        ),
    )(first, *flat)


def leave_kernel(has_received, has_made, *refs):
    first_ref, skip_ref, gate_ref, values_ref, cotangent_ref, out_gate_ref, *refs = refs
    channels, width = gate_ref.shape
    parts, rows = len(SHARES), width // LANES
    signal_refs, refs = refs[:parts], refs[parts:]
    signal = jnp.concatenate([ref[...] for ref in signal_refs], axis=1).astype(jnp.float32)
    if has_received:
        received = jnp.concatenate([ref[...] for ref in refs[:parts]], axis=1)
        signal, refs = signal + received.astype(jnp.float32), refs[parts:]
    if has_made:
        made_refs, refs = refs[:4], refs[4:]
    out_refs = refs
    signal = signal.reshape(channels, rows, LANES).reshape(channels, width)
    skip = skip_ref[...]

    def finish(left_ref, right_ref, factor_refs, result_refs, kept):
        term = product(left_ref[...], right_ref[...]).astype(jnp.float32)
        total = signal + skip * term
        for factor_ref, result_ref in zip(factor_refs, result_refs):
            result_ref[...] = (factor_ref[...].astype(jnp.float32) * total).astype(jnp.bfloat16)
        if has_made:

            @pl.when(pl.program_id(0) == 0)
            def _():
                for number in kept:
                    out_refs[number][...] = made_refs[number][...]

    @pl.when(first_ref[0] == 1)
    def _():
        finish(gate_ref, values_ref, (out_gate_ref, cotangent_ref), out_refs[:2], (2, 3))

    @pl.when(first_ref[0] == 0)
    def _():
        finish(cotangent_ref, out_gate_ref, (values_ref, gate_ref), out_refs[2:], (0, 1))


def leave(first, skip_gain, flat, signal_parts, received_parts=(), made=()):
    channels, local_len = flat[0].shape
    parts = (*signal_parts, *received_parts)
    block = (channels, EDGE_ROWS * LANES)
    flat_block = pl.BlockSpec(block, lambda i, first: (0, i))
    still_block = pl.BlockSpec(block, lambda i, first: (0, 0))
    of_first = pl.BlockSpec(block, lambda i, first: (0, i * first[0]))
    of_second = pl.BlockSpec(block, lambda i, first: (0, i * (1 - first[0])))
    before = 6 + len(parts)
    return pl.pallas_call(
        lambda *refs: leave_kernel(bool(received_parts), bool(made), *refs),
        grid_spec=pltpu.PrefetchScalarGridSpec(
            num_scalar_prefetch=1,
            grid=(local_len // (EDGE_ROWS * LANES),),
            in_specs=[pl.BlockSpec((channels, 1), lambda i, first: (0, 0))]
            + [flat_block] * 4
            + [
                pl.BlockSpec((*part.shape[:2], EDGE_ROWS, LANES), lambda i, first: (0, 0, i, 0))
                for part in parts
            ]
            + [still_block] * len(made),
            out_specs=[of_first, of_first, of_second, of_second],
        ),
        out_shape=[jax.ShapeDtypeStruct((channels, local_len), jnp.bfloat16)] * 4,
        input_output_aliases={before + number: number for number in range(len(made))},
        compiler_params=pltpu.CompilerParams(vmem_limit_bytes=VMEM_BYTES),
        cost_estimate=pl.CostEstimate(
            flops=8 * channels * local_len,
            bytes_accessed=14 * channels * local_len,
            transcendentals=0,
        ),
    )(first, skip_gain[:, None], *flat, *parts, *made)


def rotation(hop):
    return [(index, (index + hop) % 4) for index in range(4)]


def block_shards(input_gate, output_gate, values, cotangent, filter_raw, filter_decay, skip_gain):
    context_index = lax.axis_index("ctx")
    channels, local_len = input_gate.shape
    filters = filter_raw.shape[0]
    rows = local_len // LANES
    seq_len = local_len * lax.axis_size("ctx")
    data_size = lax.axis_size("dp")
    tables = block_tables(rows)
    side = jnp.where(context_index < 2, 1.0, -1.0).astype(jnp.float32).reshape(1)
    near_start = (context_index < 2).astype(jnp.int32).reshape(1)
    flat = (input_gate, values, cotangent, output_gate)
    own_parts = enter(near_start, flat, filters, SHARES)
    routes = ([(1, 2), (2, 1)], [(0, 2), (3, 1)], [(0, 1), (3, 2)])
    back_route = [(1, 0), (2, 3)]

    positions = (context_index * local_len + jnp.arange(local_len, dtype=jnp.int32)).astype(
        jnp.float32
    )
    filter_scale = seq_len ** (-0.5)

    def envelope(decay):
        return jnp.exp(-decay[:, None] * (positions[None, :] / seq_len))

    share = filters // data_size
    first_filter = lax.axis_index("dp") * share
    raw_share = lax.dynamic_slice_in_dim(filter_raw, first_filter, share, 0)
    decay_share = lax.dynamic_slice_in_dim(filter_decay, first_filter, share, 0)
    taps = (raw_share.astype(jnp.float32) * envelope(decay_share) * filter_scale).astype(
        jnp.bfloat16
    )
    taps = taps.reshape(1, share, rows, LANES)
    turned = [taps] + [lax.ppermute(taps, "ctx", rotation(hop)) for hop in (1, 2, 3)]
    turned = jnp.concatenate(turned[::-1] + turned[:0:-1], axis=0)
    taps = lax.dynamic_slice_in_dim(turned, 3 - context_index, 4, 0)
    own_parts, taps, rest = lax.optimization_barrier((own_parts, taps, 1 - near_start))
    arrivals = [lax.ppermute(own_parts[0], "ctx", route) for route in routes]
    taps = lax.all_gather(taps, "dp", axis=1, tiled=True)
    (other,) = enter(rest, flat, filters, (filters,))

    def lag_shares(pieces):
        pieces = lax.all_to_all(pieces, "dp", split_axis=0, concat_axis=0, tiled=True)
        return jnp.sum(pieces.astype(jnp.float32), axis=0).astype(jnp.bfloat16)

    def lag_sum(pieces):
        def block(index):
            return lax.dynamic_index_in_dim(pieces, index, 0, keepdims=False)

        total = block(context_index).astype(jnp.float32)
        for hop in (1, 2, 3):
            leaving = block((context_index + hop) % 4)
            total += lax.ppermute(leaving, "ctx", rotation(hop)).astype(jnp.float32)
        total = total.astype(jnp.bfloat16)
        spread = jnp.broadcast_to(total[None], (data_size, *total.shape))
        spread = lax.all_to_all(spread, "dp", split_axis=0, concat_axis=0, tiled=True)
        return jnp.transpose(spread, (1, 0, 2, 3)).reshape(total.shape[0], rows, LANES)

    near_parts, other_parts, received_parts, lag_parts = [], [], [], []
    start, pending = 0, None
    for number, own in enumerate(own_parts):
        leaving = own_parts[number + 1] if number + 1 < len(own_parts) else None
        arrivals, own, leaving, pending, received_parts, lag_parts, near_parts, other = (
            lax.optimization_barrier(
                (arrivals, own, leaving, pending, received_parts, lag_parts, near_parts, other)
            )
        )
        other_next, other_far, far = arrivals
        if leaving is not None:
            arrivals = [lax.ppermute(leaving, "ctx", route) for route in routes]
        if pending is not None:
            received_parts.append(lax.ppermute(pending[0], "ctx", back_route))
            lag_parts.append(lag_shares(pending[1]))
        near_out, other_out, *pending = block_products(
            side, (own, far, other_next, other_far), other, taps, tables, start, data_size
        )
        start += own.shape[1]
        near_parts.append(near_out)
        other_parts.append(other_out)
    pending, received_parts, lag_parts, near_parts = lax.optimization_barrier(
        (pending, received_parts, lag_parts, near_parts)
    )
    received = lax.ppermute(pending[0], "ctx", back_route)
    made = leave(near_start, skip_gain, flat, near_parts)
    received, late, made = lax.optimization_barrier((received, lag_shares(pending[1]), made))
    received_parts.append(received)
    lag = lag_sum(jnp.concatenate([*lag_parts, late], axis=1)).reshape(filters, local_len)
    grad_filter = lag.astype(jnp.float32) * envelope(filter_decay) * filter_scale
    outputs, grad_output_gate, grad_input_gate, grad_values = leave(
        1 - near_start, skip_gain, flat, other_parts, received_parts, made
    )
    return (outputs, grad_input_gate, grad_output_gate, grad_values, grad_filter)


def chosen_shards(dp, ctx):
    def run(input_gate, *others):
        channels, local_len = input_gate.shape
        filters = others[3].shape[0]
        by_blocks = (
            ctx == 4
            and local_len % (LANES * STRIP * dp) == 0
            and local_len % (LANES * EDGE_ROWS) == 0
            and channels % (2 * filters) == 0
            and filters % dp == 0
            and filters == sum(SHARES)
        )
        return (block_shards if by_blocks else shards)(input_gate, *others)

    return run


def solution(mesh):
    return jax.shard_map(
        chosen_shards(mesh.shape["dp"], mesh.shape["ctx"]),
        mesh=mesh,
        in_specs=(
            P("dp", "ctx"),
            P("dp", "ctx"),
            P("dp", "ctx"),
            P("dp", "ctx"),
            P(None, "ctx"),
            P(),
            P("dp"),
        ),
        out_specs=(P("dp", "ctx"), P("dp", "ctx"), P("dp", "ctx"), P("dp", "ctx"), P(None, "ctx")),
        check_vma=False,
    )
```

```python
import math

import jax
import jax.numpy as jnp
import ml_dtypes
import numpy as np
from jax import lax
from jax.experimental import pallas as pl
from jax.experimental.pallas import tpu as pltpu
from jax.sharding import PartitionSpec as P

N1 = 512
N2 = 512
FFT_LEN = 262144


two_pi = 2.0 * math.pi


def first_tables(row_total):
    first_index = jnp.arange(N1, dtype=jnp.int32)
    source_rows = jnp.arange(row_total, dtype=jnp.int32)
    angles = (first_index[:, None] * source_rows[None, :] % N1).astype(jnp.float32) * (two_pi / N1)
    cosine = jnp.cos(angles).astype(jnp.bfloat16)
    minus_sine = (-jnp.sin(angles)).astype(jnp.bfloat16)
    forward_table = jnp.concatenate([cosine, minus_sine], axis=0)
    inverse_table = jnp.stack([cosine.T, minus_sine.T], axis=2)
    return (forward_table, inverse_table)


def second_tables():
    second_index = jnp.arange(N2, dtype=jnp.int32)
    angles = (second_index[:, None] * second_index[None, :] % N2).astype(jnp.float32) * (
        two_pi / N2
    )
    cosine = jnp.cos(angles).astype(jnp.bfloat16)
    minus_sine = (-jnp.sin(angles)).astype(jnp.bfloat16)
    forward_table = jnp.stack(
        [
            jnp.concatenate([cosine, minus_sine], axis=1),
            jnp.concatenate([-minus_sine, cosine], axis=1),
        ],
        axis=0,
    )
    inverse_table = jnp.concatenate(
        [
            jnp.concatenate([cosine, -minus_sine], axis=1),
            jnp.concatenate([minus_sine, cosine], axis=1),
        ],
        axis=0,
    )
    return (forward_table, inverse_table)


def twiddle_table(spectrum_rows, columns):
    angles = (spectrum_rows[:, None] * columns[None, :] % FFT_LEN).astype(jnp.float32) * (
        two_pi / FFT_LEN
    )
    return (jnp.cos(angles), -jnp.sin(angles))


def halves(array):
    return (array[..., :N2], array[..., N2:])


def joined(real_part, imaginary_part):
    return jnp.concatenate([real_part, imaginary_part], axis=-1).astype(jnp.bfloat16)


def spectral_products(mix_spec, weight_spec, filter_spec, which):
    lead = mix_spec.shape[:-2]
    filters = filter_spec.shape[-2]
    filter_real, filter_imaginary = halves(filter_spec.astype(jnp.float32))
    filter_real = jnp.expand_dims(filter_real, -3)
    filter_imaginary = jnp.expand_dims(filter_imaginary, -3)
    outcome = []
    mix_real, mix_imaginary = halves(mix_spec.reshape(lead + (-1, filters, 2 * N2)))
    weight_real, weight_imaginary = halves(weight_spec.reshape(lead + (-1, filters, 2 * N2)))
    for name in which:
        if name == "convolve":
            made = joined(
                mix_real * filter_real - mix_imaginary * filter_imaginary,
                mix_real * filter_imaginary + mix_imaginary * filter_real,
            )
        elif name == "correlate":
            made = joined(
                filter_real * weight_real + filter_imaginary * weight_imaginary,
                filter_real * weight_imaginary - filter_imaginary * weight_real,
            )
        else:
            made = joined(
                mix_real * weight_real + mix_imaginary * weight_imaginary,
                mix_real * weight_imaginary - mix_imaginary * weight_real,
            )
        outcome.append(made.reshape(lead + (-1, 2 * N2)))
    return outcome


def shards(input_gate, output_gate, values, cotangent, filter_raw, filter_decay, skip_gain):
    context_size = lax.axis_size("ctx")
    context_index = lax.axis_index("ctx")
    channels, local_len = input_gate.shape
    filters = filter_raw.shape[0]
    groups = channels // filters
    row_local = local_len // N2
    row_total = row_local * context_size
    seq_len = local_len * context_size
    first_forward, first_inverse = first_tables(row_total)
    second_forward, second_inverse = second_tables()
    inverse_scale = 1.0 / FFT_LEN
    mixed_input = (input_gate.astype(jnp.float32) * values.astype(jnp.float32)).astype(jnp.bfloat16)
    weighted = (cotangent.astype(jnp.float32) * output_gate.astype(jnp.float32)).astype(
        jnp.bfloat16
    )
    global_positions = (context_index * local_len + jnp.arange(local_len, dtype=jnp.int32)).astype(
        jnp.float32
    )
    envelope = jnp.exp(-filter_decay[:, None] * (global_positions[None, :] / seq_len))
    filter_scale = seq_len ** (-0.5)
    filter_taps = (filter_raw.astype(jnp.float32) * envelope * filter_scale).astype(jnp.bfloat16)
    spread_count = filters // context_size
    full_real, full_imaginary = twiddle_table(
        jnp.arange(N1, dtype=jnp.int32), jnp.arange(N2, dtype=jnp.int32)
    )
    pair = jnp.stack([mixed_input, weighted], axis=0).reshape(2, groups, filters, row_local, N2)
    taps_block = filter_taps.reshape(1, 1, filters, row_local, N2)
    pair_whole, taps_whole = (
        lax.all_to_all(pair, "ctx", split_axis=2, concat_axis=3, tiled=True),
        lax.all_to_all(taps_block, "ctx", split_axis=2, concat_axis=3, tiled=True),
    )
    signal_count = 2 * groups * spread_count
    every = jnp.concatenate(
        [
            pair_whole.reshape(signal_count, row_total, N2),
            taps_whole.reshape(spread_count, row_total, N2),
        ],
        axis=0,
    )
    first = jnp.einsum("km,imn->ikn", first_forward, every, preferred_element_type=jnp.float32)
    first_real = first[:, :N1]
    first_imaginary = first[:, N1:]
    turned = jnp.stack(
        [
            first_real * full_real - first_imaginary * full_imaginary,
            first_real * full_imaginary + first_imaginary * full_real,
        ],
        axis=1,
    ).astype(jnp.bfloat16)
    spectra = jnp.einsum(
        "ipkn,pnl->ikl", turned, second_forward, preferred_element_type=jnp.float32
    )
    signal_spec = spectra[:signal_count].reshape(2, groups * spread_count, N1, 2 * N2)
    filter_spec = spectra[signal_count:].astype(jnp.bfloat16)
    filter_spec = jnp.transpose(filter_spec, (1, 0, 2))
    mix_spec = jnp.transpose(signal_spec[0], (1, 0, 2))
    weight_spec = jnp.transpose(signal_spec[1], (1, 0, 2))
    made = spectral_products(mix_spec, weight_spec, filter_spec, ["convolve", "correlate", "lag"])
    stacked = jnp.transpose(jnp.concatenate(made, axis=1), (1, 0, 2))
    back = jnp.einsum("ikl,lm->ikm", stacked, second_inverse, preferred_element_type=jnp.float32)
    back_real, back_imaginary = halves(back)
    rotated = jnp.stack(
        [
            (back_real * full_real + back_imaginary * full_imaginary) * inverse_scale,
            (back_imaginary * full_real - back_real * full_imaginary) * inverse_scale,
        ],
        axis=1,
    ).astype(jnp.bfloat16)
    inverted = jnp.einsum(
        "mkp,ipkn->imn", first_inverse, rotated, preferred_element_type=jnp.float32
    )
    inverted = inverted.astype(jnp.bfloat16).reshape(3, groups, spread_count, row_total, N2)
    back_rows = lax.all_to_all(inverted[:2], "ctx", split_axis=3, concat_axis=2, tiled=True)
    convolved = back_rows[0].reshape(channels, local_len)
    correlated = back_rows[1].reshape(channels, local_len)
    lag_whole = jnp.sum(inverted[2].astype(jnp.float32), axis=0)
    lag_part = (
        lax.all_to_all(
            lag_whole.astype(jnp.bfloat16), "ctx", split_axis=1, concat_axis=0, tiled=True
        )
        .astype(lag_whole.dtype)
        .reshape(filters, local_len)
    )
    summed = convolved.astype(jnp.float32) + skip_gain[:, None] * mixed_input.astype(jnp.float32)
    outputs = (output_gate.astype(jnp.float32) * summed).astype(jnp.bfloat16)
    grad_output_gate = (cotangent.astype(jnp.float32) * summed).astype(jnp.bfloat16)
    back_total = correlated.astype(jnp.float32) + skip_gain[:, None] * weighted.astype(jnp.float32)
    grad_input_gate = (back_total * values.astype(jnp.float32)).astype(jnp.bfloat16)
    grad_values = (back_total * input_gate.astype(jnp.float32)).astype(jnp.bfloat16)
    lag_total = lax.psum(lag_part.astype(jnp.bfloat16), "dp").astype(jnp.float32)
    grad_filter = lag_total * envelope * filter_scale
    return (outputs, grad_input_gate, grad_output_gate, grad_values, grad_filter)


LANES = 128
SHARES = (7, 5, 4)
STRIP = 16
EDGE_ROWS = 32
VMEM_BYTES = 60 * 2**20


def block_tables(rows):
    length = 2 * rows * LANES
    k = np.arange(rows)
    m = np.arange(rows)
    n = np.arange(LANES)
    first = np.exp(-1j * np.pi * (np.outer(2 * k + 1, m) % (4 * rows)) / (2 * rows))
    turn = np.exp(-1j * np.pi * (np.outer(2 * k + 1, n) % (2 * length)) / length)
    second = np.exp(-2j * np.pi * (np.outer(n, n) % LANES) / LANES)
    first_forward = np.concatenate([first.real, first.imag], axis=0)
    first_inverse = np.concatenate([first.real.T, first.imag.T], axis=1)
    second_forward = np.block([[second.real, second.imag], [-second.imag, second.real]])
    second_inverse = np.block([[second.real, -second.imag], [second.imag, second.real]])
    half = ml_dtypes.bfloat16
    turns = np.stack([turn.real, turn.imag]).astype(np.float32)
    return tuple(
        jnp.asarray(table)
        for table in (
            first_forward.astype(half),
            second_forward.astype(half),
            second_inverse.astype(half),
            first_inverse.astype(half),
            turns,
            (turns * np.float32(2.0 / length)),
        )
    )


def block_kernel(
    side_ref,
    own_ref,
    far_ref,
    other_own_ref,
    other_next_ref,
    other_far_ref,
    taps_ref,
    first_forward_ref,
    second_forward_ref,
    second_inverse_ref,
    first_inverse_ref,
    turn_ref,
    back_turn_ref,
    near_out_ref,
    other_out_ref,
    passed_out_ref,
    lag_out_ref,
    spectra,
    products,
):
    groups, _, rows, lanes = own_ref.shape
    side = side_ref[0]
    signals = (own_ref, far_ref, other_own_ref, other_next_ref, other_far_ref, taps_ref)
    for number, signal in enumerate(signals):
        for pair in range(signal.shape[0] // 2):
            both = jnp.concatenate([signal[2 * pair, 0], signal[2 * pair + 1, 0]], axis=1)
            first = jnp.dot(first_forward_ref[...], both, preferred_element_type=jnp.float32)
            for which in range(2):
                real = first[:rows, which * lanes : (which + 1) * lanes]
                imaginary = first[rows:, which * lanes : (which + 1) * lanes]
                turned = jnp.concatenate(
                    [
                        real * turn_ref[0] - imaginary * turn_ref[1],
                        real * turn_ref[1] + imaginary * turn_ref[0],
                    ],
                    axis=1,
                ).astype(jnp.bfloat16)
                spectra[number, 2 * pair + which] = jnp.dot(
                    turned, second_forward_ref[...], preferred_element_type=jnp.float32
                )

    row_index = lax.broadcasted_iota(jnp.int32, (STRIP, lanes), 0)
    parity = 1.0 - 2.0 * (row_index % 2).astype(jnp.float32)

    def strip(step, carry):
        at = pl.ds(pl.multiple_of(step * STRIP, STRIP), STRIP)

        def load(number, which):
            return spectra[number, which, at, :lanes], spectra[number, which, at, lanes:]

        def store(number, real, imaginary):
            products[number, at, :lanes] = real.astype(jnp.bfloat16)
            products[number, at, lanes:] = imaginary.astype(jnp.bfloat16)

        filters = [load(5, delay) for delay in range(4)]
        gains = []
        for delay in range(4):
            real, imaginary = filters[delay]
            if delay:
                before_real, before_imaginary = filters[delay - 1]
                real = real - parity * before_imaginary
                imaginary = imaginary + parity * before_real
            gains.append((real, side * imaginary))
        lag = [(jnp.zeros((STRIP, lanes), jnp.float32),) * 2 for _ in range(4)]

        def times(total, left, right):
            real = left[0] * right[0] - left[1] * right[1]
            imaginary = left[0] * right[1] + left[1] * right[0]
            return (real, imaginary) if total is None else (total[0] + real, total[1] + imaginary)

        def conjugate_times(total, left, right):
            real = left[0] * right[0] + left[1] * right[1]
            imaginary = left[0] * right[1] - left[1] * right[0]
            return (real, imaginary) if total is None else (total[0] + real, total[1] + imaginary)

        for group in range(groups):
            own, far = load(0, group), load(1, group)
            near = times(times(None, gains[0], own), gains[1], far)
            store(group, *near)
            other_own, other_next, other_far = load(2, group), load(3, group), load(4, group)
            other = conjugate_times(None, gains[0], other_own)
            other = conjugate_times(other, gains[1], other_next)
            other = conjugate_times(other, gains[2], other_far)
            store(groups + group, *other)
            passed = conjugate_times(None, gains[1], other_own)
            passed = conjugate_times(passed, gains[2], other_next)
            passed = conjugate_times(passed, gains[3], other_far)
            store(2 * groups + group, *passed)
            half_own = (0.5 * own[0], 0.5 * own[1])
            lag[0] = conjugate_times(lag[0], own, other_own)
            lag[1] = conjugate_times(lag[1], far, other_own)
            lag[1] = conjugate_times(lag[1], half_own, other_next)
            lag[2] = conjugate_times(lag[2], far, other_next)
            lag[3] = conjugate_times(lag[3], far, other_far)
        lag[3] = (0.5 * lag[3][0], 0.5 * lag[3][1])
        for delay in range(4):
            real, imaginary = lag[delay][0], side * lag[delay][1]
            if delay < 3:
                real = real + parity * (side * lag[delay + 1][1])
                imaginary = imaginary - parity * lag[delay + 1][0]
            store(3 * groups + delay, real, imaginary)
        return carry

    lax.fori_loop(0, rows // STRIP, strip, 0)

    shares = lag_out_ref.shape[0]
    for kind, out_ref in enumerate((near_out_ref, other_out_ref, passed_out_ref, None)):
        for pair in range((groups if kind < 3 else 4) // 2):
            real_parts, imaginary_parts = [], []
            for which in range(2):
                back = jnp.dot(
                    products[kind * groups + 2 * pair + which],
                    second_inverse_ref[...],
                    preferred_element_type=jnp.float32,
                )
                real, imaginary = back[:, :lanes], back[:, lanes:]
                real_parts.append(
                    (real * back_turn_ref[0] + imaginary * back_turn_ref[1]).astype(jnp.bfloat16)
                )
                imaginary_parts.append(
                    (imaginary * back_turn_ref[0] - real * back_turn_ref[1]).astype(jnp.bfloat16)
                )
            rotated = jnp.concatenate(
                [jnp.concatenate(real_parts, axis=1), jnp.concatenate(imaginary_parts, axis=1)],
                axis=0,
            )
            result = jnp.dot(first_inverse_ref[...], rotated, preferred_element_type=jnp.float32)
            result = result.astype(jnp.bfloat16)
            for which in range(2):
                column = result[:, which * lanes : (which + 1) * lanes]
                if kind < 3:
                    out_ref[2 * pair + which, 0] = column
                else:
                    column = column.reshape(shares, rows // shares, lanes)
                    lag_out_ref[:, 2 * pair + which, 0] = column


def block_products(side, signals, other, taps, tables, start, shares):
    groups, filters, rows, lanes = signals[0].shape
    block = pl.BlockSpec((groups, 1, rows, lanes), lambda f: (0, f, 0, 0))
    other_block = pl.BlockSpec((groups, 1, rows, lanes), lambda f: (0, f + start, 0, 0))
    taps_block = pl.BlockSpec((4, 1, rows, lanes), lambda f: (0, f + start, 0, 0))
    lag_block = pl.BlockSpec((shares, 4, 1, rows // shares, lanes), lambda f: (0, 0, f, 0, 0))

    def whole(table):
        return pl.BlockSpec(table.shape, lambda f: (0,) * table.ndim)

    made = jax.ShapeDtypeStruct(signals[0].shape, jnp.bfloat16)
    lag = jax.ShapeDtypeStruct((shares, 4, filters, rows // shares, lanes), jnp.bfloat16)
    own, far, other_next, other_far = signals
    return pl.pallas_call(
        block_kernel,
        grid=(filters,),
        in_specs=[pl.BlockSpec(memory_space=pltpu.SMEM)]
        + [block, block, other_block, block, block, taps_block]
        + [whole(table) for table in tables],
        out_specs=[block, block, block, lag_block],
        out_shape=[made, made, made, lag],
        scratch_shapes=[
            pltpu.VMEM((6, groups, rows, 2 * lanes), jnp.float32),
            pltpu.VMEM((3 * groups + 4, rows, 2 * lanes), jnp.bfloat16),
        ],
        compiler_params=pltpu.CompilerParams(vmem_limit_bytes=VMEM_BYTES),
        cost_estimate=pl.CostEstimate(flops=1, bytes_accessed=1, transcendentals=0),
    )(side, own, far, other, other_next, other_far, taps, *tables)


def product(left, right):
    return (left.astype(jnp.float32) * right.astype(jnp.float32)).astype(jnp.bfloat16)


def enter_kernel(first_ref, gate_ref, values_ref, cotangent_ref, out_gate_ref, *out_refs):
    channels, width = gate_ref.shape
    groups, rows = out_refs[0].shape[0], width // LANES

    def fill(left_ref, right_ref):
        made = product(left_ref[...], right_ref[...]).astype(jnp.float32)
        made = made.reshape(channels, rows, LANES).astype(jnp.bfloat16)
        made = made.reshape(groups, channels // groups, rows, LANES)
        start = 0
        for out_ref in out_refs:
            out_ref[...] = made[:, start : start + out_ref.shape[1]]
            start += out_ref.shape[1]

    @pl.when(first_ref[0] == 1)
    def _():
        fill(gate_ref, values_ref)

    @pl.when(first_ref[0] == 0)
    def _():
        fill(cotangent_ref, out_gate_ref)


def enter(first, flat, filters, counts):
    channels, local_len = flat[0].shape
    groups, rows = channels // filters, local_len // LANES
    block = (channels, EDGE_ROWS * LANES)
    of_first = pl.BlockSpec(block, lambda i, first: (0, i * first[0]))
    of_second = pl.BlockSpec(block, lambda i, first: (0, i * (1 - first[0])))
    return pl.pallas_call(
        enter_kernel,
        grid_spec=pltpu.PrefetchScalarGridSpec(
            num_scalar_prefetch=1,
            grid=(rows // EDGE_ROWS,),
            in_specs=[of_first, of_first, of_second, of_second],
            out_specs=[
                pl.BlockSpec((groups, count, EDGE_ROWS, LANES), lambda i, first: (0, 0, i, 0))
                for count in counts
            ],
        ),
        out_shape=[
            jax.ShapeDtypeStruct((groups, count, rows, LANES), jnp.bfloat16) for count in counts
        ],
        compiler_params=pltpu.CompilerParams(vmem_limit_bytes=VMEM_BYTES),
        cost_estimate=pl.CostEstimate(
            flops=2 * channels * local_len,
            bytes_accessed=6 * channels * local_len,
            transcendentals=0,
        ),
    )(first, *flat)


def leave_kernel(has_received, has_made, *refs):
    first_ref, skip_ref, gate_ref, values_ref, cotangent_ref, out_gate_ref, *refs = refs
    channels, width = gate_ref.shape
    parts, rows = len(SHARES), width // LANES
    signal_refs, refs = refs[:parts], refs[parts:]
    signal = jnp.concatenate([ref[...] for ref in signal_refs], axis=1).astype(jnp.float32)
    if has_received:
        received = jnp.concatenate([ref[...] for ref in refs[:parts]], axis=1)
        signal, refs = signal + received.astype(jnp.float32), refs[parts:]
    if has_made:
        made_refs, refs = refs[:4], refs[4:]
    out_refs = refs
    signal = signal.reshape(channels, rows, LANES).reshape(channels, width)
    skip = skip_ref[...]

    def finish(left_ref, right_ref, factor_refs, result_refs, kept):
        term = product(left_ref[...], right_ref[...]).astype(jnp.float32)
        total = signal + skip * term
        for factor_ref, result_ref in zip(factor_refs, result_refs):
            result_ref[...] = (factor_ref[...].astype(jnp.float32) * total).astype(jnp.bfloat16)
        if has_made:

            @pl.when(pl.program_id(0) == 0)
            def _():
                for number in kept:
                    out_refs[number][...] = made_refs[number][...]

    @pl.when(first_ref[0] == 1)
    def _():
        finish(gate_ref, values_ref, (out_gate_ref, cotangent_ref), out_refs[:2], (2, 3))

    @pl.when(first_ref[0] == 0)
    def _():
        finish(cotangent_ref, out_gate_ref, (values_ref, gate_ref), out_refs[2:], (0, 1))


def leave(first, skip_gain, flat, signal_parts, received_parts=(), made=()):
    channels, local_len = flat[0].shape
    parts = (*signal_parts, *received_parts)
    block = (channels, EDGE_ROWS * LANES)
    flat_block = pl.BlockSpec(block, lambda i, first: (0, i))
    still_block = pl.BlockSpec(block, lambda i, first: (0, 0))
    of_first = pl.BlockSpec(block, lambda i, first: (0, i * first[0]))
    of_second = pl.BlockSpec(block, lambda i, first: (0, i * (1 - first[0])))
    before = 6 + len(parts)
    return pl.pallas_call(
        lambda *refs: leave_kernel(bool(received_parts), bool(made), *refs),
        grid_spec=pltpu.PrefetchScalarGridSpec(
            num_scalar_prefetch=1,
            grid=(local_len // (EDGE_ROWS * LANES),),
            in_specs=[pl.BlockSpec((channels, 1), lambda i, first: (0, 0))]
            + [flat_block] * 4
            + [
                pl.BlockSpec((*part.shape[:2], EDGE_ROWS, LANES), lambda i, first: (0, 0, i, 0))
                for part in parts
            ]
            + [still_block] * len(made),
            out_specs=[of_first, of_first, of_second, of_second],
        ),
        out_shape=[jax.ShapeDtypeStruct((channels, local_len), jnp.bfloat16)] * 4,
        input_output_aliases={before + number: number for number in range(len(made))},
        compiler_params=pltpu.CompilerParams(vmem_limit_bytes=VMEM_BYTES),
        cost_estimate=pl.CostEstimate(
            flops=8 * channels * local_len,
            bytes_accessed=14 * channels * local_len,
            transcendentals=0,
        ),
    )(first, skip_gain[:, None], *flat, *parts, *made)


def rotation(hop):
    return [(index, (index + hop) % 4) for index in range(4)]


def block_shards(input_gate, output_gate, values, cotangent, filter_raw, filter_decay, skip_gain):
    context_index = lax.axis_index("ctx")
    channels, local_len = input_gate.shape
    filters = filter_raw.shape[0]
    rows = local_len // LANES
    seq_len = local_len * lax.axis_size("ctx")
    data_size = lax.axis_size("dp")
    tables = block_tables(rows)
    side = jnp.where(context_index < 2, 1.0, -1.0).astype(jnp.float32).reshape(1)
    near_start = (context_index < 2).astype(jnp.int32).reshape(1)
    flat = (input_gate, values, cotangent, output_gate)
    own_parts = enter(near_start, flat, filters, SHARES)
    routes = ([(1, 2), (2, 1)], [(0, 2), (3, 1)], [(0, 1), (3, 2)])
    back_route = [(1, 0), (2, 3)]

    positions = (context_index * local_len + jnp.arange(local_len, dtype=jnp.int32)).astype(
        jnp.float32
    )
    filter_scale = seq_len ** (-0.5)

    def envelope(decay):
        return jnp.exp(-decay[:, None] * (positions[None, :] / seq_len))

    share = filters // data_size
    first_filter = lax.axis_index("dp") * share
    raw_share = lax.dynamic_slice_in_dim(filter_raw, first_filter, share, 0)
    decay_share = lax.dynamic_slice_in_dim(filter_decay, first_filter, share, 0)
    taps = (raw_share.astype(jnp.float32) * envelope(decay_share) * filter_scale).astype(
        jnp.bfloat16
    )
    taps = taps.reshape(1, share, rows, LANES)
    turned = [taps] + [lax.ppermute(taps, "ctx", rotation(hop)) for hop in (1, 2, 3)]
    turned = jnp.concatenate(turned[::-1] + turned[:0:-1], axis=0)
    taps = lax.dynamic_slice_in_dim(turned, 3 - context_index, 4, 0)
    own_parts, taps, rest = lax.optimization_barrier((own_parts, taps, 1 - near_start))
    arrivals = [lax.ppermute(own_parts[0], "ctx", route) for route in routes]
    taps = lax.all_gather(taps, "dp", axis=1, tiled=True)
    (other,) = enter(rest, flat, filters, (filters,))

    def lag_shares(pieces):
        pieces = lax.all_to_all(pieces, "dp", split_axis=0, concat_axis=0, tiled=True)
        return jnp.sum(pieces.astype(jnp.float32), axis=0).astype(jnp.bfloat16)

    def lag_block(pieces):
        def block(index):
            return lax.dynamic_index_in_dim(pieces, index, 0, keepdims=False)

        total = block(context_index).astype(jnp.float32)
        for hop in (1, 2, 3):
            leaving = block((context_index + hop) % 4)
            total += lax.ppermute(leaving, "ctx", rotation(hop)).astype(jnp.float32)
        return total.astype(jnp.bfloat16)

    def lag_rows(total):
        spread = jnp.broadcast_to(total[None], (data_size, *total.shape))
        spread = lax.all_to_all(spread, "dp", split_axis=0, concat_axis=0, tiled=True)
        return jnp.transpose(spread, (1, 0, 2, 3)).reshape(total.shape[0], rows, LANES)

    near_parts, other_parts, received_parts, lag_parts = [], [], [], []
    start, pending = 0, None
    for number, own in enumerate(own_parts):
        leaving = own_parts[number + 1] if number + 1 < len(own_parts) else None
        arrivals, own, leaving, pending, received_parts, lag_parts, near_parts, other = (
            lax.optimization_barrier(
                (arrivals, own, leaving, pending, received_parts, lag_parts, near_parts, other)
            )
        )
        other_next, other_far, far = arrivals
        if leaving is not None:
            arrivals = [lax.ppermute(leaving, "ctx", route) for route in routes]
        if pending is not None:
            received_parts.append(lax.ppermute(pending[0], "ctx", back_route))
            lag_parts.append(lag_shares(pending[1]))
        near_out, other_out, *pending = block_products(
            side, (own, far, other_next, other_far), other, taps, tables, start, data_size
        )
        start += own.shape[1]
        near_parts.append(near_out)
        other_parts.append(other_out)
    pending, received_parts, lag_parts, near_parts = lax.optimization_barrier(
        (pending, received_parts, lag_parts, near_parts)
    )
    received = lax.ppermute(pending[0], "ctx", back_route)
    made = leave(near_start, skip_gain, flat, near_parts)
    early = lag_block(jnp.concatenate(lag_parts, axis=1))
    received, early, late, made, rest = lax.optimization_barrier(
        (received, early, lag_shares(pending[1]), made, rest)
    )
    received_parts.append(received)
    final = leave(rest, skip_gain, flat, other_parts, received_parts, made)
    early, late, final = lax.optimization_barrier((lag_rows(early), lag_block(late), final))
    outputs, grad_output_gate, grad_input_gate, grad_values = final
    lag = jnp.concatenate([early, lag_rows(late)], axis=0).reshape(filters, local_len)
    grad_filter = lag.astype(jnp.float32) * envelope(filter_decay) * filter_scale
    return (outputs, grad_input_gate, grad_output_gate, grad_values, grad_filter)


def chosen_shards(dp, ctx):
    def run(input_gate, *others):
        channels, local_len = input_gate.shape
        filters = others[3].shape[0]
        by_blocks = (
            ctx == 4
            and local_len % (LANES * STRIP * dp) == 0
            and local_len % (LANES * EDGE_ROWS) == 0
            and channels % (2 * filters) == 0
            and filters % dp == 0
            and filters == sum(SHARES)
        )
        return (block_shards if by_blocks else shards)(input_gate, *others)

    return run


def solution(mesh):
    return jax.shard_map(
        chosen_shards(mesh.shape["dp"], mesh.shape["ctx"]),
        mesh=mesh,
        in_specs=(
            P("dp", "ctx"),
            P("dp", "ctx"),
            P("dp", "ctx"),
            P("dp", "ctx"),
            P(None, "ctx"),
            P(),
            P("dp"),
        ),
        out_specs=(P("dp", "ctx"), P("dp", "ctx"), P("dp", "ctx"), P("dp", "ctx"), P(None, "ctx")),
        check_vma=False,
    )
```

```python
import math

import jax
import jax.numpy as jnp
import ml_dtypes
import numpy as np
from jax import lax
from jax.experimental import pallas as pl
from jax.experimental.pallas import tpu as pltpu
from jax.sharding import PartitionSpec as P

N1 = 512
N2 = 512
FFT_LEN = 262144


two_pi = 2.0 * math.pi


def first_tables(row_total):
    first_index = jnp.arange(N1, dtype=jnp.int32)
    source_rows = jnp.arange(row_total, dtype=jnp.int32)
    angles = (first_index[:, None] * source_rows[None, :] % N1).astype(jnp.float32) * (two_pi / N1)
    cosine = jnp.cos(angles).astype(jnp.bfloat16)
    minus_sine = (-jnp.sin(angles)).astype(jnp.bfloat16)
    forward_table = jnp.concatenate([cosine, minus_sine], axis=0)
    inverse_table = jnp.stack([cosine.T, minus_sine.T], axis=2)
    return (forward_table, inverse_table)


def second_tables():
    second_index = jnp.arange(N2, dtype=jnp.int32)
    angles = (second_index[:, None] * second_index[None, :] % N2).astype(jnp.float32) * (
        two_pi / N2
    )
    cosine = jnp.cos(angles).astype(jnp.bfloat16)
    minus_sine = (-jnp.sin(angles)).astype(jnp.bfloat16)
    forward_table = jnp.stack(
        [
            jnp.concatenate([cosine, minus_sine], axis=1),
            jnp.concatenate([-minus_sine, cosine], axis=1),
        ],
        axis=0,
    )
    inverse_table = jnp.concatenate(
        [
            jnp.concatenate([cosine, -minus_sine], axis=1),
            jnp.concatenate([minus_sine, cosine], axis=1),
        ],
        axis=0,
    )
    return (forward_table, inverse_table)


def twiddle_table(spectrum_rows, columns):
    angles = (spectrum_rows[:, None] * columns[None, :] % FFT_LEN).astype(jnp.float32) * (
        two_pi / FFT_LEN
    )
    return (jnp.cos(angles), -jnp.sin(angles))


def halves(array):
    return (array[..., :N2], array[..., N2:])


def joined(real_part, imaginary_part):
    return jnp.concatenate([real_part, imaginary_part], axis=-1).astype(jnp.bfloat16)


def spectral_products(mix_spec, weight_spec, filter_spec, which):
    lead = mix_spec.shape[:-2]
    filters = filter_spec.shape[-2]
    filter_real, filter_imaginary = halves(filter_spec.astype(jnp.float32))
    filter_real = jnp.expand_dims(filter_real, -3)
    filter_imaginary = jnp.expand_dims(filter_imaginary, -3)
    outcome = []
    mix_real, mix_imaginary = halves(mix_spec.reshape(lead + (-1, filters, 2 * N2)))
    weight_real, weight_imaginary = halves(weight_spec.reshape(lead + (-1, filters, 2 * N2)))
    for name in which:
        if name == "convolve":
            made = joined(
                mix_real * filter_real - mix_imaginary * filter_imaginary,
                mix_real * filter_imaginary + mix_imaginary * filter_real,
            )
        elif name == "correlate":
            made = joined(
                filter_real * weight_real + filter_imaginary * weight_imaginary,
                filter_real * weight_imaginary - filter_imaginary * weight_real,
            )
        else:
            made = joined(
                mix_real * weight_real + mix_imaginary * weight_imaginary,
                mix_real * weight_imaginary - mix_imaginary * weight_real,
            )
        outcome.append(made.reshape(lead + (-1, 2 * N2)))
    return outcome


def shards(input_gate, output_gate, values, cotangent, filter_raw, filter_decay, skip_gain):
    context_size = lax.axis_size("ctx")
    context_index = lax.axis_index("ctx")
    channels, local_len = input_gate.shape
    filters = filter_raw.shape[0]
    groups = channels // filters
    row_local = local_len // N2
    row_total = row_local * context_size
    seq_len = local_len * context_size
    first_forward, first_inverse = first_tables(row_total)
    second_forward, second_inverse = second_tables()
    inverse_scale = 1.0 / FFT_LEN
    mixed_input = (input_gate.astype(jnp.float32) * values.astype(jnp.float32)).astype(jnp.bfloat16)
    weighted = (cotangent.astype(jnp.float32) * output_gate.astype(jnp.float32)).astype(
        jnp.bfloat16
    )
    global_positions = (context_index * local_len + jnp.arange(local_len, dtype=jnp.int32)).astype(
        jnp.float32
    )
    envelope = jnp.exp(-filter_decay[:, None] * (global_positions[None, :] / seq_len))
    filter_scale = seq_len ** (-0.5)
    filter_taps = (filter_raw.astype(jnp.float32) * envelope * filter_scale).astype(jnp.bfloat16)
    spread_count = filters // context_size
    full_real, full_imaginary = twiddle_table(
        jnp.arange(N1, dtype=jnp.int32), jnp.arange(N2, dtype=jnp.int32)
    )
    pair = jnp.stack([mixed_input, weighted], axis=0).reshape(2, groups, filters, row_local, N2)
    taps_block = filter_taps.reshape(1, 1, filters, row_local, N2)
    pair_whole, taps_whole = (
        lax.all_to_all(pair, "ctx", split_axis=2, concat_axis=3, tiled=True),
        lax.all_to_all(taps_block, "ctx", split_axis=2, concat_axis=3, tiled=True),
    )
    signal_count = 2 * groups * spread_count
    every = jnp.concatenate(
        [
            pair_whole.reshape(signal_count, row_total, N2),
            taps_whole.reshape(spread_count, row_total, N2),
        ],
        axis=0,
    )
    first = jnp.einsum("km,imn->ikn", first_forward, every, preferred_element_type=jnp.float32)
    first_real = first[:, :N1]
    first_imaginary = first[:, N1:]
    turned = jnp.stack(
        [
            first_real * full_real - first_imaginary * full_imaginary,
            first_real * full_imaginary + first_imaginary * full_real,
        ],
        axis=1,
    ).astype(jnp.bfloat16)
    spectra = jnp.einsum(
        "ipkn,pnl->ikl", turned, second_forward, preferred_element_type=jnp.float32
    )
    signal_spec = spectra[:signal_count].reshape(2, groups * spread_count, N1, 2 * N2)
    filter_spec = spectra[signal_count:].astype(jnp.bfloat16)
    filter_spec = jnp.transpose(filter_spec, (1, 0, 2))
    mix_spec = jnp.transpose(signal_spec[0], (1, 0, 2))
    weight_spec = jnp.transpose(signal_spec[1], (1, 0, 2))
    made = spectral_products(mix_spec, weight_spec, filter_spec, ["convolve", "correlate", "lag"])
    stacked = jnp.transpose(jnp.concatenate(made, axis=1), (1, 0, 2))
    back = jnp.einsum("ikl,lm->ikm", stacked, second_inverse, preferred_element_type=jnp.float32)
    back_real, back_imaginary = halves(back)
    rotated = jnp.stack(
        [
            (back_real * full_real + back_imaginary * full_imaginary) * inverse_scale,
            (back_imaginary * full_real - back_real * full_imaginary) * inverse_scale,
        ],
        axis=1,
    ).astype(jnp.bfloat16)
    inverted = jnp.einsum(
        "mkp,ipkn->imn", first_inverse, rotated, preferred_element_type=jnp.float32
    )
    inverted = inverted.astype(jnp.bfloat16).reshape(3, groups, spread_count, row_total, N2)
    back_rows = lax.all_to_all(inverted[:2], "ctx", split_axis=3, concat_axis=2, tiled=True)
    convolved = back_rows[0].reshape(channels, local_len)
    correlated = back_rows[1].reshape(channels, local_len)
    lag_whole = jnp.sum(inverted[2].astype(jnp.float32), axis=0)
    lag_part = (
        lax.all_to_all(
            lag_whole.astype(jnp.bfloat16), "ctx", split_axis=1, concat_axis=0, tiled=True
        )
        .astype(lag_whole.dtype)
        .reshape(filters, local_len)
    )
    summed = convolved.astype(jnp.float32) + skip_gain[:, None] * mixed_input.astype(jnp.float32)
    outputs = (output_gate.astype(jnp.float32) * summed).astype(jnp.bfloat16)
    grad_output_gate = (cotangent.astype(jnp.float32) * summed).astype(jnp.bfloat16)
    back_total = correlated.astype(jnp.float32) + skip_gain[:, None] * weighted.astype(jnp.float32)
    grad_input_gate = (back_total * values.astype(jnp.float32)).astype(jnp.bfloat16)
    grad_values = (back_total * input_gate.astype(jnp.float32)).astype(jnp.bfloat16)
    lag_total = lax.psum(lag_part.astype(jnp.bfloat16), "dp").astype(jnp.float32)
    grad_filter = lag_total * envelope * filter_scale
    return (outputs, grad_input_gate, grad_output_gate, grad_values, grad_filter)


LANES = 128
SHARES = (7, 5, 4)
STRIP = 16
EDGE_ROWS = 32
VMEM_BYTES = 60 * 2**20


def block_tables(rows):
    length = 2 * rows * LANES
    k = np.arange(rows)
    m = np.arange(rows)
    n = np.arange(LANES)
    first = np.exp(-1j * np.pi * (np.outer(2 * k + 1, m) % (4 * rows)) / (2 * rows))
    turn = np.exp(-1j * np.pi * (np.outer(2 * k + 1, n) % (2 * length)) / length)
    second = np.exp(-2j * np.pi * (np.outer(n, n) % LANES) / LANES)
    first_forward = np.concatenate([first.real, first.imag], axis=0)
    first_inverse = np.concatenate([first.real.T, first.imag.T], axis=1)
    second_forward = np.block([[second.real, second.imag], [-second.imag, second.real]])
    second_inverse = np.block([[second.real, -second.imag], [second.imag, second.real]])
    half = ml_dtypes.bfloat16
    turns = np.stack([turn.real, turn.imag]).astype(np.float32)
    return tuple(
        jnp.asarray(table)
        for table in (
            first_forward.astype(half),
            second_forward.astype(half),
            second_inverse.astype(half),
            first_inverse.astype(half),
            turns,
            (turns * np.float32(2.0 / length)),
        )
    )


def block_kernel(
    side_ref,
    own_ref,
    far_ref,
    other_own_ref,
    other_next_ref,
    other_far_ref,
    taps_ref,
    first_forward_ref,
    second_forward_ref,
    second_inverse_ref,
    first_inverse_ref,
    turn_ref,
    back_turn_ref,
    near_out_ref,
    other_out_ref,
    passed_out_ref,
    lag_out_ref,
    spectra,
    products,
):
    groups, _, rows, lanes = own_ref.shape
    side = side_ref[0]
    signals = (own_ref, far_ref, other_own_ref, other_next_ref, other_far_ref, taps_ref)
    for number, signal in enumerate(signals):
        for pair in range(signal.shape[0] // 2):
            both = jnp.concatenate([signal[2 * pair, 0], signal[2 * pair + 1, 0]], axis=1)
            first = jnp.dot(first_forward_ref[...], both, preferred_element_type=jnp.float32)
            for which in range(2):
                real = first[:rows, which * lanes : (which + 1) * lanes]
                imaginary = first[rows:, which * lanes : (which + 1) * lanes]
                turned = jnp.concatenate(
                    [
                        real * turn_ref[0] - imaginary * turn_ref[1],
                        real * turn_ref[1] + imaginary * turn_ref[0],
                    ],
                    axis=1,
                ).astype(jnp.bfloat16)
                spectra[number, 2 * pair + which] = jnp.dot(
                    turned, second_forward_ref[...], preferred_element_type=jnp.float32
                )

    row_index = lax.broadcasted_iota(jnp.int32, (STRIP, lanes), 0)
    parity = 1.0 - 2.0 * (row_index % 2).astype(jnp.float32)

    def strip(step, carry):
        at = pl.ds(pl.multiple_of(step * STRIP, STRIP), STRIP)

        def load(number, which):
            return spectra[number, which, at, :lanes], spectra[number, which, at, lanes:]

        def store(number, real, imaginary):
            products[number, at, :lanes] = real.astype(jnp.bfloat16)
            products[number, at, lanes:] = imaginary.astype(jnp.bfloat16)

        filters = [load(5, delay) for delay in range(4)]
        gains = []
        for delay in range(4):
            real, imaginary = filters[delay]
            if delay:
                before_real, before_imaginary = filters[delay - 1]
                real = real - parity * before_imaginary
                imaginary = imaginary + parity * before_real
            gains.append((real, side * imaginary))
        lag = [(jnp.zeros((STRIP, lanes), jnp.float32),) * 2 for _ in range(4)]

        def times(total, left, right):
            real = left[0] * right[0] - left[1] * right[1]
            imaginary = left[0] * right[1] + left[1] * right[0]
            return (real, imaginary) if total is None else (total[0] + real, total[1] + imaginary)

        def conjugate_times(total, left, right):
            real = left[0] * right[0] + left[1] * right[1]
            imaginary = left[0] * right[1] - left[1] * right[0]
            return (real, imaginary) if total is None else (total[0] + real, total[1] + imaginary)

        for group in range(groups):
            own, far = load(0, group), load(1, group)
            near = times(times(None, gains[0], own), gains[1], far)
            store(group, *near)
            other_own, other_next, other_far = load(2, group), load(3, group), load(4, group)
            other = conjugate_times(None, gains[0], other_own)
            other = conjugate_times(other, gains[1], other_next)
            other = conjugate_times(other, gains[2], other_far)
            store(groups + group, *other)
            passed = conjugate_times(None, gains[1], other_own)
            passed = conjugate_times(passed, gains[2], other_next)
            passed = conjugate_times(passed, gains[3], other_far)
            store(2 * groups + group, *passed)
            half_own = (0.5 * own[0], 0.5 * own[1])
            lag[0] = conjugate_times(lag[0], own, other_own)
            lag[1] = conjugate_times(lag[1], far, other_own)
            lag[1] = conjugate_times(lag[1], half_own, other_next)
            lag[2] = conjugate_times(lag[2], far, other_next)
            lag[3] = conjugate_times(lag[3], far, other_far)
        lag[3] = (0.5 * lag[3][0], 0.5 * lag[3][1])
        for delay in range(4):
            real, imaginary = lag[delay][0], side * lag[delay][1]
            if delay < 3:
                real = real + parity * (side * lag[delay + 1][1])
                imaginary = imaginary - parity * lag[delay + 1][0]
            store(3 * groups + delay, real, imaginary)
        return carry

    lax.fori_loop(0, rows // STRIP, strip, 0)

    shares = lag_out_ref.shape[0]
    for kind, out_ref in enumerate((near_out_ref, other_out_ref, passed_out_ref, None)):
        for pair in range((groups if kind < 3 else 4) // 2):
            real_parts, imaginary_parts = [], []
            for which in range(2):
                back = jnp.dot(
                    products[kind * groups + 2 * pair + which],
                    second_inverse_ref[...],
                    preferred_element_type=jnp.float32,
                )
                real, imaginary = back[:, :lanes], back[:, lanes:]
                real_parts.append(
                    (real * back_turn_ref[0] + imaginary * back_turn_ref[1]).astype(jnp.bfloat16)
                )
                imaginary_parts.append(
                    (imaginary * back_turn_ref[0] - real * back_turn_ref[1]).astype(jnp.bfloat16)
                )
            rotated = jnp.concatenate(
                [jnp.concatenate(real_parts, axis=1), jnp.concatenate(imaginary_parts, axis=1)],
                axis=0,
            )
            result = jnp.dot(first_inverse_ref[...], rotated, preferred_element_type=jnp.float32)
            result = result.astype(jnp.bfloat16)
            for which in range(2):
                column = result[:, which * lanes : (which + 1) * lanes]
                if kind < 3:
                    out_ref[2 * pair + which, 0] = column
                else:
                    column = column.reshape(shares, rows // shares, lanes)
                    lag_out_ref[:, 2 * pair + which, 0] = column


def block_products(side, signals, other, taps, tables, start, shares):
    groups, filters, rows, lanes = signals[0].shape
    block = pl.BlockSpec((groups, 1, rows, lanes), lambda f: (0, f, 0, 0))
    other_block = pl.BlockSpec((groups, 1, rows, lanes), lambda f: (0, f + start, 0, 0))
    taps_block = pl.BlockSpec((4, 1, rows, lanes), lambda f: (0, f + start, 0, 0))
    lag_block = pl.BlockSpec((shares, 4, 1, rows // shares, lanes), lambda f: (0, 0, f, 0, 0))

    def whole(table):
        return pl.BlockSpec(table.shape, lambda f: (0,) * table.ndim)

    made = jax.ShapeDtypeStruct(signals[0].shape, jnp.bfloat16)
    lag = jax.ShapeDtypeStruct((shares, 4, filters, rows // shares, lanes), jnp.bfloat16)
    own, far, other_next, other_far = signals
    return pl.pallas_call(
        block_kernel,
        grid=(filters,),
        in_specs=[pl.BlockSpec(memory_space=pltpu.SMEM)]
        + [block, block, other_block, block, block, taps_block]
        + [whole(table) for table in tables],
        out_specs=[block, block, block, lag_block],
        out_shape=[made, made, made, lag],
        scratch_shapes=[
            pltpu.VMEM((6, groups, rows, 2 * lanes), jnp.float32),
            pltpu.VMEM((3 * groups + 4, rows, 2 * lanes), jnp.bfloat16),
        ],
        compiler_params=pltpu.CompilerParams(vmem_limit_bytes=VMEM_BYTES),
        cost_estimate=pl.CostEstimate(flops=1, bytes_accessed=1, transcendentals=0),
    )(side, own, far, other, other_next, other_far, taps, *tables)


def product(left, right):
    return (left.astype(jnp.float32) * right.astype(jnp.float32)).astype(jnp.bfloat16)


def enter_kernel(first_ref, gate_ref, values_ref, cotangent_ref, out_gate_ref, *out_refs):
    channels, width = gate_ref.shape
    groups, rows = out_refs[0].shape[0], width // LANES

    def fill(left_ref, right_ref):
        made = product(left_ref[...], right_ref[...]).astype(jnp.float32)
        made = made.reshape(channels, rows, LANES).astype(jnp.bfloat16)
        made = made.reshape(groups, channels // groups, rows, LANES)
        start = 0
        for out_ref in out_refs:
            out_ref[...] = made[:, start : start + out_ref.shape[1]]
            start += out_ref.shape[1]

    @pl.when(first_ref[0] == 1)
    def _():
        fill(gate_ref, values_ref)

    @pl.when(first_ref[0] == 0)
    def _():
        fill(cotangent_ref, out_gate_ref)


def enter(first, flat, filters, counts):
    channels, local_len = flat[0].shape
    groups, rows = channels // filters, local_len // LANES
    block = (channels, EDGE_ROWS * LANES)
    of_first = pl.BlockSpec(block, lambda i, first: (0, i * first[0]))
    of_second = pl.BlockSpec(block, lambda i, first: (0, i * (1 - first[0])))
    return pl.pallas_call(
        enter_kernel,
        grid_spec=pltpu.PrefetchScalarGridSpec(
            num_scalar_prefetch=1,
            grid=(rows // EDGE_ROWS,),
            in_specs=[of_first, of_first, of_second, of_second],
            out_specs=[
                pl.BlockSpec((groups, count, EDGE_ROWS, LANES), lambda i, first: (0, 0, i, 0))
                for count in counts
            ],
        ),
        out_shape=[
            jax.ShapeDtypeStruct((groups, count, rows, LANES), jnp.bfloat16) for count in counts
        ],
        compiler_params=pltpu.CompilerParams(vmem_limit_bytes=VMEM_BYTES),
        cost_estimate=pl.CostEstimate(
            flops=2 * channels * local_len,
            bytes_accessed=6 * channels * local_len,
            transcendentals=0,
        ),
    )(first, *flat)


def leave_kernel(has_received, has_made, *refs):
    first_ref, skip_ref, gate_ref, values_ref, cotangent_ref, out_gate_ref, *refs = refs
    channels, width = gate_ref.shape
    parts, rows = len(SHARES), width // LANES
    signal_refs, refs = refs[:parts], refs[parts:]
    signal = jnp.concatenate([ref[...] for ref in signal_refs], axis=1).astype(jnp.float32)
    if has_received:
        received = jnp.concatenate([ref[...] for ref in refs[:parts]], axis=1)
        signal, refs = signal + received.astype(jnp.float32), refs[parts:]
    if has_made:
        made_refs, refs = refs[:4], refs[4:]
    out_refs = refs
    signal = signal.reshape(channels, rows, LANES).reshape(channels, width)
    skip = skip_ref[...]

    def finish(left_ref, right_ref, factor_refs, result_refs, kept):
        term = product(left_ref[...], right_ref[...]).astype(jnp.float32)
        total = signal + skip * term
        for factor_ref, result_ref in zip(factor_refs, result_refs):
            result_ref[...] = (factor_ref[...].astype(jnp.float32) * total).astype(jnp.bfloat16)
        if has_made:

            @pl.when(pl.program_id(0) == 0)
            def _():
                for number in kept:
                    out_refs[number][...] = made_refs[number][...]

    @pl.when(first_ref[0] == 1)
    def _():
        finish(gate_ref, values_ref, (out_gate_ref, cotangent_ref), out_refs[:2], (2, 3))

    @pl.when(first_ref[0] == 0)
    def _():
        finish(cotangent_ref, out_gate_ref, (values_ref, gate_ref), out_refs[2:], (0, 1))


def leave(first, skip_gain, flat, signal_parts, received_parts=(), made=(), span=(0, 1)):
    channels, local_len = flat[0].shape
    parts = (*signal_parts, *received_parts)
    block = (channels, EDGE_ROWS * LANES)
    steps = local_len // (EDGE_ROWS * LANES * span[1])
    offset = span[0] * steps
    flat_block = pl.BlockSpec(block, lambda i, first: (0, i + offset))
    still_block = pl.BlockSpec(block, lambda i, first: (0, 0))
    of_first = pl.BlockSpec(block, lambda i, first: (0, (i + offset) * first[0]))
    of_second = pl.BlockSpec(block, lambda i, first: (0, (i + offset) * (1 - first[0])))
    before = 6 + len(parts)
    return pl.pallas_call(
        lambda *refs: leave_kernel(bool(received_parts), bool(made), *refs),
        grid_spec=pltpu.PrefetchScalarGridSpec(
            num_scalar_prefetch=1,
            grid=(steps,),
            in_specs=[pl.BlockSpec((channels, 1), lambda i, first: (0, 0))]
            + [flat_block] * 4
            + [
                pl.BlockSpec(
                    (*part.shape[:2], EDGE_ROWS, LANES), lambda i, first: (0, 0, i + offset, 0)
                )
                for part in parts
            ]
            + [still_block] * len(made),
            out_specs=[of_first, of_first, of_second, of_second],
        ),
        out_shape=[jax.ShapeDtypeStruct((channels, local_len), jnp.bfloat16)] * 4,
        input_output_aliases={before + number: number for number in range(len(made))},
        compiler_params=pltpu.CompilerParams(vmem_limit_bytes=VMEM_BYTES),
        cost_estimate=pl.CostEstimate(
            flops=8 * channels * local_len // span[1],
            bytes_accessed=14 * channels * local_len // span[1],
            transcendentals=0,
        ),
    )(first, skip_gain[:, None], *flat, *parts, *made)


def rotation(hop):
    return [(index, (index + hop) % 4) for index in range(4)]


def block_shards(input_gate, output_gate, values, cotangent, filter_raw, filter_decay, skip_gain):
    context_index = lax.axis_index("ctx")
    channels, local_len = input_gate.shape
    filters = filter_raw.shape[0]
    rows = local_len // LANES
    seq_len = local_len * lax.axis_size("ctx")
    data_size = lax.axis_size("dp")
    tables = block_tables(rows)
    side = jnp.where(context_index < 2, 1.0, -1.0).astype(jnp.float32).reshape(1)
    near_start = (context_index < 2).astype(jnp.int32).reshape(1)
    flat = (input_gate, values, cotangent, output_gate)
    own_parts = enter(near_start, flat, filters, SHARES)
    routes = ([(1, 2), (2, 1)], [(0, 2), (3, 1)], [(0, 1), (3, 2)])
    back_route = [(1, 0), (2, 3)]

    positions = (context_index * local_len + jnp.arange(local_len, dtype=jnp.int32)).astype(
        jnp.float32
    )
    filter_scale = seq_len ** (-0.5)

    def envelope(decay):
        return jnp.exp(-decay[:, None] * (positions[None, :] / seq_len))

    share = filters // data_size
    first_filter = lax.axis_index("dp") * share
    raw_share = lax.dynamic_slice_in_dim(filter_raw, first_filter, share, 0)
    decay_share = lax.dynamic_slice_in_dim(filter_decay, first_filter, share, 0)
    taps = (raw_share.astype(jnp.float32) * envelope(decay_share) * filter_scale).astype(
        jnp.bfloat16
    )
    taps = taps.reshape(1, share, rows, LANES)
    turned = [taps] + [lax.ppermute(taps, "ctx", rotation(hop)) for hop in (1, 2, 3)]
    turned = jnp.concatenate(turned[::-1] + turned[:0:-1], axis=0)
    taps = lax.dynamic_slice_in_dim(turned, 3 - context_index, 4, 0)
    own_parts, taps, rest = lax.optimization_barrier((own_parts, taps, 1 - near_start))
    arrivals = [lax.ppermute(own_parts[0], "ctx", route) for route in routes]
    taps = lax.all_gather(taps, "dp", axis=1, tiled=True)
    (other,) = enter(rest, flat, filters, (filters,))

    def lag_shares(pieces):
        pieces = lax.all_to_all(pieces, "dp", split_axis=0, concat_axis=0, tiled=True)
        return jnp.sum(pieces.astype(jnp.float32), axis=0).astype(jnp.bfloat16)

    def lag_block(pieces):
        def block(index):
            return lax.dynamic_index_in_dim(pieces, index, 0, keepdims=False)

        total = block(context_index).astype(jnp.float32)
        for hop in (1, 2, 3):
            leaving = block((context_index + hop) % 4)
            total += lax.ppermute(leaving, "ctx", rotation(hop)).astype(jnp.float32)
        return total.astype(jnp.bfloat16)

    def lag_rows(total):
        spread = jnp.broadcast_to(total[None], (data_size, *total.shape))
        spread = lax.all_to_all(spread, "dp", split_axis=0, concat_axis=0, tiled=True)
        return jnp.transpose(spread, (1, 0, 2, 3)).reshape(total.shape[0], rows, LANES)

    near_parts, other_parts, received_parts, lag_parts = [], [], [], []
    start, pending = 0, None
    for number, own in enumerate(own_parts):
        leaving = own_parts[number + 1] if number + 1 < len(own_parts) else None
        arrivals, own, leaving, pending, received_parts, lag_parts, near_parts, other = (
            lax.optimization_barrier(
                (arrivals, own, leaving, pending, received_parts, lag_parts, near_parts, other)
            )
        )
        other_next, other_far, far = arrivals
        if leaving is not None:
            arrivals = [lax.ppermute(leaving, "ctx", route) for route in routes]
        if pending is not None:
            received_parts.append(lax.ppermute(pending[0], "ctx", back_route))
            lag_parts.append(lag_shares(pending[1]))
        near_out, other_out, *pending = block_products(
            side, (own, far, other_next, other_far), other, taps, tables, start, data_size
        )
        start += own.shape[1]
        near_parts.append(near_out)
        other_parts.append(other_out)
    pending, received_parts, lag_parts, near_parts = lax.optimization_barrier(
        (pending, received_parts, lag_parts, near_parts)
    )
    received = lax.ppermute(pending[0], "ctx", back_route)
    made = leave(near_start, skip_gain, flat, near_parts)
    received, late, made, rest = lax.optimization_barrier(
        (received, lag_shares(pending[1]), made, rest)
    )
    received_parts.append(received)
    sides = (rest, skip_gain, flat, other_parts, received_parts)
    lag = lag_block(jnp.concatenate([*lag_parts, late], axis=1))
    lag, made, sides = lax.optimization_barrier((lag, leave(*sides, made, (0, 2)), sides))
    lag = lag_rows(lag).reshape(filters, local_len)
    outputs, grad_output_gate, grad_input_gate, grad_values = leave(*sides, made, (1, 2))
    grad_filter = lag.astype(jnp.float32) * envelope(filter_decay) * filter_scale
    return (outputs, grad_input_gate, grad_output_gate, grad_values, grad_filter)


def chosen_shards(dp, ctx):
    def run(input_gate, *others):
        channels, local_len = input_gate.shape
        filters = others[3].shape[0]
        by_blocks = (
            ctx == 4
            and local_len % (LANES * STRIP * dp) == 0
            and local_len % (LANES * EDGE_ROWS * 2) == 0
            and channels % (2 * filters) == 0
            and filters % dp == 0
            and filters == sum(SHARES)
        )
        return (block_shards if by_blocks else shards)(input_gate, *others)

    return run


def solution(mesh):
    return jax.shard_map(
        chosen_shards(mesh.shape["dp"], mesh.shape["ctx"]),
        mesh=mesh,
        in_specs=(
            P("dp", "ctx"),
            P("dp", "ctx"),
            P("dp", "ctx"),
            P("dp", "ctx"),
            P(None, "ctx"),
            P(),
            P("dp"),
        ),
        out_specs=(P("dp", "ctx"), P("dp", "ctx"), P("dp", "ctx"), P("dp", "ctx"), P(None, "ctx")),
        check_vma=False,
    )
```

```python
import math

import jax
import jax.numpy as jnp
import ml_dtypes
import numpy as np
from jax import lax
from jax.experimental import pallas as pl
from jax.experimental.pallas import tpu as pltpu
from jax.sharding import PartitionSpec as P

N1 = 512
N2 = 512
FFT_LEN = 262144


two_pi = 2.0 * math.pi


def first_tables(row_total):
    first_index = jnp.arange(N1, dtype=jnp.int32)
    source_rows = jnp.arange(row_total, dtype=jnp.int32)
    angles = (first_index[:, None] * source_rows[None, :] % N1).astype(jnp.float32) * (two_pi / N1)
    cosine = jnp.cos(angles).astype(jnp.bfloat16)
    minus_sine = (-jnp.sin(angles)).astype(jnp.bfloat16)
    forward_table = jnp.concatenate([cosine, minus_sine], axis=0)
    inverse_table = jnp.stack([cosine.T, minus_sine.T], axis=2)
    return (forward_table, inverse_table)


def second_tables():
    second_index = jnp.arange(N2, dtype=jnp.int32)
    angles = (second_index[:, None] * second_index[None, :] % N2).astype(jnp.float32) * (
        two_pi / N2
    )
    cosine = jnp.cos(angles).astype(jnp.bfloat16)
    minus_sine = (-jnp.sin(angles)).astype(jnp.bfloat16)
    forward_table = jnp.stack(
        [
            jnp.concatenate([cosine, minus_sine], axis=1),
            jnp.concatenate([-minus_sine, cosine], axis=1),
        ],
        axis=0,
    )
    inverse_table = jnp.concatenate(
        [
            jnp.concatenate([cosine, -minus_sine], axis=1),
            jnp.concatenate([minus_sine, cosine], axis=1),
        ],
        axis=0,
    )
    return (forward_table, inverse_table)


def twiddle_table(spectrum_rows, columns):
    angles = (spectrum_rows[:, None] * columns[None, :] % FFT_LEN).astype(jnp.float32) * (
        two_pi / FFT_LEN
    )
    return (jnp.cos(angles), -jnp.sin(angles))


def halves(array):
    return (array[..., :N2], array[..., N2:])


def joined(real_part, imaginary_part):
    return jnp.concatenate([real_part, imaginary_part], axis=-1).astype(jnp.bfloat16)


def spectral_products(mix_spec, weight_spec, filter_spec, which):
    lead = mix_spec.shape[:-2]
    filters = filter_spec.shape[-2]
    filter_real, filter_imaginary = halves(filter_spec.astype(jnp.float32))
    filter_real = jnp.expand_dims(filter_real, -3)
    filter_imaginary = jnp.expand_dims(filter_imaginary, -3)
    outcome = []
    mix_real, mix_imaginary = halves(mix_spec.reshape(lead + (-1, filters, 2 * N2)))
    weight_real, weight_imaginary = halves(weight_spec.reshape(lead + (-1, filters, 2 * N2)))
    for name in which:
        if name == "convolve":
            made = joined(
                mix_real * filter_real - mix_imaginary * filter_imaginary,
                mix_real * filter_imaginary + mix_imaginary * filter_real,
            )
        elif name == "correlate":
            made = joined(
                filter_real * weight_real + filter_imaginary * weight_imaginary,
                filter_real * weight_imaginary - filter_imaginary * weight_real,
            )
        else:
            made = joined(
                mix_real * weight_real + mix_imaginary * weight_imaginary,
                mix_real * weight_imaginary - mix_imaginary * weight_real,
            )
        outcome.append(made.reshape(lead + (-1, 2 * N2)))
    return outcome


def shards(input_gate, output_gate, values, cotangent, filter_raw, filter_decay, skip_gain):
    context_size = lax.axis_size("ctx")
    context_index = lax.axis_index("ctx")
    channels, local_len = input_gate.shape
    filters = filter_raw.shape[0]
    groups = channels // filters
    row_local = local_len // N2
    row_total = row_local * context_size
    seq_len = local_len * context_size
    first_forward, first_inverse = first_tables(row_total)
    second_forward, second_inverse = second_tables()
    inverse_scale = 1.0 / FFT_LEN
    mixed_input = (input_gate.astype(jnp.float32) * values.astype(jnp.float32)).astype(jnp.bfloat16)
    weighted = (cotangent.astype(jnp.float32) * output_gate.astype(jnp.float32)).astype(
        jnp.bfloat16
    )
    global_positions = (context_index * local_len + jnp.arange(local_len, dtype=jnp.int32)).astype(
        jnp.float32
    )
    envelope = jnp.exp(-filter_decay[:, None] * (global_positions[None, :] / seq_len))
    filter_scale = seq_len ** (-0.5)
    filter_taps = (filter_raw.astype(jnp.float32) * envelope * filter_scale).astype(jnp.bfloat16)
    spread_count = filters // context_size
    full_real, full_imaginary = twiddle_table(
        jnp.arange(N1, dtype=jnp.int32), jnp.arange(N2, dtype=jnp.int32)
    )
    pair = jnp.stack([mixed_input, weighted], axis=0).reshape(2, groups, filters, row_local, N2)
    taps_block = filter_taps.reshape(1, 1, filters, row_local, N2)
    pair_whole, taps_whole = (
        lax.all_to_all(pair, "ctx", split_axis=2, concat_axis=3, tiled=True),
        lax.all_to_all(taps_block, "ctx", split_axis=2, concat_axis=3, tiled=True),
    )
    signal_count = 2 * groups * spread_count
    every = jnp.concatenate(
        [
            pair_whole.reshape(signal_count, row_total, N2),
            taps_whole.reshape(spread_count, row_total, N2),
        ],
        axis=0,
    )
    first = jnp.einsum("km,imn->ikn", first_forward, every, preferred_element_type=jnp.float32)
    first_real = first[:, :N1]
    first_imaginary = first[:, N1:]
    turned = jnp.stack(
        [
            first_real * full_real - first_imaginary * full_imaginary,
            first_real * full_imaginary + first_imaginary * full_real,
        ],
        axis=1,
    ).astype(jnp.bfloat16)
    spectra = jnp.einsum(
        "ipkn,pnl->ikl", turned, second_forward, preferred_element_type=jnp.float32
    )
    signal_spec = spectra[:signal_count].reshape(2, groups * spread_count, N1, 2 * N2)
    filter_spec = spectra[signal_count:].astype(jnp.bfloat16)
    filter_spec = jnp.transpose(filter_spec, (1, 0, 2))
    mix_spec = jnp.transpose(signal_spec[0], (1, 0, 2))
    weight_spec = jnp.transpose(signal_spec[1], (1, 0, 2))
    made = spectral_products(mix_spec, weight_spec, filter_spec, ["convolve", "correlate", "lag"])
    stacked = jnp.transpose(jnp.concatenate(made, axis=1), (1, 0, 2))
    back = jnp.einsum("ikl,lm->ikm", stacked, second_inverse, preferred_element_type=jnp.float32)
    back_real, back_imaginary = halves(back)
    rotated = jnp.stack(
        [
            (back_real * full_real + back_imaginary * full_imaginary) * inverse_scale,
            (back_imaginary * full_real - back_real * full_imaginary) * inverse_scale,
        ],
        axis=1,
    ).astype(jnp.bfloat16)
    inverted = jnp.einsum(
        "mkp,ipkn->imn", first_inverse, rotated, preferred_element_type=jnp.float32
    )
    inverted = inverted.astype(jnp.bfloat16).reshape(3, groups, spread_count, row_total, N2)
    back_rows = lax.all_to_all(inverted[:2], "ctx", split_axis=3, concat_axis=2, tiled=True)
    convolved = back_rows[0].reshape(channels, local_len)
    correlated = back_rows[1].reshape(channels, local_len)
    lag_whole = jnp.sum(inverted[2].astype(jnp.float32), axis=0)
    lag_part = (
        lax.all_to_all(
            lag_whole.astype(jnp.bfloat16), "ctx", split_axis=1, concat_axis=0, tiled=True
        )
        .astype(lag_whole.dtype)
        .reshape(filters, local_len)
    )
    summed = convolved.astype(jnp.float32) + skip_gain[:, None] * mixed_input.astype(jnp.float32)
    outputs = (output_gate.astype(jnp.float32) * summed).astype(jnp.bfloat16)
    grad_output_gate = (cotangent.astype(jnp.float32) * summed).astype(jnp.bfloat16)
    back_total = correlated.astype(jnp.float32) + skip_gain[:, None] * weighted.astype(jnp.float32)
    grad_input_gate = (back_total * values.astype(jnp.float32)).astype(jnp.bfloat16)
    grad_values = (back_total * input_gate.astype(jnp.float32)).astype(jnp.bfloat16)
    lag_total = lax.psum(lag_part.astype(jnp.bfloat16), "dp").astype(jnp.float32)
    grad_filter = lag_total * envelope * filter_scale
    return (outputs, grad_input_gate, grad_output_gate, grad_values, grad_filter)


LANES = 128
SHARES = (7, 5, 4)
STRIP = 16
EDGE_ROWS = 64
VMEM_BYTES = 60 * 2**20


def block_tables(rows):
    length = 2 * rows * LANES
    k = np.arange(rows)
    m = np.arange(rows)
    n = np.arange(LANES)
    first = np.exp(-1j * np.pi * (np.outer(2 * k + 1, m) % (4 * rows)) / (2 * rows))
    turn = np.exp(-1j * np.pi * (np.outer(2 * k + 1, n) % (2 * length)) / length)
    second = np.exp(-2j * np.pi * (np.outer(n, n) % LANES) / LANES)
    first_forward = np.concatenate([first.real, first.imag], axis=0)
    first_inverse = np.concatenate([first.real.T, first.imag.T], axis=1)
    second_forward = np.block([[second.real, second.imag], [-second.imag, second.real]])
    second_inverse = np.block([[second.real, -second.imag], [second.imag, second.real]])
    half = ml_dtypes.bfloat16
    turns = np.stack([turn.real, turn.imag]).astype(np.float32)
    return tuple(
        jnp.asarray(table)
        for table in (
            first_forward.astype(half),
            second_forward.astype(half),
            second_inverse.astype(half),
            first_inverse.astype(half),
            turns,
            (turns * np.float32(2.0 / length)),
        )
    )


def block_kernel(
    side_ref,
    own_ref,
    far_ref,
    other_own_ref,
    other_next_ref,
    other_far_ref,
    taps_ref,
    first_forward_ref,
    second_forward_ref,
    second_inverse_ref,
    first_inverse_ref,
    turn_ref,
    back_turn_ref,
    near_out_ref,
    other_out_ref,
    passed_out_ref,
    lag_out_ref,
    spectra,
    products,
):
    groups, _, rows, lanes = own_ref.shape
    side = side_ref[0]
    signals = (own_ref, far_ref, other_own_ref, other_next_ref, other_far_ref, taps_ref)
    for number, signal in enumerate(signals):
        for pair in range(signal.shape[0] // 2):
            both = jnp.concatenate([signal[2 * pair, 0], signal[2 * pair + 1, 0]], axis=1)
            first = jnp.dot(first_forward_ref[...], both, preferred_element_type=jnp.float32)
            for which in range(2):
                real = first[:rows, which * lanes : (which + 1) * lanes]
                imaginary = first[rows:, which * lanes : (which + 1) * lanes]
                turned = jnp.concatenate(
                    [
                        real * turn_ref[0] - imaginary * turn_ref[1],
                        real * turn_ref[1] + imaginary * turn_ref[0],
                    ],
                    axis=1,
                ).astype(jnp.bfloat16)
                spectra[number, 2 * pair + which] = jnp.dot(
                    turned, second_forward_ref[...], preferred_element_type=jnp.float32
                )

    row_index = lax.broadcasted_iota(jnp.int32, (STRIP, lanes), 0)
    parity = 1.0 - 2.0 * (row_index % 2).astype(jnp.float32)

    def strip(step, carry):
        at = pl.ds(pl.multiple_of(step * STRIP, STRIP), STRIP)

        def load(number, which):
            return spectra[number, which, at, :lanes], spectra[number, which, at, lanes:]

        def store(number, real, imaginary):
            products[number, at, :lanes] = real.astype(jnp.bfloat16)
            products[number, at, lanes:] = imaginary.astype(jnp.bfloat16)

        filters = [load(5, delay) for delay in range(4)]
        gains = []
        for delay in range(4):
            real, imaginary = filters[delay]
            if delay:
                before_real, before_imaginary = filters[delay - 1]
                real = real - parity * before_imaginary
                imaginary = imaginary + parity * before_real
            gains.append((real, side * imaginary))
        lag = [(jnp.zeros((STRIP, lanes), jnp.float32),) * 2 for _ in range(4)]

        def times(total, left, right):
            real = left[0] * right[0] - left[1] * right[1]
            imaginary = left[0] * right[1] + left[1] * right[0]
            return (real, imaginary) if total is None else (total[0] + real, total[1] + imaginary)

        def conjugate_times(total, left, right):
            real = left[0] * right[0] + left[1] * right[1]
            imaginary = left[0] * right[1] - left[1] * right[0]
            return (real, imaginary) if total is None else (total[0] + real, total[1] + imaginary)

        for group in range(groups):
            own, far = load(0, group), load(1, group)
            near = times(times(None, gains[0], own), gains[1], far)
            store(group, *near)
            other_own, other_next, other_far = load(2, group), load(3, group), load(4, group)
            other = conjugate_times(None, gains[0], other_own)
            other = conjugate_times(other, gains[1], other_next)
            other = conjugate_times(other, gains[2], other_far)
            store(groups + group, *other)
            passed = conjugate_times(None, gains[1], other_own)
            passed = conjugate_times(passed, gains[2], other_next)
            passed = conjugate_times(passed, gains[3], other_far)
            store(2 * groups + group, *passed)
            half_own = (0.5 * own[0], 0.5 * own[1])
            lag[0] = conjugate_times(lag[0], own, other_own)
            lag[1] = conjugate_times(lag[1], far, other_own)
            lag[1] = conjugate_times(lag[1], half_own, other_next)
            lag[2] = conjugate_times(lag[2], far, other_next)
            lag[3] = conjugate_times(lag[3], far, other_far)
        lag[3] = (0.5 * lag[3][0], 0.5 * lag[3][1])
        for delay in range(4):
            real, imaginary = lag[delay][0], side * lag[delay][1]
            if delay < 3:
                real = real + parity * (side * lag[delay + 1][1])
                imaginary = imaginary - parity * lag[delay + 1][0]
            store(3 * groups + delay, real, imaginary)
        return carry

    lax.fori_loop(0, rows // STRIP, strip, 0)

    shares = lag_out_ref.shape[0]
    for kind, out_ref in enumerate((near_out_ref, other_out_ref, passed_out_ref, None)):
        for pair in range((groups if kind < 3 else 4) // 2):
            real_parts, imaginary_parts = [], []
            for which in range(2):
                back = jnp.dot(
                    products[kind * groups + 2 * pair + which],
                    second_inverse_ref[...],
                    preferred_element_type=jnp.float32,
                )
                real, imaginary = back[:, :lanes], back[:, lanes:]
                real_parts.append(
                    (real * back_turn_ref[0] + imaginary * back_turn_ref[1]).astype(jnp.bfloat16)
                )
                imaginary_parts.append(
                    (imaginary * back_turn_ref[0] - real * back_turn_ref[1]).astype(jnp.bfloat16)
                )
            rotated = jnp.concatenate(
                [jnp.concatenate(real_parts, axis=1), jnp.concatenate(imaginary_parts, axis=1)],
                axis=0,
            )
            result = jnp.dot(first_inverse_ref[...], rotated, preferred_element_type=jnp.float32)
            result = result.astype(jnp.bfloat16)
            for which in range(2):
                column = result[:, which * lanes : (which + 1) * lanes]
                if kind < 3:
                    out_ref[2 * pair + which, 0] = column
                else:
                    column = column.reshape(shares, rows // shares, lanes)
                    lag_out_ref[:, 2 * pair + which, 0] = column


def block_products(side, signals, other, taps, tables, start, shares):
    groups, filters, rows, lanes = signals[0].shape
    block = pl.BlockSpec((groups, 1, rows, lanes), lambda f: (0, f, 0, 0))
    other_block = pl.BlockSpec((groups, 1, rows, lanes), lambda f: (0, f + start, 0, 0))
    taps_block = pl.BlockSpec((4, 1, rows, lanes), lambda f: (0, f + start, 0, 0))
    lag_block = pl.BlockSpec((shares, 4, 1, rows // shares, lanes), lambda f: (0, 0, f, 0, 0))

    def whole(table):
        return pl.BlockSpec(table.shape, lambda f: (0,) * table.ndim)

    made = jax.ShapeDtypeStruct(signals[0].shape, jnp.bfloat16)
    lag = jax.ShapeDtypeStruct((shares, 4, filters, rows // shares, lanes), jnp.bfloat16)
    own, far, other_next, other_far = signals
    return pl.pallas_call(
        block_kernel,
        grid=(filters,),
        in_specs=[pl.BlockSpec(memory_space=pltpu.SMEM)]
        + [block, block, other_block, block, block, taps_block]
        + [whole(table) for table in tables],
        out_specs=[block, block, block, lag_block],
        out_shape=[made, made, made, lag],
        scratch_shapes=[
            pltpu.VMEM((6, groups, rows, 2 * lanes), jnp.float32),
            pltpu.VMEM((3 * groups + 4, rows, 2 * lanes), jnp.bfloat16),
        ],
        compiler_params=pltpu.CompilerParams(vmem_limit_bytes=VMEM_BYTES),
        cost_estimate=pl.CostEstimate(flops=1, bytes_accessed=1, transcendentals=0),
    )(side, own, far, other, other_next, other_far, taps, *tables)


def product(left, right):
    return (left.astype(jnp.float32) * right.astype(jnp.float32)).astype(jnp.bfloat16)


def enter_kernel(first_ref, gate_ref, values_ref, cotangent_ref, out_gate_ref, *out_refs):
    channels, width = gate_ref.shape
    groups, rows = out_refs[0].shape[0], width // LANES

    def fill(left_ref, right_ref):
        made = product(left_ref[...], right_ref[...]).astype(jnp.float32)
        made = made.reshape(channels, rows, LANES).astype(jnp.bfloat16)
        made = made.reshape(groups, channels // groups, rows, LANES)
        start = 0
        for out_ref in out_refs:
            out_ref[...] = made[:, start : start + out_ref.shape[1]]
            start += out_ref.shape[1]

    @pl.when(first_ref[0] == 1)
    def _():
        fill(gate_ref, values_ref)

    @pl.when(first_ref[0] == 0)
    def _():
        fill(cotangent_ref, out_gate_ref)


def enter(first, flat, filters, counts):
    channels, local_len = flat[0].shape
    groups, rows = channels // filters, local_len // LANES
    block = (channels, EDGE_ROWS * LANES)
    of_first = pl.BlockSpec(block, lambda i, first: (0, i * first[0]))
    of_second = pl.BlockSpec(block, lambda i, first: (0, i * (1 - first[0])))
    return pl.pallas_call(
        enter_kernel,
        grid_spec=pltpu.PrefetchScalarGridSpec(
            num_scalar_prefetch=1,
            grid=(rows // EDGE_ROWS,),
            in_specs=[of_first, of_first, of_second, of_second],
            out_specs=[
                pl.BlockSpec((groups, count, EDGE_ROWS, LANES), lambda i, first: (0, 0, i, 0))
                for count in counts
            ],
        ),
        out_shape=[
            jax.ShapeDtypeStruct((groups, count, rows, LANES), jnp.bfloat16) for count in counts
        ],
        compiler_params=pltpu.CompilerParams(vmem_limit_bytes=VMEM_BYTES),
        cost_estimate=pl.CostEstimate(
            flops=2 * channels * local_len,
            bytes_accessed=6 * channels * local_len,
            transcendentals=0,
        ),
    )(first, *flat)


def leave_kernel(has_received, has_made, *refs):
    first_ref, skip_ref, gate_ref, values_ref, cotangent_ref, out_gate_ref, *refs = refs
    channels, width = gate_ref.shape
    parts, rows = len(SHARES), width // LANES
    signal_refs, refs = refs[:parts], refs[parts:]
    signal = jnp.concatenate([ref[...] for ref in signal_refs], axis=1).astype(jnp.float32)
    if has_received:
        received = jnp.concatenate([ref[...] for ref in refs[:parts]], axis=1)
        signal, refs = signal + received.astype(jnp.float32), refs[parts:]
    if has_made:
        made_refs, refs = refs[:4], refs[4:]
    out_refs = refs
    signal = signal.reshape(channels, rows, LANES).reshape(channels, width)
    skip = skip_ref[...]

    def finish(left_ref, right_ref, factor_refs, result_refs, kept):
        term = product(left_ref[...], right_ref[...]).astype(jnp.float32)
        total = signal + skip * term
        for factor_ref, result_ref in zip(factor_refs, result_refs):
            result_ref[...] = (factor_ref[...].astype(jnp.float32) * total).astype(jnp.bfloat16)
        if has_made:

            @pl.when(pl.program_id(0) == 0)
            def _():
                for number in kept:
                    out_refs[number][...] = made_refs[number][...]

    @pl.when(first_ref[0] == 1)
    def _():
        finish(gate_ref, values_ref, (out_gate_ref, cotangent_ref), out_refs[:2], (2, 3))

    @pl.when(first_ref[0] == 0)
    def _():
        finish(cotangent_ref, out_gate_ref, (values_ref, gate_ref), out_refs[2:], (0, 1))


def leave(first, skip_gain, flat, signal_parts, received_parts=(), made=(), span=(0, 1)):
    channels, local_len = flat[0].shape
    parts = (*signal_parts, *received_parts)
    block = (channels, EDGE_ROWS * LANES)
    steps = local_len // (EDGE_ROWS * LANES * span[1])
    offset = span[0] * steps
    flat_block = pl.BlockSpec(block, lambda i, first: (0, i + offset))
    still_block = pl.BlockSpec(block, lambda i, first: (0, 0))
    of_first = pl.BlockSpec(block, lambda i, first: (0, (i + offset) * first[0]))
    of_second = pl.BlockSpec(block, lambda i, first: (0, (i + offset) * (1 - first[0])))
    before = 6 + len(parts)
    return pl.pallas_call(
        lambda *refs: leave_kernel(bool(received_parts), bool(made), *refs),
        grid_spec=pltpu.PrefetchScalarGridSpec(
            num_scalar_prefetch=1,
            grid=(steps,),
            in_specs=[pl.BlockSpec((channels, 1), lambda i, first: (0, 0))]
            + [flat_block] * 4
            + [
                pl.BlockSpec(
                    (*part.shape[:2], EDGE_ROWS, LANES), lambda i, first: (0, 0, i + offset, 0)
                )
                for part in parts
            ]
            + [still_block] * len(made),
            out_specs=[of_first, of_first, of_second, of_second],
        ),
        out_shape=[jax.ShapeDtypeStruct((channels, local_len), jnp.bfloat16)] * 4,
        input_output_aliases={before + number: number for number in range(len(made))},
        compiler_params=pltpu.CompilerParams(vmem_limit_bytes=VMEM_BYTES),
        cost_estimate=pl.CostEstimate(
            flops=8 * channels * local_len // span[1],
            bytes_accessed=14 * channels * local_len // span[1],
            transcendentals=0,
        ),
    )(first, skip_gain[:, None], *flat, *parts, *made)


def rotation(hop):
    return [(index, (index + hop) % 4) for index in range(4)]


def block_shards(input_gate, output_gate, values, cotangent, filter_raw, filter_decay, skip_gain):
    context_index = lax.axis_index("ctx")
    channels, local_len = input_gate.shape
    filters = filter_raw.shape[0]
    rows = local_len // LANES
    seq_len = local_len * lax.axis_size("ctx")
    data_size = lax.axis_size("dp")
    tables = block_tables(rows)
    side = jnp.where(context_index < 2, 1.0, -1.0).astype(jnp.float32).reshape(1)
    near_start = (context_index < 2).astype(jnp.int32).reshape(1)
    flat = (input_gate, values, cotangent, output_gate)
    own_parts = enter(near_start, flat, filters, SHARES)
    routes = ([(1, 2), (2, 1)], [(0, 2), (3, 1)], [(0, 1), (3, 2)])
    back_route = [(1, 0), (2, 3)]

    positions = (context_index * local_len + jnp.arange(local_len, dtype=jnp.int32)).astype(
        jnp.float32
    )
    filter_scale = seq_len ** (-0.5)

    def envelope(decay):
        return jnp.exp(-decay[:, None] * (positions[None, :] / seq_len))

    share = filters // data_size
    first_filter = lax.axis_index("dp") * share
    raw_share = lax.dynamic_slice_in_dim(filter_raw, first_filter, share, 0)
    decay_share = lax.dynamic_slice_in_dim(filter_decay, first_filter, share, 0)
    taps = (raw_share.astype(jnp.float32) * envelope(decay_share) * filter_scale).astype(
        jnp.bfloat16
    )
    taps = taps.reshape(1, share, rows, LANES)
    turned = [taps] + [lax.ppermute(taps, "ctx", rotation(hop)) for hop in (1, 2, 3)]
    turned = jnp.concatenate(turned[::-1] + turned[:0:-1], axis=0)
    taps = lax.dynamic_slice_in_dim(turned, 3 - context_index, 4, 0)
    own_parts, taps, rest = lax.optimization_barrier((own_parts, taps, 1 - near_start))
    arrivals = [lax.ppermute(own_parts[0], "ctx", route) for route in routes]
    taps = lax.all_gather(taps, "dp", axis=1, tiled=True)
    (other,) = enter(rest, flat, filters, (filters,))

    def lag_shares(pieces):
        pieces = lax.all_to_all(pieces, "dp", split_axis=0, concat_axis=0, tiled=True)
        return jnp.sum(pieces.astype(jnp.float32), axis=0).astype(jnp.bfloat16)

    def lag_block(pieces):
        def block(index):
            return lax.dynamic_index_in_dim(pieces, index, 0, keepdims=False)

        total = block(context_index).astype(jnp.float32)
        for hop in (1, 2, 3):
            leaving = block((context_index + hop) % 4)
            total += lax.ppermute(leaving, "ctx", rotation(hop)).astype(jnp.float32)
        return total.astype(jnp.bfloat16)

    def lag_rows(total):
        spread = jnp.broadcast_to(total[None], (data_size, *total.shape))
        spread = lax.all_to_all(spread, "dp", split_axis=0, concat_axis=0, tiled=True)
        return jnp.transpose(spread, (1, 0, 2, 3)).reshape(total.shape[0], rows, LANES)

    near_parts, other_parts, received_parts, lag_parts = [], [], [], []
    start, pending = 0, None
    for number, own in enumerate(own_parts):
        leaving = own_parts[number + 1] if number + 1 < len(own_parts) else None
        arrivals, own, leaving, pending, received_parts, lag_parts, near_parts, other = (
            lax.optimization_barrier(
                (arrivals, own, leaving, pending, received_parts, lag_parts, near_parts, other)
            )
        )
        other_next, other_far, far = arrivals
        if leaving is not None:
            arrivals = [lax.ppermute(leaving, "ctx", route) for route in routes]
        if pending is not None:
            received_parts.append(lax.ppermute(pending[0], "ctx", back_route))
            lag_parts.append(lag_shares(pending[1]))
        near_out, other_out, *pending = block_products(
            side, (own, far, other_next, other_far), other, taps, tables, start, data_size
        )
        start += own.shape[1]
        near_parts.append(near_out)
        other_parts.append(other_out)
    pending, received_parts, lag_parts, near_parts = lax.optimization_barrier(
        (pending, received_parts, lag_parts, near_parts)
    )
    received = lax.ppermute(pending[0], "ctx", back_route)
    made = leave(near_start, skip_gain, flat, near_parts)
    received, late, made, rest = lax.optimization_barrier(
        (received, lag_shares(pending[1]), made, rest)
    )
    received_parts.append(received)
    sides = (rest, skip_gain, flat, other_parts, received_parts)
    lag = lag_block(jnp.concatenate([*lag_parts, late], axis=1))
    lag, made, sides = lax.optimization_barrier((lag, leave(*sides, made, (0, 2)), sides))
    lag = lag_rows(lag).reshape(filters, local_len)
    outputs, grad_output_gate, grad_input_gate, grad_values = leave(*sides, made, (1, 2))
    grad_filter = lag.astype(jnp.float32) * envelope(filter_decay) * filter_scale
    return (outputs, grad_input_gate, grad_output_gate, grad_values, grad_filter)


def chosen_shards(dp, ctx):
    def run(input_gate, *others):
        channels, local_len = input_gate.shape
        filters = others[3].shape[0]
        by_blocks = (
            ctx == 4
            and local_len % (LANES * STRIP * dp) == 0
            and local_len % (LANES * EDGE_ROWS * 2) == 0
            and channels % (2 * filters) == 0
            and filters % dp == 0
            and filters == sum(SHARES)
        )
        return (block_shards if by_blocks else shards)(input_gate, *others)

    return run


def solution(mesh):
    return jax.shard_map(
        chosen_shards(mesh.shape["dp"], mesh.shape["ctx"]),
        mesh=mesh,
        in_specs=(
            P("dp", "ctx"),
            P("dp", "ctx"),
            P("dp", "ctx"),
            P("dp", "ctx"),
            P(None, "ctx"),
            P(),
            P("dp"),
        ),
        out_specs=(P("dp", "ctx"), P("dp", "ctx"), P("dp", "ctx"), P("dp", "ctx"), P(None, "ctx")),
        check_vma=False,
    )
```
